32 devices in a mesh: groups: 2 (over x), tensor: 4 (over y, core), dp: 4 (over z).
Axes of the slice: x: 2, y: 2, z: 4, core: 2. Of those that a mesh axis runs over, the one named last changes fastest.
Arguments:
- layer_input: bfloat16 [1024, 8192], P(('groups', 'dp'), 'tensor'), parts along dimension 0, may hold values from -6 to 6
- out_grad: bfloat16 [1024, 8192], P(('groups', 'dp'), 'tensor'), parts along dimension 0, may hold values from -6 to 6
- gate_pre: bfloat16 [1024, 14336], P(('groups', 'tensor'), 'dp'), parts along dimension 0, may hold values from -6 to 6
- up_pre: bfloat16 [1024, 14336], P(('groups', 'tensor'), 'dp'), parts along dimension 0, may hold values from -6 to 6
- adapter_acts: bfloat16 [1024, 48], P('groups'), parts along dimension 0, may hold values from -6 to 6
- gate_weight: bfloat16 [8192, 14336], P('tensor', 'dp'), may hold values from -0.0625 to 0.0625
- up_weight: bfloat16 [8192, 14336], P('tensor', 'dp'), may hold values from -0.0625 to 0.0625
- down_weight: bfloat16 [14336, 8192], P('dp', 'tensor'), may hold values from -0.046875 to 0.046875
- adapter_a_gu: bfloat16 [4, 8192, 32], P(None, 'tensor'), may hold values from -0.5 to 0.5
- adapter_b_gu: bfloat16 [4, 32, 14336], P(None, None, 'dp'), may hold values from -0.046875 to 0.046875
- adapter_a_down: bfloat16 [4, 14336, 16], P(None, 'dp'), may hold values from -0.75 to 0.75
- adapter_b_down: bfloat16 [4, 16, 8192], P(None, None, 'tensor'), may hold values from -0.0625 to 0.0625
- block_tenant: int32 [8], P('groups'), parts along dimension 0, may hold values from 0 to 3, as said below
Outputs:
- block_input_grad: bfloat16 [1024, 8192], P(('groups', 'dp'), 'tensor'), parts along dimension 0
- grad_a_gu: float32 [8, 8192, 32], P('groups', 'tensor'), parts along dimension 0
- grad_b_gu: float32 [8, 32, 14336], P('groups', None, 'dp'), parts along dimension 0
- grad_a_down: float32 [8, 14336, 16], P('groups', 'dp'), parts along dimension 0
- grad_b_down: float32 [8, 16, 8192], P('groups', None, 'tensor'), parts along dimension 0
The draws below stay inside these ranges and needn't reach their ends.
There are 2 independent parts, one for each index of `groups`. The reference program is written for one: setup_inputs(seed, part) draws one part's arguments, and reference() takes and returns one part's arrays. A program takes and returns all parts, laid end to end along the dimension named above; an argument that names none is the same for every part. Nothing has to cross between parts.
Inputs may be any that keep to these rules, and one draw needn't show every extreme that they name: `block_tenant`: entry b names the tenant of tokens b * 128 to (b + 1) * 128 - 1. Every tenant owns at least one block, and the block counts of any two tenants differ by at most one.
All inputs are finite; a program needn't handle non-finite values.
Results may differ from the reference program's by a relative error of at most 0.017.
Values may be sent and summed in bfloat16 or wider, within the bound.
No kernel may reach another device: no remote copies, remote signals or barrier semaphores. Data moves between devices by JAX's collectives and lax.ppermute only.
A program may use at most 192 MiB of HBM per device.

```python
import jax
import jax.numpy as jnp
from jax import lax

D = 8192
FF = 14336
R = 16
TENANTS = 4
BLOCK = 128
TOKENS = 512
BLOCKS = 4
N_TENSOR = 4


def draw_block_tenant(key, part):
    key = jax.random.fold_in(key, 7)
    order = jax.random.permutation(key, BLOCKS)
    return (order % TENANTS).astype(jnp.int32)


def block_levels(key, dims, cuts, smallest, largest):
    gain, own = 1.0, jax.random.fold_in(key, 6)
    for position, blocks in cuts:
        heights = jnp.exp(jax.random.uniform(jax.random.fold_in(own, position), (blocks,), jnp.float32, smallest / len(cuts), largest / len(cuts)))
        gain = gain * jnp.repeat(heights, dims[position] // blocks).reshape([-1 if axis == position else 1 for axis in range(len(dims))])
    return gain


def scatter_about(stream_key, dims, spread, most, shards=(), kind=jnp.bfloat16):
    result = jax.random.normal(stream_key, dims, jnp.float32) * spread
    if len(shards) > 0:
        result = block_levels(stream_key, dims, shards, -0.22, 0.18) * result
    return jnp.clip(result, min=-most, max=most).astype(kind)


def setup_inputs(seed: int = 0, part: int = 0) -> dict:
    key_of = jax.random.split(jax.random.key(seed), 14)
    part_splits = jax.random.split(jax.random.fold_in(key_of[13], part), 14)
    layer_input = scatter_about(part_splits[0], (TOKENS, D), 1.0, 6.0, ((0, 4), (1, 4)))
    out_grad = scatter_about(part_splits[1], (TOKENS, D), 1.0, 6.0, ((0, 4), (1, 4)))
    gate_pre = scatter_about(part_splits[2], (TOKENS, FF), 1.0, 6.0, ((0, 4), (1, 4)))
    up_pre = scatter_about(part_splits[3], (TOKENS, FF), 1.0, 6.0, ((0, 4), (1, 4)))
    adapter_acts = scatter_about(part_splits[4], (TOKENS, 3 * R), 1.0, 6.0)
    gate_weight = scatter_about(key_of[5], (D, FF), D ** -0.5, 0.0625, ((0, 4), (1, 4)))
    up_weight = scatter_about(key_of[6], (D, FF), D ** -0.5, 0.0625, ((0, 4), (1, 4)))
    down_weight = scatter_about(key_of[7], (FF, D), FF ** -0.5, 0.046875, ((0, 4), (1, 4)))
    adapter_a_gu = scatter_about(key_of[8], (TENANTS, D, 2 * R), (8 * R) ** -0.5, 0.5, ((1, 4),))
    adapter_b_gu = scatter_about(key_of[9], (TENANTS, 2 * R, FF), FF ** -0.5, 0.046875, ((2, 4),))
    adapter_a_down = scatter_about(key_of[10], (TENANTS, FF, R), (4 * R) ** -0.5, 0.75, ((1, 4),))
    adapter_b_down = scatter_about(key_of[11], (TENANTS, R, D), D ** -0.5, 0.0625, ((2, 4),))
    block_tenant = draw_block_tenant(jax.random.fold_in(jax.random.fold_in(key_of[13], part), 71), part)
    return dict(layer_input=layer_input, out_grad=out_grad, gate_pre=gate_pre, up_pre=up_pre, adapter_acts=adapter_acts, gate_weight=gate_weight, up_weight=up_weight, down_weight=down_weight, adapter_a_gu=adapter_a_gu, adapter_b_gu=adapter_b_gu, adapter_a_down=adapter_a_down, adapter_b_down=adapter_b_down, block_tenant=block_tenant)


ADAPTER_SCALE = 2.0


def swiglu_grads(hidden_grad, gate_pre, up_pre):
    gate_value = gate_pre.astype(jnp.float32)
    up_value = up_pre.astype(jnp.float32)
    sigmoid_value = jax.nn.sigmoid(gate_value)
    hidden = (gate_value * sigmoid_value * up_value).astype(jnp.bfloat16)
    gate_grad = (hidden_grad * up_value * sigmoid_value * (1.0 + gate_value * (1.0 - sigmoid_value))).astype(jnp.bfloat16)
    up_grad = (hidden_grad * gate_value * sigmoid_value).astype(jnp.bfloat16)
    return hidden, gate_grad, up_grad


def combine(tenant_indicator, block_wise):
    return ADAPTER_SCALE * jnp.einsum("me,msl->esl", tenant_indicator, block_wise, precision=lax.Precision.HIGHEST)


def reference(layer_input, out_grad, gate_pre, up_pre, adapter_acts, gate_weight, up_weight, down_weight, adapter_a_gu, adapter_b_gu, adapter_a_down, adapter_b_down, block_tenant):
    blocks_all = TOKENS // BLOCK
    tenant_indicator = (block_tenant[:, None] == jnp.arange(TENANTS, dtype=jnp.int32)[None, :]).astype(jnp.float32)
    feature_span = D // N_TENSOR
    down_proj = adapter_b_down[block_tenant].astype(jnp.float32)
    down_lift = adapter_a_down[block_tenant].astype(jnp.float32)

    def shard_step(running, shard_index):
        hidden_sum, down_sum = running
        offset = (shard_index * feature_span).astype(jnp.int32)
        grad_part = lax.dynamic_slice_in_dim(out_grad, offset, feature_span, 1)
        weight_part = lax.dynamic_slice_in_dim(down_weight, offset, feature_span, 1)
        proj_part = lax.dynamic_slice_in_dim(down_proj, offset, feature_span, 2)
        projected = jnp.einsum("bnd,brd->bnr", grad_part.reshape(blocks_all, BLOCK, feature_span).astype(jnp.float32), proj_part, precision=lax.Precision.HIGHEST)
        frozen_path_part = jnp.dot(grad_part, weight_part.T, preferred_element_type=jnp.float32)
        rank_raised = jnp.einsum("bnr,bfr->bnf", projected, down_lift, precision=lax.Precision.HIGHEST).reshape(TOKENS, FF)
        partition_contribution = frozen_path_part + ADAPTER_SCALE * rank_raised
        rounded_term = lax.optimization_barrier(partition_contribution.astype(jnp.bfloat16)).astype(jnp.float32)
        rounded_proj = lax.optimization_barrier(projected.reshape(TOKENS, R).astype(jnp.bfloat16)).astype(jnp.float32)
        return (hidden_sum + rounded_term, down_sum + rounded_proj), None

    initial = (jnp.zeros((TOKENS, FF), jnp.float32), jnp.zeros((TOKENS, R), jnp.float32))
    (hidden_grad, down_sum), unused = lax.scan(shard_step, initial, jnp.arange(N_TENSOR, dtype=jnp.int32))
    down_in = down_sum.astype(jnp.bfloat16)
    hidden, gate_grad, up_grad = swiglu_grads(hidden_grad, gate_pre, up_pre)

    gate_blocks = gate_grad.reshape(blocks_all, BLOCK, FF).astype(jnp.float32)
    up_blocks = up_grad.reshape(blocks_all, BLOCK, FF).astype(jnp.float32)
    gu_proj = adapter_b_gu[block_tenant].astype(jnp.float32)
    query_gate = jnp.einsum("bnf,brf->bnr", gate_blocks, gu_proj[:, :R], precision=lax.Precision.HIGHEST)
    query_up = jnp.einsum("bnf,brf->bnr", up_blocks, gu_proj[:, R:], precision=lax.Precision.HIGHEST)
    query = jnp.concatenate([query_gate, query_up], axis=2)
    gu_lift = adapter_a_gu[block_tenant].astype(jnp.float32)
    frozen_path_input = jnp.dot(gate_grad, gate_weight.T, preferred_element_type=jnp.float32) + jnp.dot(up_grad, up_weight.T, preferred_element_type=jnp.float32)
    rank_raised_input = jnp.einsum("bnr,bdr->bnd", query, gu_lift, precision=lax.Precision.HIGHEST).reshape(TOKENS, D)
    block_input_grad = (frozen_path_input + ADAPTER_SCALE * rank_raised_input).astype(jnp.bfloat16)
    query_low = lax.optimization_barrier(query.astype(jnp.bfloat16)).astype(jnp.float32)

    input_blocks = layer_input.reshape(blocks_all, BLOCK, D).astype(jnp.float32)
    grad_a_gu = combine(tenant_indicator, jnp.einsum("bnd,bnr->bdr", input_blocks, query_low, precision=lax.Precision.HIGHEST))
    adapter_rows = adapter_acts.reshape(blocks_all, BLOCK, 3 * R).astype(jnp.float32)
    bgrad_gate = jnp.einsum("bnr,bnf->brf", adapter_rows[:, :, :R], gate_blocks, precision=lax.Precision.HIGHEST)
    bgrad_up = jnp.einsum("bnr,bnf->brf", adapter_rows[:, :, R:2 * R], up_blocks, precision=lax.Precision.HIGHEST)
    grad_b_gu = combine(tenant_indicator, jnp.concatenate([bgrad_gate, bgrad_up], axis=1))
    hidden_blocks = hidden.reshape(blocks_all, BLOCK, FF).astype(jnp.float32)
    down_blocks = down_in.reshape(blocks_all, BLOCK, R).astype(jnp.float32)
    grad_a_down = combine(tenant_indicator, jnp.einsum("bnf,bnr->bfr", hidden_blocks, down_blocks, precision=lax.Precision.HIGHEST))
    grad_blocks = out_grad.reshape(blocks_all, BLOCK, D).astype(jnp.float32)
    grad_b_down = combine(tenant_indicator, jnp.einsum("bnr,bnd->brd", adapter_rows[:, :, 2 * R:], grad_blocks, precision=lax.Precision.HIGHEST))
    return block_input_grad, grad_a_gu, grad_b_gu, grad_a_down, grad_b_down
```

```python
import functools

import jax
import jax.numpy as jnp
from jax import lax
from jax.experimental import pallas as pl
from jax.experimental.pallas import tpu as pltpu
from jax.sharding import PartitionSpec as P

R = 16
TENANTS = 4
BLOCK = 128
CHUNKS = 2
LANES = 128
VMEM_LIMIT = 56 * 1024 * 1024

ADAPTER_SCALE = 2.0

NT = (((1,), (1,)), ((), ()))
NN = (((1,), (0,)), ((), ()))


def fdot(lhs, rhs, dims):
    return lax.dot_general(lhs, rhs, dims, preferred_element_type=jnp.float32)


def tile_of(width, most):
    tile = most
    while width % tile:
        tile -= LANES
    return tile


def whole(shape):
    return pl.BlockSpec(shape, lambda *_: (0,) * len(shape))


def hidden_kernel(sizes, meta, *refs):
    n_dp, n_t, g, own_t, rc, tile = sizes
    ny = n_t // 2
    pieces, (w_ref, bd_ref, ad_ref, keep_ref, send_ref, x_scr, p_scr) = refs[:n_dp], refs[n_dp:]
    step = pl.program_id(0)
    z, t = meta[0], meta[1]
    y, c = t // 2, t % 2
    width = w_ref.shape[1]
    hidden_width = keep_ref.shape[2] - LANES

    @pl.when(step == 0)
    def _():
        for k in range(n_dp):
            for j in range(g):
                owner = lax.rem(z + (n_dp - k), n_dp) * g + j
                away = jnp.where(owner % 2 == c, 0, ny)
                x_scr[away + lax.rem(owner // 2 + ny - y, ny)] = pieces[k][j]
        x_all = x_scr[...].reshape(n_t * rc, width)
        proj = fdot(x_all, bd_ref[...], NT)
        lane = lax.broadcasted_iota(jnp.int32, (rc, TENANTS * R), 1) // R
        zeros = jnp.zeros((rc, LANES - TENANTS * R), jnp.bfloat16)
        for s in range(n_t):
            owner = lax.rem(y + s % ny, ny) * 2 + (c if s < ny else 1 - c)
            tenant = meta[2 + (owner * own_t) // BLOCK]
            own = jnp.where(lane == tenant, proj[s * rc : (s + 1) * rc], 0.0)
            p_scr[s * rc : (s + 1) * rc, :] = (ADAPTER_SCALE * own).astype(jnp.bfloat16)
            out = keep_ref if s < ny else send_ref
            out[s % ny, :, hidden_width:] = jnp.concatenate([own.astype(jnp.bfloat16), zeros], axis=1)

    acc = fdot(x_scr[...].reshape(n_t * rc, width), w_ref[...], NT) + fdot(p_scr[...], ad_ref[...], NN)
    acc = acc.astype(jnp.bfloat16).reshape(n_t, rc, tile)
    at = pl.ds(pl.multiple_of(step * tile, LANES), tile)
    keep_ref[:, :, at] = acc[:ny]
    send_ref[:, :, at] = acc[ny:]


def hidden_partial(meta, pieces, down_weight, b_down, a_down, n_t, own_t):
    n_dp = len(pieces)
    g, rc, width = pieces[0].shape
    ny = n_t // 2
    hidden_width = down_weight.shape[0]
    tile = tile_of(hidden_width, 512)
    low = TENANTS * R
    out = jax.ShapeDtypeStruct((ny, rc, hidden_width + LANES), jnp.bfloat16)
    return pl.pallas_call(
        functools.partial(hidden_kernel, (n_dp, n_t, g, own_t, rc, tile)),
        out_shape=(out, out),
        grid_spec=pltpu.PrefetchScalarGridSpec(
            num_scalar_prefetch=1,
            grid=(hidden_width // tile,),
            in_specs=[whole((g, rc, width))] * n_dp
            + [
                pl.BlockSpec((tile, width), lambda f, *_: (f, 0)),
                whole((low, width)),
                pl.BlockSpec((low, tile), lambda f, *_: (0, f)),
            ],
            out_specs=[whole(out.shape)] * 2,
            scratch_shapes=[
                pltpu.VMEM((n_t, rc, width), jnp.bfloat16),
                pltpu.VMEM((n_t * rc, low), jnp.bfloat16),
            ],
        ),
        compiler_params=pltpu.CompilerParams(vmem_limit_bytes=VMEM_LIMIT),
        cost_estimate=pl.CostEstimate(
            flops=2 * n_t * rc * width * hidden_width,
            bytes_accessed=2 * width * hidden_width,
            transcendentals=0,
        ),
        name="hidden_partial",
    )(meta, *pieces, down_weight, b_down, a_down)


def act_kernel(keep_ref, pair_ref, far_ref, dgate_ref, dup_ref, out_ref, low_ref):
    width = out_ref.shape[2]
    total = keep_ref[0].astype(jnp.float32) + pair_ref[0].astype(jnp.float32)
    total = total + far_ref[...].astype(jnp.float32)
    low_ref[...] = total[:, width:].astype(jnp.bfloat16)
    hidden_grad = total[:, :width]
    out_ref[0] = (hidden_grad * dgate_ref[...]).astype(jnp.bfloat16)
    out_ref[1] = (hidden_grad * dup_ref[...]).astype(jnp.bfloat16)


def act(keep, pair, far, dgate, dup, q):
    ny, rc, padded = keep.shape
    width = padded - LANES
    return pl.pallas_call(
        act_kernel,
        out_shape=(
            jax.ShapeDtypeStruct((2, rc, width), jnp.bfloat16),
            jax.ShapeDtypeStruct((rc, LANES), jnp.bfloat16),
        ),
        grid=(1,),
        in_specs=[
            whole((1, rc, padded)),
            whole((1, rc, padded)),
            whole((rc, padded)),
            pl.BlockSpec((rc, width), lambda f: (q, 0)),
            pl.BlockSpec((rc, width), lambda f: (q, 0)),
        ],
        out_specs=[whole((2, rc, width)), whole((rc, LANES))],
        compiler_params=pltpu.CompilerParams(vmem_limit_bytes=VMEM_LIMIT),
        cost_estimate=pl.CostEstimate(
            flops=4 * rc * width, bytes_accessed=18 * rc * width, transcendentals=0
        ),
        name="act_grads",
    )(keep, pair, far, dgate, dup)


def owner_of(p, y, c, ny):
    return lax.rem(y + ny - p // 2, ny) * 2 + (c if p % 2 == 0 else 1 - c)


def input_kernel(sizes, meta, *refs):
    n_dp, n_t, g, own_t, rc, tile = sizes
    ny = n_t // 2
    pieces, (gw_ref, uw_ref, b_ref, a_ref), refs = refs[:n_t], refs[n_t : n_t + 4], refs[n_t + 4 :]
    outs, queries, (g_scr, u_scr, q_scr) = refs[:n_dp], refs[n_dp : 2 * n_dp], refs[2 * n_dp :]
    step = pl.program_id(0)
    z, t = meta[0], meta[1]
    y, c = t // 2, t % 2
    width = gw_ref.shape[1]
    rows = n_t * rc

    @pl.when(step == 0)
    def _():
        for p in range(n_t):
            owner = owner_of(p, y, c, ny)
            slot = lax.rem(owner // g + n_dp - z, n_dp) * g + owner % g
            g_scr[slot] = pieces[p][0]
            u_scr[slot] = pieces[p][1]
        q_gate = fdot(g_scr[...].reshape(rows, width), b_ref[...], NT)
        q_up = fdot(u_scr[...].reshape(rows, width), b_ref[...], NT)
        lane = lax.broadcasted_iota(jnp.int32, (rc, 2 * R * TENANTS), 1)
        for r in range(n_dp):
            for j in range(g):
                s = r * g + j
                owner = lax.rem(z + r, n_dp) * g + j
                tenant = meta[2 + (owner * own_t) // BLOCK]
                at = slice(s * rc, (s + 1) * rc)
                query = jnp.where(lane % (2 * R) < R, q_gate[at], q_up[at])
                query = jnp.where(lane // (2 * R) == tenant, query, 0.0)
                q_scr[at, :] = (ADAPTER_SCALE * query).astype(jnp.bfloat16)
                queries[r][j * rc : (j + 1) * rc, :] = query.astype(jnp.bfloat16)

    acc = fdot(g_scr[...].reshape(rows, width), gw_ref[...], NT)
    acc = acc + fdot(u_scr[...].reshape(rows, width), uw_ref[...], NT)
    acc = acc + fdot(q_scr[...], a_ref[...], NN)
    acc = acc.astype(jnp.bfloat16)
    at = pl.ds(pl.multiple_of(step * tile, LANES), tile)
    for r in range(n_dp):
        outs[r][:, at] = acc[r * g * rc : (r + 1) * g * rc]


def input_partial(meta, pieces, gate_weight, up_weight, b_gu, a_gu, n_dp, own_t):
    n_t = len(pieces)
    _, rc, hidden_width = pieces[0].shape
    g = n_t // n_dp
    width = gate_weight.shape[0]
    tile = tile_of(width, 256)
    low = 2 * R * TENANTS
    rows = n_t * rc
    outs = [jax.ShapeDtypeStruct((g * rc, width), jnp.bfloat16)] * n_dp
    queries = [jax.ShapeDtypeStruct((g * rc, low), jnp.bfloat16)] * n_dp
    result = pl.pallas_call(
        functools.partial(input_kernel, (n_dp, n_t, g, own_t, rc, tile)),
        out_shape=outs + queries,
        grid_spec=pltpu.PrefetchScalarGridSpec(
            num_scalar_prefetch=1,
            grid=(width // tile,),
            in_specs=[whole((2, rc, hidden_width))] * n_t
            + [
                pl.BlockSpec((tile, hidden_width), lambda d, *_: (d, 0)),
                pl.BlockSpec((tile, hidden_width), lambda d, *_: (d, 0)),
                whole((low, hidden_width)),
                pl.BlockSpec((low, tile), lambda d, *_: (0, d)),
            ],
            out_specs=[whole(o.shape) for o in outs + queries],
            scratch_shapes=[
                pltpu.VMEM((n_t, rc, hidden_width), jnp.bfloat16),
                pltpu.VMEM((n_t, rc, hidden_width), jnp.bfloat16),
                pltpu.VMEM((rows, low), jnp.bfloat16),
            ],
        ),
        compiler_params=pltpu.CompilerParams(vmem_limit_bytes=VMEM_LIMIT),
        cost_estimate=pl.CostEstimate(
            flops=4 * rows * width * hidden_width,
            bytes_accessed=4 * width * hidden_width,
            transcendentals=0,
        ),
        name="input_partial",
    )(meta, *pieces, gate_weight, up_weight, b_gu, a_gu)
    return result[:n_dp], result[n_dp:]


def outer_kernel(owners, count, meta, *refs):
    pieces, left_ref, out_ref = refs[:count], refs[count], refs[count + 1]
    for layer in range(out_ref.shape[0]):
        total = None
        for k in range(count):
            owner, q, layer_at = owners(k, meta, layer)
            term = fdot(left_ref[layer, owner, q], pieces[k][layer_at], NN)
            total = term if total is None else total + term
        out_ref[layer] = ADAPTER_SCALE * total


def outer(meta, pieces, left, owners, layers, name):
    count = len(pieces)
    depth, rc, width = pieces[0].shape
    tile = tile_of(width, 512)
    rows = left.shape[3]
    return pl.pallas_call(
        functools.partial(outer_kernel, owners, count),
        out_shape=jax.ShapeDtypeStruct((layers, rows, width), jnp.float32),
        grid_spec=pltpu.PrefetchScalarGridSpec(
            num_scalar_prefetch=1,
            grid=(width // tile,),
            in_specs=[pl.BlockSpec((depth, rc, tile), lambda f, *_: (0, 0, f))] * count
            + [whole(left.shape)],
            out_specs=pl.BlockSpec((layers, rows, tile), lambda f, *_: (0, 0, f)),
        ),
        compiler_params=pltpu.CompilerParams(vmem_limit_bytes=VMEM_LIMIT),
        cost_estimate=pl.CostEstimate(
            flops=2 * count * layers * rows * rc * width,
            bytes_accessed=2 * count * depth * rc * width + 4 * layers * rows * width,
            transcendentals=0,
        ),
        name=name,
    )(meta, *pieces, left)


def ring(n, by):
    return [(k, (k + by) % n) for k in range(n)]


def add32(*terms):
    return sum(term.astype(jnp.float32) for term in terms)


def spread(tenants, parts):
    heads = jnp.arange(TENANTS, dtype=jnp.int32)
    total = 0.0
    for tenant, part in zip(tenants, parts):
        chosen = (heads == tenant).astype(jnp.float32)[:, None, None]
        total = total + chosen * part.astype(jnp.float32)[None]
    return ADAPTER_SCALE * total


def per_device(
    layer_input,
    out_grad,
    gate_pre,
    up_pre,
    adapter_acts,
    gate_weight,
    up_weight,
    down_weight,
    adapter_a_gu,
    adapter_b_gu,
    adapter_a_down,
    adapter_b_down,
    block_tenant,
):
    n_dp, n_t = lax.axis_size("dp"), lax.axis_size("tensor")
    ny = n_t // 2
    z, t = lax.axis_index("dp"), lax.axis_index("tensor")
    y, c = t // 2, t % 2
    own_rows, width = out_grad.shape
    own_t, hidden_width = gate_pre.shape
    tokens = adapter_acts.shape[0]
    g = own_rows // own_t
    rc = own_t // CHUNKS
    assert own_rows == BLOCK and g * own_t == own_rows and n_t == 2 * ny and n_t == g * n_dp

    meta = jnp.concatenate([jnp.stack([z, t]).astype(jnp.int32), block_tenant])
    b_down = adapter_b_down.reshape(TENANTS * R, width)
    a_down = jnp.transpose(adapter_a_down, (0, 2, 1)).reshape(TENANTS * R, hidden_width)
    b_gu = adapter_b_gu.reshape(TENANTS * 2 * R, hidden_width)
    a_gu = jnp.transpose(adapter_a_gu, (0, 2, 1)).reshape(TENANTS * 2 * R, width)

    pair = [(k, k ^ 1) for k in range(n_t)]
    y_next = ring(n_t, 2)
    z_next = ring(n_dp, 1)

    grads = []
    for q in range(CHUNKS):
        piece = out_grad.reshape(g, own_t, width)[:, q * rc : (q + 1) * rc]
        pieces = [piece]
        for _ in range(n_dp - 1):
            piece = lax.ppermute(piece, "dp", z_next)
            pieces.append(piece)
        grads.append(pieces)

    gate_value = gate_pre.astype(jnp.float32)
    up_value = up_pre.astype(jnp.float32)
    sigmoid_value = jax.nn.sigmoid(gate_value)
    hidden = (gate_value * sigmoid_value * up_value).astype(jnp.bfloat16)
    dgate = up_value * sigmoid_value * (1.0 + gate_value * (1.0 - sigmoid_value))
    dup = gate_value * sigmoid_value
    onehot = (
        jnp.arange(TENANTS, dtype=jnp.int32)[:, None] == jnp.repeat(block_tenant, BLOCK)[None, :]
    ).astype(jnp.bfloat16)
    acts = adapter_acts.T.reshape(3, 1, R, tokens) * onehot[None, :, None, :]
    acts = acts.reshape(3, TENANTS * R, n_t, CHUNKS, rc).transpose(0, 2, 3, 1, 4)

    gathered, lows = [], []
    for q in range(CHUNKS):
        keep, send = hidden_partial(meta, grads[q], down_weight, b_down, a_down, n_t, own_t)
        other = lax.ppermute(send, "tensor", pair)
        message = add32(keep[ny - 1], other[ny - 1]).astype(jnp.bfloat16)
        for s in range(ny - 1):
            far = lax.ppermute(message, "tensor", y_next)
            if s < ny - 2:
                message = add32(keep[ny - 2 - s], other[ny - 2 - s], far).astype(jnp.bfloat16)
        own, low = act(keep, other, far, dgate, dup, q)
        lows.append(low)
        pieces = [own, lax.ppermute(own, "tensor", pair)]
        for _ in range(ny - 1):
            own = lax.ppermute(own, "tensor", y_next)
            pieces += [own, lax.ppermute(own, "tensor", pair)]
        gathered.append(pieces)

    low = jnp.concatenate(lows, axis=0)[:, : TENANTS * R]
    a_part = lax.dot_general(low, hidden, (((0,), (0,)), ((), ())), preferred_element_type=jnp.float32)
    a_part = a_part.reshape(TENANTS, R, hidden_width).sum(0).astype(jnp.bfloat16)
    column = [a_part] + [lax.ppermute(a_part, "tensor", ring(n_t, 2 * s)) for s in range(1, ny)]
    beside = lax.ppermute(jnp.concatenate(column, axis=0), "tensor", pair)
    a_parts = []
    for s in range(ny):
        a_parts += [column[s], beside[s * R : (s + 1) * R]]
    a_tenants = [block_tenant[(owner_of(p, y, c, ny) * own_t) // BLOCK] for p in range(n_t)]
    grad_a_down = spread(a_tenants, a_parts).transpose(0, 2, 1)

    input_parts, in_parts = [], 0.0
    for q in range(CHUNKS):
        outs, queries = input_partial(
            meta, gathered[q], gate_weight, up_weight, b_gu, a_gu, n_dp, own_t
        )
        query = add32(
            queries[0], *[lax.ppermute(queries[r], "dp", ring(n_dp, r)) for r in range(1, n_dp)]
        ).astype(jnp.bfloat16)
        rows_in = layer_input.reshape(g, own_t, width)[:, q * rc : (q + 1) * rc].reshape(g * rc, width)
        part = lax.dot_general(query, rows_in, (((0,), (0,)), ((), ())), preferred_element_type=jnp.float32)
        in_parts = in_parts + part.reshape(TENANTS, 2 * R, width).sum(0)
        message = outs[n_dp - 1]
        for s in range(n_dp - 1):
            message = lax.ppermute(message, "dp", z_next)
            message = add32(message, outs[n_dp - 2 - s]).astype(jnp.bfloat16)
        input_parts.append(message.reshape(g, rc, width))
    block_input_grad = jnp.concatenate(input_parts, axis=1).reshape(own_rows, width)

    in_part = in_parts.astype(jnp.bfloat16)
    in_all = [in_part] + [lax.ppermute(in_part, "dp", ring(n_dp, r)) for r in range(1, n_dp)]
    in_tenants = [block_tenant[lax.rem(z + n_dp - r, n_dp)] for r in range(n_dp)]
    grad_a_gu = spread(in_tenants, in_all).transpose(0, 2, 1)

    def grad_owner(k, meta, layer):
        q, k = divmod(k, n_dp * g)
        k, j = divmod(k, g)
        return lax.rem(meta[0] + (n_dp - k), n_dp) * g + j, q, 0

    def gathered_owner(k, meta, layer):
        q, p = divmod(k, n_t)
        return owner_of(p, meta[1] // 2, meta[1] % 2, ny), q, layer

    x_pieces = [x[j : j + 1] for pieces in grads for x in pieces for j in range(g)]
    grad_b_down = outer(meta, x_pieces, acts[2:], grad_owner, 1, "down_outer")
    grad_b_down = grad_b_down.reshape(TENANTS, R, width)
    gu_pieces = [piece for pieces in gathered for piece in pieces]
    grad_b_gu = outer(meta, gu_pieces, acts[:2], gathered_owner, 2, "gate_up_outer")
    grad_b_gu = grad_b_gu.reshape(2, TENANTS, R, hidden_width).transpose(1, 0, 2, 3)
    grad_b_gu = grad_b_gu.reshape(TENANTS, 2 * R, hidden_width)
    return (block_input_grad, grad_a_gu, grad_b_gu, grad_a_down, grad_b_down)


def solution(mesh):
    placed = (
        P(("groups", "dp"), "tensor"),
        P(("groups", "dp"), "tensor"),
        P(("groups", "tensor"), "dp"),
        P(("groups", "tensor"), "dp"),
        P("groups", None),
        P("tensor", "dp"),
        P("tensor", "dp"),
        P("dp", "tensor"),
        P(None, "tensor", None),
        P(None, None, "dp"),
        P(None, "dp", None),
        P(None, None, "tensor"),
        P("groups"),
    )
    return jax.shard_map(
        per_device,
        mesh=mesh,
        in_specs=placed,
        out_specs=(
            P(("groups", "dp"), "tensor"),
            P("groups", "tensor", None),
            P("groups", None, "dp"),
            P("groups", "dp", None),
            P("groups", None, "tensor"),
        ),
        check_vma=False,
    )
```

```python
import functools

import jax
import jax.numpy as jnp
from jax import lax
from jax.experimental import pallas as pl
from jax.experimental.pallas import tpu as pltpu
from jax.sharding import PartitionSpec as P

R = 16
TENANTS = 4
BLOCK = 128
SHARES = (1, 2, 1)
LANES = 128
VMEM_LIMIT = 56 * 1024 * 1024

ADAPTER_SCALE = 2.0

NT = (((1,), (1,)), ((), ()))
NN = (((1,), (0,)), ((), ()))


def fdot(lhs, rhs, dims):
    return lax.dot_general(lhs, rhs, dims, preferred_element_type=jnp.float32)


def tile_of(width, most):
    tile = most
    while width % tile:
        tile -= LANES
    return tile


def whole(shape):
    return pl.BlockSpec(shape, lambda *_: (0,) * len(shape))


def tenant_of(meta, owner, own_t):
    return meta[2 + (owner * own_t) // BLOCK]


def hidden_kernel(sizes, meta, *refs):
    n_dp, n_t, g, own_t, rc, tile = sizes
    ny = n_t // 2
    pieces, (w_ref, bd_ref, ad_ref, keep_ref, send_ref, x_scr, xt_scr, p_scr) = refs[:n_dp], refs[n_dp:]
    step = pl.program_id(0)
    z, t = meta[0], meta[1]
    y, c = t // 2, t % 2
    width = w_ref.shape[1]
    hidden_width = keep_ref.shape[2] - LANES

    @pl.when(step == 0)
    def _():
        for k in range(n_dp):
            for j in range(g):
                owner = lax.rem(z + (n_dp - k), n_dp) * g + j
                away = jnp.where(owner % 2 == c, 0, ny)
                x_scr[away + lax.rem(owner // 2 + ny - y, ny)] = pieces[k][j]
        x_all = x_scr[...].reshape(n_t * rc, width)
        xt_scr[...] = x_all.T
        proj = fdot(x_all, bd_ref[...], NT)
        lane = lax.broadcasted_iota(jnp.int32, (rc, TENANTS * R), 1) // R
        zeros = jnp.zeros((rc, LANES - TENANTS * R), jnp.bfloat16)
        for s in range(n_t):
            owner = lax.rem(y + s % ny, ny) * 2 + (c if s < ny else 1 - c)
            own = jnp.where(lane == tenant_of(meta, owner, own_t), proj[s * rc : (s + 1) * rc], 0.0)
            p_scr[s * rc : (s + 1) * rc, :] = (ADAPTER_SCALE * own).astype(jnp.bfloat16)
            out = keep_ref if s < ny else send_ref
            out[s % ny, :, hidden_width:] = jnp.concatenate([own.astype(jnp.bfloat16), zeros], axis=1)

    acc = fdot(w_ref[...], xt_scr[...], NN).T + fdot(p_scr[...], ad_ref[...], NN)
    acc = acc.astype(jnp.bfloat16).reshape(n_t, rc, tile)
    at = pl.ds(pl.multiple_of(step * tile, LANES), tile)
    keep_ref[:, :, at] = acc[:ny]
    send_ref[:, :, at] = acc[ny:]


def hidden_partial(meta, pieces, down_weight, b_down, a_down, n_t, own_t):
    n_dp = len(pieces)
    g, rc, width = pieces[0].shape
    ny = n_t // 2
    hidden_width = down_weight.shape[0]
    tile = tile_of(hidden_width, 512)
    low = TENANTS * R
    out = jax.ShapeDtypeStruct((ny, rc, hidden_width + LANES), jnp.bfloat16)
    return pl.pallas_call(
        functools.partial(hidden_kernel, (n_dp, n_t, g, own_t, rc, tile)),
        out_shape=(out, out),
        grid_spec=pltpu.PrefetchScalarGridSpec(
            num_scalar_prefetch=1,
            grid=(hidden_width // tile,),
            in_specs=[whole((g, rc, width))] * n_dp
            + [
                pl.BlockSpec((tile, width), lambda f, *_: (f, 0)),
                whole((low, width)),
                pl.BlockSpec((low, tile), lambda f, *_: (0, f)),
            ],
            out_specs=[whole(out.shape)] * 2,
            scratch_shapes=[
                pltpu.VMEM((n_t, rc, width), jnp.bfloat16),
                pltpu.VMEM((width, n_t * rc), jnp.bfloat16),
                pltpu.VMEM((n_t * rc, low), jnp.bfloat16),
            ],
        ),
        compiler_params=pltpu.CompilerParams(vmem_limit_bytes=VMEM_LIMIT),
        cost_estimate=pl.CostEstimate(
            flops=2 * n_t * rc * width * hidden_width,
            bytes_accessed=2 * width * hidden_width,
            transcendentals=0,
        ),
        name="hidden_partial",
    )(meta, *pieces, down_weight, b_down, a_down)


def act_kernel(keep_ref, pair_ref, far_ref, dgate_ref, dup_ref, out_ref, low_ref):
    width = out_ref.shape[2]
    total = keep_ref[0].astype(jnp.float32) + pair_ref[0].astype(jnp.float32)
    total = total + far_ref[...].astype(jnp.float32)
    low_ref[...] = total[:, width:].astype(jnp.bfloat16)
    hidden_grad = total[:, :width]
    out_ref[0] = (hidden_grad * dgate_ref[...]).astype(jnp.bfloat16)
    out_ref[1] = (hidden_grad * dup_ref[...]).astype(jnp.bfloat16)


def act(keep, pair, far, dgate, dup):
    ny, rc, padded = keep.shape
    width = padded - LANES
    return pl.pallas_call(
        act_kernel,
        out_shape=(
            jax.ShapeDtypeStruct((2, rc, width), jnp.bfloat16),
            jax.ShapeDtypeStruct((rc, LANES), jnp.bfloat16),
        ),
        grid=(1,),
        in_specs=[
            whole((1, rc, padded)),
            whole((1, rc, padded)),
            whole((rc, padded)),
            whole((rc, width)),
            whole((rc, width)),
        ],
        out_specs=[whole((2, rc, width)), whole((rc, LANES))],
        compiler_params=pltpu.CompilerParams(vmem_limit_bytes=VMEM_LIMIT),
        cost_estimate=pl.CostEstimate(
            flops=4 * rc * width, bytes_accessed=18 * rc * width, transcendentals=0
        ),
        name="act_grads",
    )(keep, pair, far, dgate, dup)


def owner_of(p, y, c, ny):
    return lax.rem(y + ny - p // 2, ny) * 2 + (c if p % 2 == 0 else 1 - c)


def input_kernel(sizes, meta, *refs):
    n_dp, n_t, g, own_t, rc, tile = sizes
    ny = n_t // 2
    pieces, (gw_ref, uw_ref, b_ref, a_ref), refs = refs[:n_t], refs[n_t : n_t + 4], refs[n_t + 4 :]
    outs, (g_scr, u_scr, acc, query) = refs[:n_dp], refs[n_dp:]
    step = pl.program_id(0)
    z, t = meta[0], meta[1]
    y, c = t // 2, t % 2
    rows = n_t * rc
    width = gw_ref.shape[0]

    @pl.when(step == 0)
    def _():
        acc[...] = jnp.zeros_like(acc)
        query[...] = jnp.zeros_like(query)

    for p in range(n_t):
        owner = owner_of(p, y, c, ny)
        slot = lax.rem(owner // g + n_dp - z, n_dp) * g + owner % g
        g_scr[slot] = pieces[p][0]
        u_scr[slot] = pieces[p][1]
    gate = g_scr[...].reshape(rows, tile).T
    up = u_scr[...].reshape(rows, tile).T
    low = lax.broadcasted_iota(jnp.int32, (2 * R * TENANTS, rows), 0) % (2 * R)
    query[...] += jnp.where(low < R, fdot(b_ref[...], gate, NN), fdot(b_ref[...], up, NN))
    acc[...] += fdot(gw_ref[...], gate, NN) + fdot(uw_ref[...], up, NN)

    @pl.when(step == pl.num_programs(0) - 1)
    def _():
        lane = lax.broadcasted_iota(jnp.int32, (rc, 2 * R * TENANTS), 1) // (2 * R)
        turned = query[...].T
        own = []
        for r in range(n_dp):
            for j in range(g):
                s = r * g + j
                tenant = tenant_of(meta, lax.rem(z + r, n_dp) * g + j, own_t)
                own.append(jnp.where(lane == tenant, turned[s * rc : (s + 1) * rc], 0.0))
        own = (ADAPTER_SCALE * jnp.concatenate(own, axis=0)).astype(jnp.bfloat16)
        cols = tile_of(width, 512)
        for d in range(0, width, cols):
            part = acc[d : d + cols, :].T + fdot(own, a_ref[:, d : d + cols], NN)
            part = part.astype(jnp.bfloat16)
            for r in range(n_dp):
                outs[r][:, d : d + cols] = part[r * g * rc : (r + 1) * g * rc]


def input_partial(meta, pieces, gate_weight, up_weight, b_gu, a_gu, n_dp, own_t):
    n_t = len(pieces)
    _, rc, hidden_width = pieces[0].shape
    g = n_t // n_dp
    width = gate_weight.shape[0]
    tile = tile_of(hidden_width, 512)
    low = 2 * R * TENANTS
    rows = n_t * rc
    outs = [jax.ShapeDtypeStruct((g * rc, width), jnp.bfloat16)] * n_dp
    return pl.pallas_call(
        functools.partial(input_kernel, (n_dp, n_t, g, own_t, rc, tile)),
        out_shape=outs,
        grid_spec=pltpu.PrefetchScalarGridSpec(
            num_scalar_prefetch=1,
            grid=(hidden_width // tile,),
            in_specs=[pl.BlockSpec((2, rc, tile), lambda f, *_: (0, 0, f))] * n_t
            + [
                pl.BlockSpec((width, tile), lambda f, *_: (0, f)),
                pl.BlockSpec((width, tile), lambda f, *_: (0, f)),
                pl.BlockSpec((low, tile), lambda f, *_: (0, f)),
                whole((low, width)),
            ],
            out_specs=[whole(o.shape) for o in outs],
            scratch_shapes=[
                pltpu.VMEM((n_t, rc, tile), jnp.bfloat16),
                pltpu.VMEM((n_t, rc, tile), jnp.bfloat16),
                pltpu.VMEM((width, rows), jnp.float32),
                pltpu.VMEM((low, rows), jnp.float32),
            ],
        ),
        compiler_params=pltpu.CompilerParams(vmem_limit_bytes=VMEM_LIMIT),
        cost_estimate=pl.CostEstimate(
            flops=4 * rows * width * hidden_width,
            bytes_accessed=4 * width * hidden_width,
            transcendentals=0,
        ),
        name="input_partial",
    )(meta, *pieces, gate_weight, up_weight, b_gu, a_gu)


def query_kernel(own_t, count, meta, *refs):
    pieces, b_ref, out_ref = refs[:count], refs[count], refs[count + 1]
    gate = jnp.concatenate([piece[0] for piece in pieces], axis=0)
    up = jnp.concatenate([piece[1] for piece in pieces], axis=0)
    lane = lax.broadcasted_iota(jnp.int32, out_ref.shape, 1)
    query = jnp.where(lane % (2 * R) < R, fdot(gate, b_ref[...], NT), fdot(up, b_ref[...], NT))
    tenant = tenant_of(meta, meta[1], own_t)
    out_ref[...] = jnp.where(lane // (2 * R) == tenant, query, 0.0).astype(jnp.bfloat16)


def own_query(meta, pieces, b_gu, own_t):
    out = jax.ShapeDtypeStruct((own_t, b_gu.shape[0]), jnp.bfloat16)
    return pl.pallas_call(
        functools.partial(query_kernel, own_t, len(pieces)),
        out_shape=out,
        grid_spec=pltpu.PrefetchScalarGridSpec(
            num_scalar_prefetch=1,
            grid=(1,),
            in_specs=[whole(piece.shape) for piece in pieces] + [whole(b_gu.shape)],
            out_specs=whole(out.shape),
        ),
        compiler_params=pltpu.CompilerParams(vmem_limit_bytes=VMEM_LIMIT),
        name="own_query",
    )(meta, *pieces, b_gu)


def outer_kernel(plan, layers, counts, meta, *refs):
    sources, j_of, owner_at = plan
    pieces, left_ref, out_ref = refs[: counts], refs[counts], refs[counts + 1]
    owners = [owner_at(s, meta) for s in range(len(sources))]
    for layer in range(layers):
        left = jnp.concatenate([left_ref[layer, owner] for owner in owners], axis=1)
        right = [pieces[k][j_of(s, layer)] for s, ks in enumerate(sources) for k in ks]
        out_ref[layer] = ADAPTER_SCALE * fdot(left, jnp.concatenate(right, axis=0), NN)


def outer(meta, pieces, left, plan, layers, name):
    width = pieces[0].shape[2]
    tile = tile_of(width, 512)
    rows = left.shape[2]
    return pl.pallas_call(
        functools.partial(outer_kernel, plan, layers, len(pieces)),
        out_shape=jax.ShapeDtypeStruct((layers, rows, width), jnp.float32),
        grid_spec=pltpu.PrefetchScalarGridSpec(
            num_scalar_prefetch=1,
            grid=(width // tile,),
            in_specs=[
                pl.BlockSpec(piece.shape[:2] + (tile,), lambda f, *_: (0, 0, f)) for piece in pieces
            ]
            + [whole(left.shape)],
            out_specs=pl.BlockSpec((layers, rows, tile), lambda f, *_: (0, 0, f)),
        ),
        compiler_params=pltpu.CompilerParams(vmem_limit_bytes=VMEM_LIMIT),
        name=name,
    )(meta, *pieces, left)


def spread_kernel(tenant_at, rows, meta, *refs):
    parts, out_ref = refs[:-1], refs[-1]
    out_ref[...] = jnp.zeros_like(out_ref)
    at = 0
    for part in parts:
        for k in range(part.shape[0] // rows):
            tenant = tenant_at(at, meta)
            term = part[k * rows : (k + 1) * rows].astype(jnp.float32)
            out_ref[tenant] = out_ref[tenant] + ADAPTER_SCALE * term
            at += 1


def spread(meta, parts, tenant_at, rows, name):
    width = parts[0].shape[1]
    out = jax.ShapeDtypeStruct((TENANTS, rows, width), jnp.float32)
    tile = tile_of(width, 1024)
    return pl.pallas_call(
        functools.partial(spread_kernel, tenant_at, rows),
        out_shape=out,
        grid_spec=pltpu.PrefetchScalarGridSpec(
            num_scalar_prefetch=1,
            grid=(width // tile,),
            in_specs=[pl.BlockSpec((part.shape[0], tile), lambda f, *_: (0, f)) for part in parts],
            out_specs=pl.BlockSpec((TENANTS, rows, tile), lambda f, *_: (0, 0, f)),
        ),
        compiler_params=pltpu.CompilerParams(vmem_limit_bytes=VMEM_LIMIT),
        name=name,
    )(meta, *parts)


def ring(n, by):
    return [(k, (k + by) % n) for k in range(n)]


def add32(*terms):
    return sum(term.astype(jnp.float32) for term in terms)


def after(value, *done):
    return lax.optimization_barrier((value,) + done)[0]


def per_device(
    layer_input,
    out_grad,
    gate_pre,
    up_pre,
    adapter_acts,
    gate_weight,
    up_weight,
    down_weight,
    adapter_a_gu,
    adapter_b_gu,
    adapter_a_down,
    adapter_b_down,
    block_tenant,
):
    n_dp, n_t = lax.axis_size("dp"), lax.axis_size("tensor")
    ny = n_t // 2
    z, t = lax.axis_index("dp"), lax.axis_index("tensor")
    own_rows, width = out_grad.shape
    own_t, hidden_width = gate_pre.shape
    tokens = adapter_acts.shape[0]
    g = own_rows // own_t
    assert own_rows == BLOCK and g * own_t == own_rows and n_t == 2 * ny and n_t == g * n_dp
    chunks, at = [], 0
    for share in SHARES:
        chunks.append((at, own_t * share // sum(SHARES)))
        at += chunks[-1][1]

    meta = jnp.concatenate([jnp.stack([z, t]).astype(jnp.int32), block_tenant])
    b_down = adapter_b_down.reshape(TENANTS * R, width)
    a_down = jnp.transpose(adapter_a_down, (0, 2, 1)).reshape(TENANTS * R, hidden_width)
    b_gu = adapter_b_gu.reshape(TENANTS * 2 * R, hidden_width)
    a_gu = jnp.transpose(adapter_a_gu, (0, 2, 1)).reshape(TENANTS * 2 * R, width)

    pair = [(k, k ^ 1) for k in range(n_t)]
    y_next = ring(n_t, 2)
    z_next = ring(n_dp, 1)

    grads, last = [], None
    for at, rc in chunks:
        piece = out_grad.reshape(g, own_t, width)[:, at : at + rc]
        if last is not None:
            piece = after(piece, last)
        pieces = [piece]
        for _ in range(n_dp - 1):
            piece = lax.ppermute(piece, "dp", z_next)
            pieces.append(piece)
        last = pieces[n_dp - 2]
        grads.append(pieces)

    hidden, dgates, dups = [], [], []
    for at, rc in chunks:
        gate_value = gate_pre[at : at + rc].astype(jnp.float32)
        up_value = up_pre[at : at + rc].astype(jnp.float32)
        sigmoid_value = jax.nn.sigmoid(gate_value)
        hidden.append((gate_value * sigmoid_value * up_value).astype(jnp.bfloat16))
        dgates.append(up_value * sigmoid_value * (1.0 + gate_value * (1.0 - sigmoid_value)))
        dups.append(gate_value * sigmoid_value)
    hidden = jnp.concatenate(hidden, axis=0)
    onehot = (
        jnp.arange(TENANTS, dtype=jnp.int32)[:, None] == jnp.repeat(block_tenant, BLOCK)[None, :]
    ).astype(jnp.bfloat16)
    acts = adapter_acts.T.reshape(3, 1, R, tokens) * onehot[None, :, None, :]
    acts = acts.reshape(3, TENANTS * R, n_t, own_t).transpose(0, 2, 1, 3)

    def first(q, done):
        pieces = [after(grads[q][0], *done)] + grads[q][1:]
        keep, send = hidden_partial(meta, pieces, down_weight, b_down, a_down, n_t, own_t)
        return keep, lax.ppermute(send, "tensor", pair)

    def reduce(keep, other):
        message = add32(keep[ny - 1], other[ny - 1]).astype(jnp.bfloat16)
        for s in range(ny - 1):
            far = lax.ppermute(message, "tensor", y_next)
            if s < ny - 2:
                message = add32(keep[ny - 2 - s], other[ny - 2 - s], far).astype(jnp.bfloat16)
        return message, far

    def gather(own, done):
        own = after(own, *done)
        pieces = [own, lax.ppermute(own, "tensor", pair)]
        for _ in range(ny - 1):
            own = lax.ppermute(own, "tensor", y_next)
            pieces += [own, lax.ppermute(own, "tensor", pair)]
        return pieces

    def second(pieces, done):
        pieces = [after(pieces[0], *done)] + pieces[1:]
        outs = input_partial(meta, pieces, gate_weight, up_weight, b_gu, a_gu, n_dp, own_t)
        there = [lax.ppermute(outs[r], "dp", ring(n_dp, r)) for r in range(1, n_dp)]
        return outs, there

    def finish(outs, there, rc):
        return add32(outs[0], *there).astype(jnp.bfloat16).reshape(g, rc, width)

    keep_a, other_a = first(0, ())
    sum_a, far_a = reduce(keep_a, other_a)
    own_a, low_a = act(keep_a, other_a, far_a, dgates[0], dups[0])
    full_a = gather(own_a, ())

    keep_b, other_b = first(1, (own_a,))
    sum_b, far_b = reduce(keep_b, other_b)
    keep_c, other_c = first(2, (sum_b,))
    sum_c, far_c = reduce(keep_c, other_c)
    own_b, low_b = act(after(keep_b, sum_c), other_b, far_b, dgates[1], dups[1])
    full_b = gather(own_b, ())
    own_c, low_c = act(after(keep_c, own_b), other_c, far_c, dgates[2], dups[2])

    query = own_query(meta, [own_a, own_b, own_c], b_gu, own_t)
    query_there = [lax.ppermute(query, "dp", ring(n_dp, r)) for r in range(1, n_dp)]

    outs_a, there_a = second(full_a, (query,))

    low = jnp.concatenate([low_a, low_b, low_c], axis=0)[:, : TENANTS * R]
    a_part = fdot(after(low, outs_a[0]), hidden, (((0,), (0,)), ((), ())))
    a_part = a_part.reshape(TENANTS, R, hidden_width).sum(0).astype(jnp.bfloat16)
    a_column = [a_part] + [lax.ppermute(a_part, "tensor", ring(n_t, 2 * s)) for s in range(1, ny)]

    query = add32(after(query, a_part), *query_there).astype(jnp.bfloat16)
    queries = [query] + [lax.ppermute(query, "tensor", ring(n_t, 2 * s)) for s in range(1, ny)]
    queries = jnp.stack(queries)
    queries = [queries, lax.ppermute(queries, "tensor", pair)]

    full_c = gather(own_c, (full_b[2],))
    outs_b, there_b = second(full_b, (queries[0], full_c[0]))

    a_beside = lax.ppermute(jnp.concatenate(a_column, axis=0), "tensor", pair)
    rows_query = []
    for j in range(g):
        owner = z * g + j
        from_far = lax.rem(t // 2 + ny - owner // 2, ny)
        mine = jnp.where(owner % 2 == t % 2, queries[0], queries[1])
        rows_query.append(lax.dynamic_index_in_dim(mine, from_far, 0, keepdims=False))
    rows_query = jnp.concatenate(rows_query, axis=0)
    in_part = fdot(after(rows_query, outs_b[0]), layer_input, (((0,), (0,)), ((), ())))
    in_part = in_part.reshape(TENANTS, 2 * R, width).sum(0).astype(jnp.bfloat16)
    in_all = [in_part] + [lax.ppermute(in_part, "dp", ring(n_dp, r)) for r in range(1, n_dp)]

    outs_c, there_c = second(full_c, (in_part,))

    def gathered_plan():
        sources = [[q * n_t + p for q in range(len(chunks))] for p in range(n_t)]
        return sources, lambda s, layer: layer, lambda s, m: owner_of(s, m[1] // 2, m[1] % 2, ny)

    def grads_plan():
        sources = [[q * n_dp + s // g for q in range(len(chunks))] for s in range(n_t)]
        return (
            sources,
            lambda s, layer: s % g,
            lambda s, m: lax.rem(m[0] + (n_dp - s // g), n_dp) * g + s % g,
        )

    x_pieces = [x for pieces in grads for x in pieces]
    grad_b_down = outer(meta, x_pieces, after(acts[2:], outs_c[0]), grads_plan(), 1, "down_outer")
    gu_pieces = full_a + full_b + full_c
    left = after(acts[:2], grad_b_down)
    grad_b_gu = outer(meta, gu_pieces, left, gathered_plan(), 2, "gate_up_outer")
    grad_b_down = grad_b_down.reshape(TENANTS, R, width)
    grad_b_gu = grad_b_gu.reshape(2, TENANTS, R, hidden_width).transpose(1, 0, 2, 3)
    grad_b_gu = grad_b_gu.reshape(TENANTS, 2 * R, hidden_width)

    def column_tenant(p, m):
        owner = lax.rem(m[1] // 2 + ny - p % ny, ny) * 2
        return tenant_of(m, owner + (m[1] % 2 if p < ny else 1 - m[1] % 2), own_t)

    grad_a_down = spread(meta, a_column + [a_beside], column_tenant, R, "spread_a_down")
    grad_a_gu = spread(
        meta, in_all, lambda r, m: m[2 + lax.rem(m[0] + n_dp - r, n_dp)], 2 * R, "spread_a_gu"
    )

    parts = [
        finish(outs, there, rc)
        for (outs, there), (_, rc) in zip(
            ((outs_a, there_a), (outs_b, there_b), (outs_c, there_c)), chunks
        )
    ]
    block_input_grad = jnp.concatenate(parts, axis=1).reshape(own_rows, width)
    return (
        block_input_grad,
        grad_a_gu.transpose(0, 2, 1),
        grad_b_gu,
        grad_a_down.transpose(0, 2, 1),
        grad_b_down,
    )


def solution(mesh):
    placed = (
        P(("groups", "dp"), "tensor"),
        P(("groups", "dp"), "tensor"),
        P(("groups", "tensor"), "dp"),
        P(("groups", "tensor"), "dp"),
        P("groups", None),
        P("tensor", "dp"),
        P("tensor", "dp"),
        P("dp", "tensor"),
        P(None, "tensor", None),
        P(None, None, "dp"),
        P(None, "dp", None),
        P(None, None, "tensor"),
        P("groups"),
    )
    return jax.shard_map(
        per_device,
        mesh=mesh,
        in_specs=placed,
        out_specs=(
            P(("groups", "dp"), "tensor"),
            P("groups", "tensor", None),
            P("groups", None, "dp"),
            P("groups", "dp", None),
            P("groups", None, "tensor"),
        ),
        check_vma=False,
    )
```

```python
import functools

import jax
import jax.numpy as jnp
from jax import lax
from jax.experimental import pallas as pl
from jax.experimental.pallas import tpu as pltpu
from jax.sharding import PartitionSpec as P

R = 16
TENANTS = 4
BLOCK = 128
SHARES = (1, 1)
LANES = 128
SLOTS = 4
VMEM_LIMIT = 60 * 1024 * 1024

ADAPTER_SCALE = 2.0

NT = (((1,), (1,)), ((), ()))
NN = (((1,), (0,)), ((), ()))
ANY = pl.BlockSpec(memory_space=pl.ANY)


def fdot(lhs, rhs, dims):
    return lax.dot_general(lhs, rhs, dims, preferred_element_type=jnp.float32)


def tile_of(width, most):
    tile = most
    while width % tile:
        tile -= LANES
    return tile


def whole(shape):
    return pl.BlockSpec(shape, lambda *_: (0,) * len(shape))


def tenant_of(meta, owner, own_t):
    return meta[2 + (owner * own_t) // BLOCK]


def owner_of(p, y, c, ny):
    return lax.rem(y + ny - p // 2, ny) * 2 + (c if p % 2 == 0 else 1 - c)


def hidden_kernel(sizes, meta, *refs):
    n_dp, n_t, g, own_t, rc, tile = sizes
    ny = n_t // 2
    pieces, (w_ref, bd_ref, ad_ref, keep_ref, send_ref), refs = refs[:n_dp], refs[n_dp : n_dp + 5], refs[n_dp + 5 :]
    x_scr, xt_scr, p_scr, w_scr, x_sem, w_sem = refs
    z, t = meta[0], meta[1]
    y, c = t // 2, t % 2
    width = w_ref.shape[1]
    hidden_width = w_ref.shape[0]
    steps = hidden_width // tile

    x_copies = []
    for k in range(n_dp):
        for j in range(g):
            owner = lax.rem(z + (n_dp - k), n_dp) * g + j
            away = jnp.where(owner % 2 == c, 0, ny)
            slot = away + lax.rem(owner // 2 + ny - y, ny)
            x_copies.append(pltpu.make_async_copy(pieces[k].at[j], x_scr.at[slot], x_sem.at[k * g + j]))
    w_copies = [
        pltpu.make_async_copy(w_ref.at[pl.ds(f * tile, tile)], w_scr.at[f], w_sem.at[f]) for f in range(steps)
    ]
    for copy in x_copies + w_copies:
        copy.start()
    for copy in x_copies:
        copy.wait()

    x_all = x_scr[...].reshape(n_t * rc, width)
    xt_scr[...] = x_all.T
    proj = fdot(x_all, bd_ref[...], NT)
    lane = lax.broadcasted_iota(jnp.int32, (rc, TENANTS * R), 1) // R
    zeros = jnp.zeros((rc, LANES - TENANTS * R), jnp.bfloat16)
    for s in range(n_t):
        owner = lax.rem(y + s % ny, ny) * 2 + (c if s < ny else 1 - c)
        own = jnp.where(lane == tenant_of(meta, owner, own_t), proj[s * rc : (s + 1) * rc], 0.0)
        p_scr[s * rc : (s + 1) * rc, :] = (ADAPTER_SCALE * own).astype(jnp.bfloat16)
        out = keep_ref if s < ny else send_ref
        out[s % ny, :, hidden_width:] = jnp.concatenate([own.astype(jnp.bfloat16), zeros], axis=1)

    for f in range(steps):
        w_copies[f].wait()
        at = slice(f * tile, (f + 1) * tile)
        acc = fdot(w_scr[f], xt_scr[...], NN).T + fdot(p_scr[...], ad_ref[:, at], NN)
        acc = acc.astype(jnp.bfloat16).reshape(n_t, rc, tile)
        keep_ref[:, :, at] = acc[:ny]
        send_ref[:, :, at] = acc[ny:]


def hidden_partial(meta, pieces, down_weight, b_down, a_down, n_t, own_t):
    n_dp = len(pieces)
    g, rc, width = pieces[0].shape
    ny = n_t // 2
    hidden_width = down_weight.shape[0]
    tile = tile_of(hidden_width, 512)
    steps = hidden_width // tile
    low = TENANTS * R
    out = jax.ShapeDtypeStruct((ny, rc, hidden_width + LANES), jnp.bfloat16)
    return pl.pallas_call(
        functools.partial(hidden_kernel, (n_dp, n_t, g, own_t, rc, tile)),
        out_shape=(out, out),
        grid_spec=pltpu.PrefetchScalarGridSpec(
            num_scalar_prefetch=1,
            grid=(1,),
            in_specs=[ANY] * n_dp + [ANY, whole((low, width)), whole((low, hidden_width))],
            out_specs=[whole(out.shape)] * 2,
            scratch_shapes=[
                pltpu.VMEM((n_t, rc, width), jnp.bfloat16),
                pltpu.VMEM((width, n_t * rc), jnp.bfloat16),
                pltpu.VMEM((n_t * rc, low), jnp.bfloat16),
                pltpu.VMEM((steps, tile, width), jnp.bfloat16),
                pltpu.SemaphoreType.DMA((n_t,)),
                pltpu.SemaphoreType.DMA((steps,)),
            ],
        ),
        compiler_params=pltpu.CompilerParams(vmem_limit_bytes=VMEM_LIMIT),
        cost_estimate=pl.CostEstimate(
            flops=2 * n_t * rc * width * hidden_width,
            bytes_accessed=2 * width * hidden_width,
            transcendentals=0,
        ),
        name="hidden_partial",
    )(meta, *pieces, down_weight, b_down, a_down)


def grads_of(total, factors):
    total = total.astype(jnp.float32)
    return [(total * factors[k].astype(jnp.float32)).astype(jnp.bfloat16) for k in range(2)]


def input_kernel(sizes, meta, *refs):
    n_dp, n_t, g, own_t, rc, tile = sizes
    ny = n_t // 2
    factors, sums, (gw_ref, uw_ref, b_ref, a_ref) = refs[:n_t], refs[n_t : n_t + 2], refs[n_t + 2 : n_t + 6]
    outs, query_ref, refs = refs[n_t + 6 : n_t + 6 + n_dp], refs[n_t + 6 + n_dp], refs[n_t + 7 + n_dp :]
    f_scr, s_scr, w_scr, g_scr, u_scr, acc, query, f_sem, s_sem, w_sem = refs
    z, t = meta[0], meta[1]
    y, c = t // 2, t % 2
    rows = n_t * rc
    width, hidden_width = gw_ref.shape
    steps, slots = hidden_width // tile, w_scr.shape[0]

    copies = []
    for f in range(steps):
        at = pl.ds(f * tile, tile)
        mine = [
            pltpu.make_async_copy(factors[p].at[:, :, at], f_scr.at[f, p], f_sem.at[f, p]) for p in range(n_t)
        ]
        mine += [pltpu.make_async_copy(sums[k].at[:, :, at], s_scr.at[f, k], s_sem.at[f, k]) for k in range(2)]
        mine += [
            pltpu.make_async_copy(w.at[:, at], w_scr.at[f % slots, k], w_sem.at[f, k])
            for k, w in enumerate((gw_ref, uw_ref))
        ]
        copies.append(mine)
    for mine in copies[:slots]:
        for copy in mine:
            copy.start()

    low = lax.broadcasted_iota(jnp.int32, (2 * R * TENANTS, rows), 0) % (2 * R)
    for f in range(steps):
        for copy in copies[f]:
            copy.wait()
        for p in range(n_t):
            owner = owner_of(p, y, c, ny)
            slot = lax.rem(owner // g + n_dp - z, n_dp) * g + owner % g
            total = s_scr[f, p % 2, (ny - p // 2) % ny]
            g_scr[slot], u_scr[slot] = grads_of(total, f_scr[f, p])
        gate = g_scr[...].reshape(rows, tile).T
        up = u_scr[...].reshape(rows, tile).T
        b_part = b_ref[:, f * tile : (f + 1) * tile]
        share = jnp.where(low < R, fdot(b_part, gate, NN), fdot(b_part, up, NN))
        part = fdot(w_scr[f % slots, 0], gate, NN) + fdot(w_scr[f % slots, 1], up, NN)
        if f == 0:
            query[...] = share
            acc[...] = part
        else:
            query[...] += share
            acc[...] += part
        if f + slots < steps:
            for copy in copies[f + slots]:
                copy.start()

    lane = lax.broadcasted_iota(jnp.int32, (2 * R * TENANTS, rows), 1) // rc
    head = lax.broadcasted_iota(jnp.int32, (2 * R * TENANTS, rows), 0) // (2 * R)
    tenants = jnp.zeros((2 * R * TENANTS, rows), jnp.int32)
    for s in range(n_t):
        tenants = jnp.where(lane == s, tenant_of(meta, lax.rem(z + s // g, n_dp) * g + s % g, own_t), tenants)
    own = jnp.where(head == tenants, query[...], 0.0)
    folded = sum(own[e * 2 * R : (e + 1) * 2 * R] for e in range(TENANTS)).astype(jnp.bfloat16)
    for r in range(n_dp):
        query_ref[lax.rem(z + r, n_dp)] = folded[:, r * g * rc : (r + 1) * g * rc]
    own = (ADAPTER_SCALE * own).T.astype(jnp.bfloat16)
    cols = tile_of(width, 512)
    for d in range(0, width, cols):
        part = acc[d : d + cols, :].T + fdot(own, a_ref[:, d : d + cols], NN)
        part = part.astype(jnp.bfloat16)
        for r in range(n_dp):
            outs[r][:, d : d + cols] = part[r * g * rc : (r + 1) * g * rc]


def input_partial(meta, factors, sums, gate_weight, up_weight, b_gu, a_gu, n_dp, own_t):
    n_t = len(factors)
    _, rc, hidden_width = factors[0].shape
    ny = n_t // 2
    g = n_t // n_dp
    width = gate_weight.shape[0]
    tile = tile_of(hidden_width, 512)
    steps = hidden_width // tile
    low = 2 * R * TENANTS
    rows = n_t * rc
    outs = [jax.ShapeDtypeStruct((g * rc, width), jnp.bfloat16)] * n_dp
    outs = outs + [jax.ShapeDtypeStruct((n_dp, 2 * R, g * rc), jnp.bfloat16)]
    result = pl.pallas_call(
        functools.partial(input_kernel, (n_dp, n_t, g, own_t, rc, tile)),
        out_shape=outs,
        grid_spec=pltpu.PrefetchScalarGridSpec(
            num_scalar_prefetch=1,
            grid=(1,),
            in_specs=[ANY] * (n_t + 4) + [whole((low, hidden_width)), whole((low, width))],
            out_specs=[whole(o.shape) for o in outs],
            scratch_shapes=[
                pltpu.VMEM((steps, n_t, 2, rc, tile), jnp.bfloat16),
                pltpu.VMEM((steps, 2, ny, rc, tile), jnp.bfloat16),
                pltpu.VMEM((min(steps, SLOTS), 2, width, tile), jnp.bfloat16),
                pltpu.VMEM((n_t, rc, tile), jnp.bfloat16),
                pltpu.VMEM((n_t, rc, tile), jnp.bfloat16),
                pltpu.VMEM((width, rows), jnp.float32),
                pltpu.VMEM((low, rows), jnp.float32),
                pltpu.SemaphoreType.DMA((steps, n_t)),
                pltpu.SemaphoreType.DMA((steps, 2)),
                pltpu.SemaphoreType.DMA((steps, 2)),
            ],
        ),
        compiler_params=pltpu.CompilerParams(vmem_limit_bytes=VMEM_LIMIT),
        cost_estimate=pl.CostEstimate(
            flops=4 * rows * width * hidden_width,
            bytes_accessed=4 * width * hidden_width,
            transcendentals=0,
        ),
        name="input_partial",
    )(meta, *factors, *sums, gate_weight, up_weight, b_gu, a_gu)
    return result[:n_dp], result[n_dp]


def left_of(left_ref, layer, owners):
    return jnp.concatenate([left_ref[layer, owner] for owner in owners], axis=1)


def down_outer_kernel(n_dp, g, chunks, meta, *refs):
    pieces, (left_ref, out_ref) = refs[: n_dp * chunks], refs[n_dp * chunks :]
    owners = [lax.rem(meta[0] + (n_dp - k), n_dp) * g + j for k in range(n_dp) for j in range(g)]
    right = [pieces[q * n_dp + k][j] for k in range(n_dp) for j in range(g) for q in range(chunks)]
    out = ADAPTER_SCALE * fdot(left_of(left_ref, 0, owners), jnp.concatenate(right, axis=0), NN)
    out_ref[...] = out.reshape(out_ref.shape)


def down_outer(meta, grads, left):
    n_dp, chunks = len(grads[0]), len(grads)
    pieces = [piece for pieces in grads for piece in pieces]
    g, _, width = pieces[0].shape
    tile = tile_of(width, 512)
    return pl.pallas_call(
        functools.partial(down_outer_kernel, n_dp, g, chunks),
        out_shape=jax.ShapeDtypeStruct((TENANTS, R, width), jnp.float32),
        grid_spec=pltpu.PrefetchScalarGridSpec(
            num_scalar_prefetch=1,
            grid=(width // tile,),
            in_specs=[
                pl.BlockSpec(piece.shape[:2] + (tile,), lambda f, *_: (0, 0, f)) for piece in pieces
            ]
            + [whole(left.shape)],
            out_specs=pl.BlockSpec((TENANTS, R, tile), lambda f, *_: (0, 0, f)),
        ),
        compiler_params=pltpu.CompilerParams(vmem_limit_bytes=VMEM_LIMIT),
        name="down_outer",
    )(meta, *pieces, left)


def gate_up_outer_kernel(n_t, meta, *refs):
    ny = n_t // 2
    factors, sums, (left_ref, so_far, out_ref) = refs[:n_t], refs[n_t : n_t + 2], refs[n_t + 2 :]
    y, c = meta[1] // 2, meta[1] % 2
    owners = [owner_of(p, y, c, ny) for p in range(n_t)]
    grads = [grads_of(sums[p % 2][(ny - p // 2) % ny], factors[p]) for p in range(n_t)]
    for layer in range(2):
        right = jnp.concatenate([grad[layer] for grad in grads], axis=0)
        out = ADAPTER_SCALE * fdot(left_of(left_ref, layer, owners), right, NN)
        at = slice(layer * R, (layer + 1) * R)
        out_ref[:, at, :] = so_far[:, at, :] + out.reshape(TENANTS, R, out.shape[1])


def gate_up_outer(meta, factors, sums, left, so_far):
    n_t = len(factors)
    _, rc, width = factors[0].shape
    tile = tile_of(width, 896)
    block = pl.BlockSpec((TENANTS, 2 * R, tile), lambda f, *_: (0, 0, f))
    return pl.pallas_call(
        functools.partial(gate_up_outer_kernel, n_t),
        out_shape=jax.ShapeDtypeStruct((TENANTS, 2 * R, width), jnp.float32),
        grid_spec=pltpu.PrefetchScalarGridSpec(
            num_scalar_prefetch=1,
            grid=(width // tile,),
            in_specs=[pl.BlockSpec((2, rc, tile), lambda f, *_: (0, 0, f))] * n_t
            + [pl.BlockSpec((n_t // 2, rc, tile), lambda f, *_: (0, 0, f))] * 2
            + [whole(left.shape), block],
            out_specs=block,
        ),
        compiler_params=pltpu.CompilerParams(vmem_limit_bytes=VMEM_LIMIT),
        name="gate_up_outer",
    )(meta, *factors, *sums, left, so_far)


def spread_kernel(tenant_at, rows, meta, *refs):
    parts, out_ref = refs[:-1], refs[-1]
    out_ref[...] = jnp.zeros_like(out_ref)
    at = 0
    for part in parts:
        for k in range(part.shape[0] // rows):
            tenant = tenant_at(at, meta)
            term = part[k * rows : (k + 1) * rows].astype(jnp.float32)
            out_ref[tenant] = out_ref[tenant] + ADAPTER_SCALE * term
            at += 1


def spread(meta, parts, tenant_at, rows, name):
    width = parts[0].shape[1]
    out = jax.ShapeDtypeStruct((TENANTS, rows, width), jnp.float32)
    tile = tile_of(width, 1024)
    return pl.pallas_call(
        functools.partial(spread_kernel, tenant_at, rows),
        out_shape=out,
        grid_spec=pltpu.PrefetchScalarGridSpec(
            num_scalar_prefetch=1,
            grid=(width // tile,),
            in_specs=[pl.BlockSpec((part.shape[0], tile), lambda f, *_: (0, f)) for part in parts],
            out_specs=pl.BlockSpec((TENANTS, rows, tile), lambda f, *_: (0, 0, f)),
        ),
        compiler_params=pltpu.CompilerParams(vmem_limit_bytes=VMEM_LIMIT),
        name=name,
    )(meta, *parts)


def in_outer_kernel(n_dp, chunks, g, meta, *refs):
    queries, inputs, out_ref = refs[:n_dp], refs[n_dp : 2 * n_dp], refs[2 * n_dp]
    out_ref[...] = jnp.zeros_like(out_ref)
    for k in range(n_dp):
        block = lax.rem(meta[0] + n_dp - k, n_dp)
        total = None
        parts = []
        for q in range(chunks):
            total = sum(query[q, block].astype(jnp.float32) for query in queries)
            parts.append(total.astype(jnp.bfloat16))
        rc = parts[0].shape[1] // g
        low = jnp.concatenate([part[:, j * rc : (j + 1) * rc] for j in range(g) for part in parts], axis=1)
        tenant = meta[2 + block]
        out_ref[tenant] = out_ref[tenant] + ADAPTER_SCALE * fdot(low, inputs[k][...], NN)


def in_outer(meta, queries, inputs, g):
    n_dp = len(inputs)
    rows, width = inputs[0].shape
    tile = tile_of(width, 1024)
    return pl.pallas_call(
        functools.partial(in_outer_kernel, n_dp, queries[0].shape[0], g),
        out_shape=jax.ShapeDtypeStruct((TENANTS, 2 * R, width), jnp.float32),
        grid_spec=pltpu.PrefetchScalarGridSpec(
            num_scalar_prefetch=1,
            grid=(width // tile,),
            in_specs=[whole(query.shape) for query in queries]
            + [pl.BlockSpec((rows, tile), lambda f, *_: (0, f))] * n_dp,
            out_specs=pl.BlockSpec((TENANTS, 2 * R, tile), lambda f, *_: (0, 0, f)),
        ),
        compiler_params=pltpu.CompilerParams(vmem_limit_bytes=VMEM_LIMIT),
        name="in_outer",
    )(meta, *queries, *inputs)


def ring(n, by):
    return [(k, (k + by) % n) for k in range(n)]


def add32(*terms):
    return sum(term.astype(jnp.float32) for term in terms)


def after(value, *done):
    return lax.optimization_barrier((value,) + done)[0]


def per_device(
    layer_input,
    out_grad,
    gate_pre,
    up_pre,
    adapter_acts,
    gate_weight,
    up_weight,
    down_weight,
    adapter_a_gu,
    adapter_b_gu,
    adapter_a_down,
    adapter_b_down,
    block_tenant,
):
    n_dp, n_t = lax.axis_size("dp"), lax.axis_size("tensor")
    ny = n_t // 2
    z, t = lax.axis_index("dp"), lax.axis_index("tensor")
    own_rows, width = out_grad.shape
    own_t, hidden_width = gate_pre.shape
    tokens = adapter_acts.shape[0]
    g = own_rows // own_t
    assert own_rows == BLOCK and g * own_t == own_rows and n_t == 2 * ny and n_t == g * n_dp
    chunks, at = [], 0
    for share in SHARES:
        chunks.append((at, own_t * share // sum(SHARES)))
        at += chunks[-1][1]

    meta = jnp.concatenate([jnp.stack([z, t]).astype(jnp.int32), block_tenant])
    b_down = adapter_b_down.reshape(TENANTS * R, width)
    a_down = jnp.transpose(adapter_a_down, (0, 2, 1)).reshape(TENANTS * R, hidden_width)
    b_gu = adapter_b_gu.reshape(TENANTS * 2 * R, hidden_width)
    a_gu = jnp.transpose(adapter_a_gu, (0, 2, 1)).reshape(TENANTS * 2 * R, width)

    pair = [(k, k ^ 1) for k in range(n_t)]
    y_next = ring(n_t, 2)
    z_next = ring(n_dp, 1)

    def factors_of(at, rc):
        gate_value = gate_pre[at : at + rc].astype(jnp.float32)
        up_value = up_pre[at : at + rc].astype(jnp.float32)
        sigmoid_value = jax.nn.sigmoid(gate_value)
        hidden = (gate_value * sigmoid_value * up_value).astype(jnp.bfloat16)
        dgate = up_value * sigmoid_value * (1.0 + gate_value * (1.0 - sigmoid_value))
        dup = gate_value * sigmoid_value
        return hidden, jnp.stack([dgate, dup]).astype(jnp.bfloat16)

    grads, hidden, own_factors = [], [], []
    for at, rc in chunks:
        pieces = [out_grad.reshape(g, own_t, width)[:, at : at + rc]]
        grads.append(pieces)
        mine, factor = factors_of(at, rc)
        hidden.append(mine)
        own_factors.append(factor)
    hidden = jnp.concatenate(hidden, axis=0)
    for _ in range(n_dp - 1):
        for pieces in grads:
            pieces.append(lax.ppermute(pieces[-1], "dp", z_next))
    factors = []
    for factor in own_factors:
        pieces = [factor, lax.ppermute(factor, "tensor", pair)]
        for s in range(1, ny):
            far = lax.ppermute(factor, "tensor", ring(n_t, 2 * s))
            pieces += [far, lax.ppermute(far, "tensor", pair)]
        factors.append(pieces)

    inputs = [after(layer_input, grads[-1][-1])]
    for _ in range(n_dp - 1):
        inputs.append(lax.ppermute(inputs[-1], "dp", z_next))

    onehot = (
        jnp.arange(TENANTS, dtype=jnp.int32)[:, None] == jnp.repeat(block_tenant, BLOCK)[None, :]
    ).astype(jnp.bfloat16)
    acts = adapter_acts.T.reshape(3, 1, R, tokens) * onehot[None, :, None, :]
    acts = acts.reshape(3, TENANTS * R, n_t, own_t).transpose(0, 2, 1, 3)

    def first(q, done):
        pieces = [after(grads[q][0], *done)] + grads[q][1:]
        keep, send = hidden_partial(meta, pieces, down_weight, b_down, a_down, n_t, own_t)
        return keep, lax.ppermute(send, "tensor", pair)

    def exchange(keep, other):
        mine = add32(keep, other).astype(jnp.bfloat16)
        return mine, [lax.ppermute(mine, "tensor", ring(n_t, 2 * s)) for s in range(1, ny)]

    def total(mine, far):
        turned = [jnp.roll(there, -(s + 1), axis=0) for s, there in enumerate(far)]
        both = add32(mine, *turned).astype(jnp.bfloat16)
        return [both, lax.ppermute(both, "tensor", pair)]

    def second(q, sums, done):
        sums = [after(sums[0], *done), sums[1]]
        outs, query = input_partial(
            meta, factors[q], sums, gate_weight, up_weight, b_gu, a_gu, n_dp, own_t
        )
        there = [lax.ppermute(outs[r], "dp", ring(n_dp, r)) for r in range(1, n_dp)]
        return outs[0], query, there

    def finish(out, there, rc, done):
        return add32(after(out, *done), *there).astype(jnp.bfloat16).reshape(g, rc, width)

    keep_a, other_a = first(0, (grads[1][n_dp - 2], *factors[0]))
    mine_a, far_a = exchange(keep_a, other_a)
    keep_b, other_b = first(1, (mine_a, *factors[1]))
    mine_b, far_b = exchange(keep_b, other_b)
    grad_b_down = down_outer(meta, grads, after(acts[2:], mine_b))
    sums_a = total(after(mine_a, grad_b_down), far_a)
    out_a, query_a, there_a = second(0, sums_a, ())
    left = [acts[:2, :, :, at : at + rc] for at, rc in chunks]
    zeros = jnp.zeros((TENANTS, 2 * R, hidden_width), jnp.float32)
    grad_b_gu = gate_up_outer(meta, factors[0], sums_a, after(left[0], query_a), zeros)
    sums_b = total(after(mine_b, grad_b_gu, inputs[-1], there_a[0]), far_b)
    out_b, query_b, there_b = second(1, sums_b, ())
    half_a = finish(out_a, there_a, chunks[0][1], (out_b,))

    query = jnp.stack([query_a, query_b])
    queries = [query] + [lax.ppermute(query, "dp", ring(n_dp, r)) for r in range(1, n_dp)]
    low = jnp.concatenate([sums_a[0][0], sums_b[0][0]], axis=0)
    low = after(low[:, hidden_width : hidden_width + TENANTS * R], half_a)
    a_part = fdot(low, hidden, (((0,), (0,)), ((), ())))
    a_part = a_part.reshape(TENANTS, R, hidden_width).sum(0).astype(jnp.bfloat16)
    a_column = [a_part] + [lax.ppermute(a_part, "tensor", ring(n_t, 2 * s)) for s in range(1, ny)]
    grad_b_gu = gate_up_outer(meta, factors[1], sums_b, after(left[1], a_part), grad_b_gu)
    a_beside = lax.ppermute(jnp.concatenate(a_column, axis=0), "tensor", pair)
    grad_a_gu = in_outer(meta, [after(queries[0], grad_b_gu)] + queries[1:], inputs, g)

    def column_tenant(p, m):
        owner = lax.rem(m[1] // 2 + ny - p % ny, ny) * 2
        return tenant_of(m, owner + (m[1] % 2 if p < ny else 1 - m[1] % 2), own_t)

    a_column[0] = after(a_column[0], grad_a_gu)
    grad_a_down = spread(meta, a_column + [a_beside], column_tenant, R, "spread_a_down")
    half_b = finish(out_b, there_b, chunks[1][1], (grad_a_down,))
    block_input_grad = jnp.concatenate([half_a, half_b], axis=1).reshape(own_rows, width)
    return (
        block_input_grad,
        grad_a_gu.transpose(0, 2, 1),
        grad_b_gu,
        grad_a_down.transpose(0, 2, 1),
        grad_b_down,
    )


def solution(mesh):
    placed = (
        P(("groups", "dp"), "tensor"),
        P(("groups", "dp"), "tensor"),
        P(("groups", "tensor"), "dp"),
        P(("groups", "tensor"), "dp"),
        P("groups", None),
        P("tensor", "dp"),
        P("tensor", "dp"),
        P("dp", "tensor"),
        P(None, "tensor", None),
        P(None, None, "dp"),
        P(None, "dp", None),
        P(None, None, "tensor"),
        P("groups"),
    )
    return jax.shard_map(
        per_device,
        mesh=mesh,
        in_specs=placed,
        out_specs=(
            P(("groups", "dp"), "tensor"),
            P("groups", "tensor", None),
            P("groups", None, "dp"),
            P("groups", "dp", None),
            P("groups", None, "tensor"),
        ),
        check_vma=False,
    )
```

```python
import functools

import jax
import jax.numpy as jnp
from jax import lax
from jax.experimental import pallas as pl
from jax.experimental.pallas import tpu as pltpu
from jax.sharding import PartitionSpec as P

R = 16
TENANTS = 4
BLOCK = 128
SHARES = (1, 1)
LANES = 128
VMEM_LIMIT = 60 * 1024 * 1024

ADAPTER_SCALE = 2.0

NT = (((1,), (1,)), ((), ()))
NN = (((1,), (0,)), ((), ()))
TN = (((0,), (0,)), ((), ()))
NO_COST = pl.CostEstimate(flops=1, bytes_accessed=1, transcendentals=0)


def fdot(lhs, rhs, dims):
    return lax.dot_general(lhs, rhs, dims, preferred_element_type=jnp.float32)


def tile_of(width, most):
    tile = most
    while width % tile:
        tile -= LANES
    return tile


def whole(shape):
    return pl.BlockSpec(shape, lambda *_: (0,) * len(shape))


def tenant_of(meta, owner, own_t):
    return meta[2 + (owner * own_t) // BLOCK]


def owner_of(p, y, c, ny):
    return lax.rem(y + ny - p // 2, ny) * 2 + (c if p % 2 == 0 else 1 - c)


def hidden_kernel(sizes, meta, *refs):
    n_dp, n_t, g, own_t, rc, tile = sizes
    ny = n_t // 2
    pieces, (w_ref, bd_ref, ad_ref, keep_ref, send_ref, x_scr, p_scr) = refs[:n_dp], refs[n_dp:]
    step = pl.program_id(0)
    z, t = meta[0], meta[1]
    y, c = t // 2, t % 2
    width = w_ref.shape[1]
    hidden_width = keep_ref.shape[2] - LANES

    @pl.when(step == 0)
    def _():
        for k in range(n_dp):
            for j in range(g):
                owner = lax.rem(z + (n_dp - k), n_dp) * g + j
                away = jnp.where(owner % 2 == c, 0, ny)
                x_scr[away + lax.rem(owner // 2 + ny - y, ny)] = pieces[k][j]
        proj = fdot(x_scr[...].reshape(n_t * rc, width), bd_ref[...], NT)
        lane = lax.broadcasted_iota(jnp.int32, (rc, TENANTS * R), 1) // R
        zeros = jnp.zeros((rc, LANES - TENANTS * R), jnp.bfloat16)
        for s in range(n_t):
            owner = lax.rem(y + s % ny, ny) * 2 + (c if s < ny else 1 - c)
            own = jnp.where(lane == tenant_of(meta, owner, own_t), proj[s * rc : (s + 1) * rc], 0.0)
            p_scr[s * rc : (s + 1) * rc, :] = (ADAPTER_SCALE * own).astype(jnp.bfloat16)
            out = keep_ref if s < ny else send_ref
            out[s % ny, :, hidden_width:] = jnp.concatenate([own.astype(jnp.bfloat16), zeros], axis=1)

    acc = fdot(x_scr[...].reshape(n_t * rc, width), w_ref[...], NT) + fdot(p_scr[...], ad_ref[...], NN)
    acc = acc.astype(jnp.bfloat16).reshape(n_t, rc, tile)
    at = pl.ds(pl.multiple_of(step * tile, LANES), tile)
    keep_ref[:, :, at] = acc[:ny]
    send_ref[:, :, at] = acc[ny:]


def hidden_partial(meta, pieces, down_weight, b_down, a_down, n_t, own_t):
    n_dp = len(pieces)
    g, rc, width = pieces[0].shape
    ny = n_t // 2
    hidden_width = down_weight.shape[0]
    tile = tile_of(hidden_width, 896)
    low = TENANTS * R
    out = jax.ShapeDtypeStruct((ny, rc, hidden_width + LANES), jnp.bfloat16)
    return pl.pallas_call(
        functools.partial(hidden_kernel, (n_dp, n_t, g, own_t, rc, tile)),
        out_shape=(out, out),
        grid_spec=pltpu.PrefetchScalarGridSpec(
            num_scalar_prefetch=1,
            grid=(hidden_width // tile,),
            in_specs=[whole((g, rc, width))] * n_dp
            + [
                pl.BlockSpec((tile, width), lambda f, *_: (f, 0)),
                whole((low, width)),
                pl.BlockSpec((low, tile), lambda f, *_: (0, f)),
            ],
            out_specs=[whole(out.shape)] * 2,
            scratch_shapes=[
                pltpu.VMEM((n_t, rc, width), jnp.bfloat16),
                pltpu.VMEM((n_t * rc, low), jnp.bfloat16),
            ],
        ),
        compiler_params=pltpu.CompilerParams(vmem_limit_bytes=VMEM_LIMIT),
        cost_estimate=NO_COST,
        name="hidden_partial",
    )(meta, *pieces, down_weight, b_down, a_down)


def grads_of(total, factors):
    total = total.astype(jnp.float32)
    return [(total * factor[...].astype(jnp.float32)).astype(jnp.bfloat16) for factor in factors]


def input_kernel(sizes, meta, *refs):
    n_dp, n_t, g, own_t, rc, tile = sizes
    ny = n_t // 2
    factors, refs = [refs[2 * p : 2 * p + 2] for p in range(n_t)], refs[2 * n_t :]
    sums, (gw_ref, uw_ref, b_ref, a_ref) = refs[:2], refs[2:6]
    outs, (g_scr, u_scr, acc, query) = refs[6 : 6 + n_dp], refs[6 + n_dp :]
    step = pl.program_id(0)
    z, t = meta[0], meta[1]
    y, c = t // 2, t % 2
    rows = n_t * rc
    width = gw_ref.shape[0]

    @pl.when(step == 0)
    def _():
        acc[...] = jnp.zeros_like(acc)
        query[...] = jnp.zeros_like(query)

    for p in range(n_t):
        owner = owner_of(p, y, c, ny)
        slot = lax.rem(owner // g + n_dp - z, n_dp) * g + owner % g
        g_scr[slot], u_scr[slot] = grads_of(sums[p % 2][(ny - p // 2) % ny], factors[p])
    gate = g_scr[...].reshape(rows, tile).T
    up = u_scr[...].reshape(rows, tile).T
    low = lax.broadcasted_iota(jnp.int32, (2 * R * TENANTS, rows), 0) % (2 * R)
    query[...] += jnp.where(low < R, fdot(b_ref[...], gate, NN), fdot(b_ref[...], up, NN))
    cols = tile_of(width, 512)
    for d in range(0, width, cols):
        at = slice(d, d + cols)
        acc[at, :] += fdot(gw_ref[at, :], gate, NN) + fdot(uw_ref[at, :], up, NN)

    @pl.when(step == pl.num_programs(0) - 1)
    def _():
        lane = lax.broadcasted_iota(jnp.int32, (rc, 2 * R * TENANTS), 1) // (2 * R)
        turned = query[...].T
        own, shares = [], []
        for r in range(n_dp):
            share = []
            for j in range(g):
                s = r * g + j
                tenant = tenant_of(meta, lax.rem(z + r, n_dp) * g + j, own_t)
                mine = jnp.where(lane == tenant, turned[s * rc : (s + 1) * rc], 0.0)
                own.append(mine)
                share.append(sum(mine[:, e * 2 * R : (e + 1) * 2 * R] for e in range(TENANTS)))
            shares.append(jnp.concatenate(share, axis=0))
        share = jnp.concatenate(shares, axis=1).astype(jnp.bfloat16)
        own = (ADAPTER_SCALE * jnp.concatenate(own, axis=0)).astype(jnp.bfloat16)
        for d in range(0, width, cols):
            part = acc[d : d + cols, :].T + fdot(own, a_ref[:, d : d + cols], NN)
            part = part.astype(jnp.bfloat16)
            for r in range(n_dp):
                outs[r][:, d : d + cols] = part[r * g * rc : (r + 1) * g * rc]
        for r in range(n_dp):
            outs[r][:, width:] = share


def input_partial(meta, factors, q, sums, gate_weight, up_weight, b_gu, a_gu, n_dp, own_t):
    n_t = len(factors)
    ny, rc, _ = sums[0].shape
    g = n_t // n_dp
    width, hidden_width = gate_weight.shape
    tile = tile_of(hidden_width, 512)
    low = 2 * R * TENANTS
    rows = n_t * rc
    outs = [jax.ShapeDtypeStruct((g * rc, width + n_dp * 2 * R), jnp.bfloat16)] * n_dp
    return pl.pallas_call(
        functools.partial(input_kernel, (n_dp, n_t, g, own_t, rc, tile)),
        out_shape=outs,
        grid_spec=pltpu.PrefetchScalarGridSpec(
            num_scalar_prefetch=1,
            grid=(hidden_width // tile,),
            in_specs=[pl.BlockSpec((rc, tile), lambda f, *_: (q, f))] * (2 * n_t)
            + [pl.BlockSpec((ny, rc, tile), lambda f, *_: (0, 0, f))] * 2
            + [pl.BlockSpec((width, tile), lambda f, *_: (0, f))] * 2
            + [pl.BlockSpec((low, tile), lambda f, *_: (0, f)), whole((low, width))],
            out_specs=[whole(o.shape) for o in outs],
            scratch_shapes=[
                pltpu.VMEM((n_t, rc, tile), jnp.bfloat16),
                pltpu.VMEM((n_t, rc, tile), jnp.bfloat16),
                pltpu.VMEM((width, rows), jnp.float32),
                pltpu.VMEM((low, rows), jnp.float32),
            ],
        ),
        compiler_params=pltpu.CompilerParams(vmem_limit_bytes=VMEM_LIMIT),
        cost_estimate=NO_COST,
        name="input_partial",
    )(meta, *[x for pair in factors for x in pair], *sums, gate_weight, up_weight, b_gu, a_gu)


def left_of(left_ref, layer, owners):
    return jnp.concatenate([left_ref[layer, owner] for owner in owners], axis=1)


def down_outer_kernel(n_dp, g, chunks, meta, *refs):
    pieces, (left_ref, out_ref) = refs[: n_dp * chunks], refs[n_dp * chunks :]
    owners = [lax.rem(meta[0] + (n_dp - k), n_dp) * g + j for k in range(n_dp) for j in range(g)]
    right = [pieces[q * n_dp + k][j] for k in range(n_dp) for j in range(g) for q in range(chunks)]
    out = ADAPTER_SCALE * fdot(left_of(left_ref, 0, owners), jnp.concatenate(right, axis=0), NN)
    out_ref[...] = out.reshape(out_ref.shape)


def down_outer(meta, grads, left):
    n_dp, chunks = len(grads[0]), len(grads)
    pieces = [piece for pieces in grads for piece in pieces]
    g, _, width = pieces[0].shape
    tile = tile_of(width, 512)
    return pl.pallas_call(
        functools.partial(down_outer_kernel, n_dp, g, chunks),
        out_shape=jax.ShapeDtypeStruct((TENANTS, R, width), jnp.float32),
        grid_spec=pltpu.PrefetchScalarGridSpec(
            num_scalar_prefetch=1,
            grid=(width // tile,),
            in_specs=[
                pl.BlockSpec(piece.shape[:2] + (tile,), lambda f, *_: (0, 0, f)) for piece in pieces
            ]
            + [whole(left.shape)],
            out_specs=pl.BlockSpec((TENANTS, R, tile), lambda f, *_: (0, 0, f)),
        ),
        compiler_params=pltpu.CompilerParams(vmem_limit_bytes=VMEM_LIMIT),
        cost_estimate=NO_COST,
        name="down_outer",
    )(meta, *pieces, left)


def gate_up_outer_kernel(n_t, meta, *refs):
    ny = n_t // 2
    factors, refs = [refs[2 * p : 2 * p + 2] for p in range(n_t)], refs[2 * n_t :]
    sums, (left_ref, so_far, out_ref) = refs[:2], refs[2:]
    y, c = meta[1] // 2, meta[1] % 2
    owners = [owner_of(p, y, c, ny) for p in range(n_t)]
    grads = [grads_of(sums[p % 2][(ny - p // 2) % ny], factors[p]) for p in range(n_t)]
    for layer in range(2):
        right = jnp.concatenate([grad[layer] for grad in grads], axis=0)
        out = ADAPTER_SCALE * fdot(left_of(left_ref, layer, owners), right, NN)
        at = slice(layer * R, (layer + 1) * R)
        out_ref[:, at, :] = so_far[:, at, :] + out.reshape(TENANTS, R, out.shape[1])


def gate_up_outer(meta, factors, q, sums, left, so_far):
    n_t = len(factors)
    rc, width = sums[0].shape[1], factors[0][0].shape[1]
    tile = tile_of(width, 896)
    block = pl.BlockSpec((TENANTS, 2 * R, tile), lambda f, *_: (0, 0, f))
    return pl.pallas_call(
        functools.partial(gate_up_outer_kernel, n_t),
        out_shape=jax.ShapeDtypeStruct((TENANTS, 2 * R, width), jnp.float32),
        grid_spec=pltpu.PrefetchScalarGridSpec(
            num_scalar_prefetch=1,
            grid=(width // tile,),
            in_specs=[pl.BlockSpec((rc, tile), lambda f, *_: (q, f))] * (2 * n_t)
            + [pl.BlockSpec((n_t // 2, rc, tile), lambda f, *_: (0, 0, f))] * 2
            + [whole(left.shape), block],
            out_specs=block,
        ),
        compiler_params=pltpu.CompilerParams(vmem_limit_bytes=VMEM_LIMIT),
        cost_estimate=NO_COST,
        name="gate_up_outer",
    )(meta, *[x for pair in factors for x in pair], *sums, left, so_far)


def spread_kernel(tenant_at, rows, meta, *refs):
    parts, out_ref = refs[:-1], refs[-1]
    out_ref[...] = jnp.zeros_like(out_ref)
    at = 0
    for part in parts:
        for k in range(part.shape[0] // rows):
            tenant = tenant_at(at, meta)
            term = part[k * rows : (k + 1) * rows].astype(jnp.float32)
            out_ref[tenant] = out_ref[tenant] + ADAPTER_SCALE * term
            at += 1


def spread(meta, parts, tenant_at, rows, name):
    width = parts[0].shape[1]
    out = jax.ShapeDtypeStruct((TENANTS, rows, width), jnp.float32)
    tile = tile_of(width, 1024)
    return pl.pallas_call(
        functools.partial(spread_kernel, tenant_at, rows),
        out_shape=out,
        grid_spec=pltpu.PrefetchScalarGridSpec(
            num_scalar_prefetch=1,
            grid=(width // tile,),
            in_specs=[pl.BlockSpec((part.shape[0], tile), lambda f, *_: (0, f)) for part in parts],
            out_specs=pl.BlockSpec((TENANTS, rows, tile), lambda f, *_: (0, 0, f)),
        ),
        compiler_params=pltpu.CompilerParams(vmem_limit_bytes=VMEM_LIMIT),
        cost_estimate=NO_COST,
        name=name,
    )(meta, *parts)


def in_outer_kernel(n_dp, chunks, g, meta, *refs):
    shares, inputs, out_ref = refs[: n_dp * chunks], refs[n_dp * chunks : -1], refs[-1]
    out_ref[...] = jnp.zeros_like(out_ref)
    own_t = inputs[0].shape[0] // g
    rc = own_t // chunks
    for k in range(n_dp):
        tenant = meta[2 + lax.rem(meta[0] + n_dp - k, n_dp)]
        total = 0.0
        for q in range(chunks):
            query = 0.0
            for s in range(n_dp):
                at = (s + n_dp - k) % n_dp * 2 * R
                query = query + shares[q * n_dp + s][:, at : at + 2 * R].astype(jnp.float32)
            query = query.astype(jnp.bfloat16)
            for j in range(g):
                rows = inputs[k][j * own_t + q * rc : j * own_t + (q + 1) * rc, :]
                total = total + fdot(query[j * rc : (j + 1) * rc], rows, TN)
        out_ref[tenant] = out_ref[tenant] + ADAPTER_SCALE * total


def in_outer(meta, shares, inputs, g):
    n_dp, chunks = len(inputs), len(shares)
    shares = [share for there in shares for share in there]
    rows, width = inputs[0].shape
    rc = shares[0].shape[0]
    low = n_dp * 2 * R
    tile = tile_of(width, 1024)
    return pl.pallas_call(
        functools.partial(in_outer_kernel, n_dp, chunks, g),
        out_shape=jax.ShapeDtypeStruct((TENANTS, 2 * R, width), jnp.float32),
        grid_spec=pltpu.PrefetchScalarGridSpec(
            num_scalar_prefetch=1,
            grid=(width // tile,),
            in_specs=[pl.BlockSpec((rc, low), lambda f, *_: (0, width // low))] * len(shares)
            + [pl.BlockSpec((rows, tile), lambda f, *_: (0, f))] * n_dp,
            out_specs=pl.BlockSpec((TENANTS, 2 * R, tile), lambda f, *_: (0, 0, f)),
        ),
        compiler_params=pltpu.CompilerParams(vmem_limit_bytes=VMEM_LIMIT),
        cost_estimate=NO_COST,
        name="in_outer",
    )(meta, *shares, *inputs)


def ring(n, by):
    return [(k, (k + by) % n) for k in range(n)]


def add32(*terms):
    return sum(term.astype(jnp.float32) for term in terms)


def after(value, *done):
    return lax.optimization_barrier((value,) + done)[0]


def per_device(
    layer_input,
    out_grad,
    gate_pre,
    up_pre,
    adapter_acts,
    gate_weight,
    up_weight,
    down_weight,
    adapter_a_gu,
    adapter_b_gu,
    adapter_a_down,
    adapter_b_down,
    block_tenant,
):
    n_dp, n_t = lax.axis_size("dp"), lax.axis_size("tensor")
    ny = n_t // 2
    z, t = lax.axis_index("dp"), lax.axis_index("tensor")
    own_rows, width = out_grad.shape
    own_t, hidden_width = gate_pre.shape
    tokens = adapter_acts.shape[0]
    g = own_rows // own_t
    assert own_rows == BLOCK and g * own_t == own_rows and n_t == 2 * ny and n_t == g * n_dp
    chunks, at = [], 0
    for share in SHARES:
        chunks.append((at, own_t * share // sum(SHARES)))
        at += chunks[-1][1]

    meta = jnp.concatenate([jnp.stack([z, t]).astype(jnp.int32), block_tenant])
    b_down = adapter_b_down.reshape(TENANTS * R, width)
    a_down = jnp.transpose(adapter_a_down, (0, 2, 1)).reshape(TENANTS * R, hidden_width)
    b_gu = adapter_b_gu.reshape(TENANTS * 2 * R, hidden_width)
    a_gu = jnp.transpose(adapter_a_gu, (0, 2, 1)).reshape(TENANTS * 2 * R, width)

    pair = [(k, k ^ 1) for k in range(n_t)]
    z_next = ring(n_dp, 1)

    grads = [[out_grad.reshape(g, own_t, width)[:, at : at + rc]] for at, rc in chunks]
    for _ in range(n_dp - 1):
        for pieces in grads:
            pieces.append(lax.ppermute(pieces[-1], "dp", z_next))
    stored = (gate_pre, up_pre)
    far_stored = [[lax.ppermute(x, "tensor", ring(n_t, 2 * s)) for x in stored] for s in range(1, ny)]
    pair_stored = [lax.ppermute(x, "tensor", pair) for x in stored]

    onehot = (
        jnp.arange(TENANTS, dtype=jnp.int32)[:, None] == jnp.repeat(block_tenant, BLOCK)[None, :]
    ).astype(jnp.bfloat16)
    acts = adapter_acts.T.reshape(3, 1, R, tokens) * onehot[None, :, None, :]
    acts = acts.reshape(3, TENANTS * R, n_t, own_t).transpose(0, 2, 1, 3)

    def factors_of(gate_pre, up_pre):
        gate_value = gate_pre.astype(jnp.float32)
        up_value = up_pre.astype(jnp.float32)
        sigmoid_value = jax.nn.sigmoid(gate_value)
        dgate = up_value * sigmoid_value * (1.0 + gate_value * (1.0 - sigmoid_value))
        dup = gate_value * sigmoid_value
        return [x.astype(jnp.bfloat16) for x in (dgate, dup, dup * up_value)]

    def first(q, done):
        pieces = [after(grads[q][0], *done)] + grads[q][1:]
        keep, send = hidden_partial(meta, pieces, down_weight, b_down, a_down, n_t, own_t)
        return keep, lax.ppermute(send, "tensor", pair)

    def exchange(keep, other):
        mine = add32(keep, other).astype(jnp.bfloat16)
        return mine, [lax.ppermute(mine, "tensor", ring(n_t, 2 * s)) for s in range(1, ny)]

    def total(mine, far):
        turned = [jnp.roll(there, -(s + 1), axis=0) for s, there in enumerate(far)]
        both = add32(mine, *turned).astype(jnp.bfloat16)
        return [both, lax.ppermute(both, "tensor", pair)]

    def second(q, sums, done):
        sums = [after(sums[0], *done), sums[1]]
        outs = input_partial(meta, factors, q, sums, gate_weight, up_weight, b_gu, a_gu, n_dp, own_t)
        return [outs[0]] + [lax.ppermute(outs[r], "dp", ring(n_dp, r)) for r in range(1, n_dp)]

    def finish(there, rc):
        return add32(*[x[:, :width] for x in there]).astype(jnp.bfloat16).reshape(g, rc, width)

    keep_a, other_a = first(0, (grads[1][n_dp - 2],))
    mine_a, far_a = exchange(keep_a, other_a)
    inputs = [after(layer_input, grads[-1][-1])]
    for _ in range(n_dp - 1):
        inputs.append(lax.ppermute(inputs[-1], "dp", z_next))
    *near, hidden = factors_of(*stored)
    factors = [near, factors_of(*pair_stored)[:2]]
    keep_b, other_b = first(1, (mine_a, near[0], factors[1][0]))
    mine_b, far_b = exchange(keep_b, other_b)
    for there in far_stored:
        there = [after(x, keep_a) for x in there]
        beside = [lax.ppermute(x, "tensor", pair) for x in there]
        there[0] = after(there[0], mine_b)
        factors += [factors_of(*there)[:2], factors_of(*beside)[:2]]
    grad_b_down = down_outer(meta, grads, after(acts[2:], *[pair[0] for pair in factors]))
    sums_a = total(after(mine_a, grad_b_down), far_a)
    there_a = second(0, sums_a, ())
    left = [acts[:2, :, :, at : at + rc] for at, rc in chunks]
    zeros = jnp.zeros((TENANTS, 2 * R, hidden_width), jnp.float32)
    grad_b_gu = gate_up_outer(meta, factors, 0, sums_a, after(left[0], there_a[0]), zeros)
    sums_b = total(after(mine_b, grad_b_gu, inputs[-1], there_a[1]), far_b)

    low = jnp.concatenate([sums_a[0][0], sums_b[0][0]], axis=0)
    low = low[:, hidden_width : hidden_width + TENANTS * R]
    a_part = fdot(low, hidden, TN).reshape(TENANTS, R, hidden_width).sum(0).astype(jnp.bfloat16)
    a_column = [a_part] + [lax.ppermute(a_part, "tensor", ring(n_t, 2 * s)) for s in range(1, ny)]
    there_b = second(1, sums_b, (a_part,))

    a_column = [after(a_column[0], there_b[0])] + a_column[1:]
    a_beside = lax.ppermute(jnp.concatenate(a_column, axis=0), "tensor", pair)
    half_a = finish([after(there_a[0], there_b[0])] + there_a[1:], chunks[0][1])
    grad_b_gu = gate_up_outer(meta, factors, 1, sums_b, after(left[1], half_a), grad_b_gu)

    def column_tenant(p, m):
        owner = lax.rem(m[1] // 2 + ny - p % ny, ny) * 2
        return tenant_of(m, owner + (m[1] % 2 if p < ny else 1 - m[1] % 2), own_t)

    a_column[0] = after(a_column[0], grad_b_gu)
    grad_a_down = spread(meta, a_column + [a_beside], column_tenant, R, "spread_a_down")
    there_b[0] = after(there_b[0], grad_a_down)
    grad_a_gu = in_outer(meta, [there_a, there_b], inputs, g)
    half_b = finish(there_b, chunks[1][1])
    block_input_grad = jnp.concatenate([half_a, half_b], axis=1).reshape(own_rows, width)
    return (
        block_input_grad,
        grad_a_gu.transpose(0, 2, 1),
        grad_b_gu,
        grad_a_down.transpose(0, 2, 1),
        grad_b_down,
    )


def solution(mesh):
    placed = (
        P(("groups", "dp"), "tensor"),
        P(("groups", "dp"), "tensor"),
        P(("groups", "tensor"), "dp"),
        P(("groups", "tensor"), "dp"),
        P("groups", None),
        P("tensor", "dp"),
        P("tensor", "dp"),
        P("dp", "tensor"),
        P(None, "tensor", None),
        P(None, None, "dp"),
        P(None, "dp", None),
        P(None, None, "tensor"),
        P("groups"),
    )
    return jax.shard_map(
        per_device,
        mesh=mesh,
        in_specs=placed,
        out_specs=(
            P(("groups", "dp"), "tensor"),
            P("groups", "tensor", None),
            P("groups", None, "dp"),
            P("groups", "dp", None),
            P("groups", None, "tensor"),
        ),
        check_vma=False,
    )
```

```python
import functools

import jax
import jax.numpy as jnp
from jax import lax
from jax.experimental import pallas as pl
from jax.experimental.pallas import tpu as pltpu
from jax.sharding import PartitionSpec as P

R = 16
TENANTS = 4
BLOCK = 128
SHARES = (1, 1)
LANES = 128
VMEM_LIMIT = 12 * 1024 * 1024
STREAM_LIMIT = 50 * 1024 * 1024

ADAPTER_SCALE = 2.0

NT = (((1,), (1,)), ((), ()))
NN = (((1,), (0,)), ((), ()))
TN = (((0,), (0,)), ((), ()))
ANY = pl.BlockSpec(memory_space=pl.ANY)
SMEM = pl.BlockSpec(memory_space=pltpu.SMEM)
VMEM = pl.BlockSpec(memory_space=pltpu.VMEM)
NO_COST = pl.CostEstimate(flops=1, bytes_accessed=1, transcendentals=0)


def fdot(lhs, rhs, dims):
    return lax.dot_general(lhs, rhs, dims, preferred_element_type=jnp.float32)


def tile_of(width, most):
    tile = most
    while width % tile:
        tile -= LANES
    return tile


def whole(shape):
    return pl.BlockSpec(shape, lambda *_: (0,) * len(shape))


def tenant_of(meta, owner, own_t):
    return meta[2 + (owner * own_t) // BLOCK]


def owner_of(p, y, c, ny):
    return lax.rem(y + ny - p // 2, ny) * 2 + (c if p % 2 == 0 else 1 - c)


def hidden_kernel(sizes, meta, *refs):
    n_dp, n_t, g, own_t, rc, tile = sizes
    ny = n_t // 2
    pieces, (w_ref, bd_ref, ad_ref, keep_ref, send_ref), refs = refs[:n_dp], refs[n_dp : n_dp + 5], refs[n_dp + 5 :]
    x_scr, p_scr, w_scr, w_sem = refs
    z, t = meta[0], meta[1]
    y, c = t // 2, t % 2
    hidden_width, width = w_ref.shape
    steps = hidden_width // tile

    def fetch(f):
        rows = pl.ds(pl.multiple_of(f * tile, LANES), tile)
        return pltpu.make_async_copy(w_ref.at[rows], w_scr.at[f], w_sem.at[f])

    for f in range(steps):
        fetch(f).start()

    for k in range(n_dp):
        for j in range(g):
            owner = lax.rem(z + (n_dp - k), n_dp) * g + j
            away = jnp.where(owner % 2 == c, 0, ny)
            x_scr[away + lax.rem(owner // 2 + ny - y, ny)] = pieces[k][j]
    proj = fdot(x_scr[...].reshape(n_t * rc, width), bd_ref[...], NT)
    lane = lax.broadcasted_iota(jnp.int32, (rc, TENANTS * R), 1) // R
    zeros = jnp.zeros((rc, LANES - TENANTS * R), jnp.bfloat16)
    for s in range(n_t):
        owner = lax.rem(y + s % ny, ny) * 2 + (c if s < ny else 1 - c)
        own = jnp.where(lane == tenant_of(meta, owner, own_t), proj[s * rc : (s + 1) * rc], 0.0)
        p_scr[s * rc : (s + 1) * rc, :] = (ADAPTER_SCALE * own).astype(jnp.bfloat16)
        out = keep_ref if s < ny else send_ref
        out[s % ny, :, hidden_width:] = jnp.concatenate([own.astype(jnp.bfloat16), zeros], axis=1)

    def body(step, carry):
        at = pl.ds(pl.multiple_of(step * tile, LANES), tile)
        fetch(step).wait()
        acc = fdot(x_scr[...].reshape(n_t * rc, width), w_scr[step], NT)
        acc = (acc + fdot(p_scr[...], ad_ref[:, at], NN)).astype(jnp.bfloat16).reshape(n_t, rc, tile)
        keep_ref[:, :, at] = acc[:ny]
        send_ref[:, :, at] = acc[ny:]
        return carry

    lax.fori_loop(0, steps, body, 0)


def hidden_partial(meta, pieces, down_weight, b_down, a_down, n_t, own_t):
    n_dp = len(pieces)
    g, rc, width = pieces[0].shape
    ny = n_t // 2
    hidden_width = down_weight.shape[0]
    tile = tile_of(hidden_width, 512)
    low = TENANTS * R
    out = jax.ShapeDtypeStruct((ny, rc, hidden_width + LANES), jnp.bfloat16)
    return pl.pallas_call(
        functools.partial(hidden_kernel, (n_dp, n_t, g, own_t, rc, tile)),
        out_shape=(out, out),
        in_specs=[SMEM] + [VMEM] * n_dp + [ANY] + [VMEM] * 2,
        out_specs=[VMEM] * 2,
        scratch_shapes=[
            pltpu.VMEM((n_t, rc, width), jnp.bfloat16),
            pltpu.VMEM((n_t * rc, low), jnp.bfloat16),
            pltpu.VMEM((hidden_width // tile, tile, width), jnp.bfloat16),
            pltpu.SemaphoreType.DMA((hidden_width // tile,)),
        ],
        compiler_params=pltpu.CompilerParams(vmem_limit_bytes=STREAM_LIMIT),
        cost_estimate=NO_COST,
        name="hidden_partial",
    )(meta, *pieces, down_weight, b_down, a_down)


def grads_of(total, factors):
    total = total.astype(jnp.float32)
    return [(total * factor[...].astype(jnp.float32)).astype(jnp.bfloat16) for factor in factors]


def input_kernel(sizes, meta, *refs):
    n_dp, n_t, g, own_t, rc, q, tile = sizes
    ny = n_t // 2
    factors, refs = [refs[2 * p : 2 * p + 2] for p in range(n_t)], refs[2 * n_t :]
    sums, (gw_ref, uw_ref, b_ref, a_ref) = refs[:2], refs[2:6]
    outs, (g_scr, u_scr, q_scr, w_scr, w_sem) = refs[6 : 6 + n_dp], refs[6 + n_dp :]
    z, t = meta[0], meta[1]
    y, c = t // 2, t % 2
    rows = n_t * rc
    width, hidden_width = gw_ref.shape
    steps = width // tile

    def fetch(f):
        at = pl.ds(pl.multiple_of(f * tile, LANES), tile)
        return [
            pltpu.make_async_copy(w.at[at], w_scr.at[f, k], w_sem.at[f, k]) for k, w in enumerate((gw_ref, uw_ref))
        ]

    for f in range(steps):
        for copy in fetch(f):
            copy.start()

    for p in range(n_t):
        owner = owner_of(p, y, c, ny)
        slot = lax.rem(owner // g + n_dp - z, n_dp) * g + owner % g
        mine = [factor[q * rc : (q + 1) * rc, :] for factor in factors[p]]
        g_scr[slot], u_scr[slot] = grads_of(sums[p % 2][(ny - p // 2) % ny, :, :hidden_width], mine)
    q_gate = fdot(g_scr[...].reshape(rows, hidden_width), b_ref[...], NT)
    q_up = fdot(u_scr[...].reshape(rows, hidden_width), b_ref[...], NT)
    lane = lax.broadcasted_iota(jnp.int32, (rc, 2 * R * TENANTS), 1)
    shares = []
    for r in range(n_dp):
        share = []
        for j in range(g):
            at = slice((r * g + j) * rc, (r * g + j + 1) * rc)
            tenant = tenant_of(meta, lax.rem(z + r, n_dp) * g + j, own_t)
            mine = jnp.where(lane % (2 * R) < R, q_gate[at], q_up[at])
            mine = jnp.where(lane // (2 * R) == tenant, mine, 0.0)
            q_scr[at, :] = (ADAPTER_SCALE * mine).astype(jnp.bfloat16)
            share.append(sum(mine[:, e * 2 * R : (e + 1) * 2 * R] for e in range(TENANTS)))
        shares.append(jnp.concatenate(share, axis=0))
    share = jnp.concatenate(shares, axis=1).astype(jnp.bfloat16)
    for r in range(n_dp):
        outs[r][:, width:] = share

    def body(step, carry):
        at = pl.ds(pl.multiple_of(step * tile, LANES), tile)
        for copy in fetch(step):
            copy.wait()
        acc = fdot(g_scr[...].reshape(rows, hidden_width), w_scr[step, 0], NT)
        acc = acc + fdot(u_scr[...].reshape(rows, hidden_width), w_scr[step, 1], NT)
        acc = (acc + fdot(q_scr[...], a_ref[:, at], NN)).astype(jnp.bfloat16)
        for r in range(n_dp):
            outs[r][:, at] = acc[r * g * rc : (r + 1) * g * rc]
        return carry

    lax.fori_loop(0, steps, body, 0)


def input_partial(meta, factors, q, sums, gate_weight, up_weight, b_gu, a_gu, n_dp, own_t):
    n_t = len(factors)
    ny, rc, _ = sums[0].shape
    g = n_t // n_dp
    width, hidden_width = gate_weight.shape
    tile = tile_of(width, 256)
    low = 2 * R * TENANTS
    rows = n_t * rc
    outs = [jax.ShapeDtypeStruct((g * rc, width + n_dp * 2 * R), jnp.bfloat16)] * n_dp
    return pl.pallas_call(
        functools.partial(input_kernel, (n_dp, n_t, g, own_t, rc, q, tile)),
        out_shape=outs,
        in_specs=[SMEM] + [VMEM] * (2 * n_t + 2) + [ANY] * 2 + [VMEM] * 2,
        out_specs=[VMEM] * n_dp,
        scratch_shapes=[
            pltpu.VMEM((n_t, rc, hidden_width), jnp.bfloat16),
            pltpu.VMEM((n_t, rc, hidden_width), jnp.bfloat16),
            pltpu.VMEM((rows, low), jnp.bfloat16),
            pltpu.VMEM((width // tile, 2, tile, hidden_width), jnp.bfloat16),
            pltpu.SemaphoreType.DMA((width // tile, 2)),
        ],
        compiler_params=pltpu.CompilerParams(vmem_limit_bytes=STREAM_LIMIT),
        cost_estimate=NO_COST,
        name="input_partial",
    )(meta, *[x for pair in factors for x in pair], *sums, gate_weight, up_weight, b_gu, a_gu)


def left_of(left_ref, layer, owners):
    return jnp.concatenate([left_ref[layer, owner] for owner in owners], axis=1)


def down_outer_kernel(n_dp, g, chunks, meta, *refs):
    pieces, (left_ref, out_ref) = refs[: n_dp * chunks], refs[n_dp * chunks :]
    owners = [lax.rem(meta[0] + (n_dp - k), n_dp) * g + j for k in range(n_dp) for j in range(g)]
    right = [pieces[q * n_dp + k][j] for k in range(n_dp) for j in range(g) for q in range(chunks)]
    out = ADAPTER_SCALE * fdot(left_of(left_ref, 0, owners), jnp.concatenate(right, axis=0), NN)
    out_ref[...] = out.reshape(out_ref.shape)


def down_outer(meta, grads, left):
    n_dp, chunks = len(grads[0]), len(grads)
    pieces = [piece for pieces in grads for piece in pieces]
    g, _, width = pieces[0].shape
    tile = tile_of(width, 512)
    return pl.pallas_call(
        functools.partial(down_outer_kernel, n_dp, g, chunks),
        out_shape=jax.ShapeDtypeStruct((TENANTS, R, width), jnp.float32),
        grid_spec=pltpu.PrefetchScalarGridSpec(
            num_scalar_prefetch=1,
            grid=(width // tile,),
            in_specs=[
                pl.BlockSpec(piece.shape[:2] + (tile,), lambda f, *_: (0, 0, f)) for piece in pieces
            ]
            + [whole(left.shape)],
            out_specs=pl.BlockSpec((TENANTS, R, tile), lambda f, *_: (0, 0, f)),
        ),
        compiler_params=pltpu.CompilerParams(vmem_limit_bytes=VMEM_LIMIT),
        cost_estimate=NO_COST,
        name="down_outer",
    )(meta, *pieces, left)


def gate_up_outer_kernel(n_t, meta, *refs):
    ny = n_t // 2
    factors, refs = [refs[2 * p : 2 * p + 2] for p in range(n_t)], refs[2 * n_t :]
    sums, (left_ref, so_far, out_ref) = refs[:2], refs[2:]
    y, c = meta[1] // 2, meta[1] % 2
    owners = [owner_of(p, y, c, ny) for p in range(n_t)]
    grads = [grads_of(sums[p % 2][(ny - p // 2) % ny], factors[p]) for p in range(n_t)]
    for layer in range(2):
        right = jnp.concatenate([grad[layer] for grad in grads], axis=0)
        out = ADAPTER_SCALE * fdot(left_of(left_ref, layer, owners), right, NN)
        at = slice(layer * R, (layer + 1) * R)
        out_ref[:, at, :] = so_far[:, at, :] + out.reshape(TENANTS, R, out.shape[1])


def gate_up_outer(meta, factors, q, sums, left, so_far):
    n_t = len(factors)
    rc, width = sums[0].shape[1], factors[0][0].shape[1]
    tile = tile_of(width, 896)
    block = pl.BlockSpec((TENANTS, 2 * R, tile), lambda f, *_: (0, 0, f))
    return pl.pallas_call(
        functools.partial(gate_up_outer_kernel, n_t),
        out_shape=jax.ShapeDtypeStruct((TENANTS, 2 * R, width), jnp.float32),
        grid_spec=pltpu.PrefetchScalarGridSpec(
            num_scalar_prefetch=1,
            grid=(width // tile,),
            in_specs=[pl.BlockSpec((rc, tile), lambda f, *_: (q, f))] * (2 * n_t)
            + [pl.BlockSpec((n_t // 2, rc, tile), lambda f, *_: (0, 0, f))] * 2
            + [whole(left.shape), block],
            out_specs=block,
        ),
        compiler_params=pltpu.CompilerParams(vmem_limit_bytes=VMEM_LIMIT),
        cost_estimate=NO_COST,
        name="gate_up_outer",
    )(meta, *[x for pair in factors for x in pair], *sums, left, so_far)


def spread_kernel(tenant_at, rows, meta, *refs):
    parts, out_ref = refs[:-1], refs[-1]
    out_ref[...] = jnp.zeros_like(out_ref)
    at = 0
    for part in parts:
        for k in range(part.shape[0] // rows):
            tenant = tenant_at(at, meta)
            term = part[k * rows : (k + 1) * rows].astype(jnp.float32)
            out_ref[tenant] = out_ref[tenant] + ADAPTER_SCALE * term
            at += 1


def spread(meta, parts, tenant_at, rows, name):
    width = parts[0].shape[1]
    out = jax.ShapeDtypeStruct((TENANTS, rows, width), jnp.float32)
    tile = tile_of(width, 1024)
    return pl.pallas_call(
        functools.partial(spread_kernel, tenant_at, rows),
        out_shape=out,
        grid_spec=pltpu.PrefetchScalarGridSpec(
            num_scalar_prefetch=1,
            grid=(width // tile,),
            in_specs=[pl.BlockSpec((part.shape[0], tile), lambda f, *_: (0, f)) for part in parts],
            out_specs=pl.BlockSpec((TENANTS, rows, tile), lambda f, *_: (0, 0, f)),
        ),
        compiler_params=pltpu.CompilerParams(vmem_limit_bytes=VMEM_LIMIT),
        cost_estimate=NO_COST,
        name=name,
    )(meta, *parts)


def in_outer_kernel(n_dp, chunks, g, meta, *refs):
    shares, inputs, out_ref = refs[: n_dp * chunks], refs[n_dp * chunks : -1], refs[-1]
    out_ref[...] = jnp.zeros_like(out_ref)
    own_t = inputs[0].shape[0] // g
    rc = own_t // chunks
    for k in range(n_dp):
        tenant = meta[2 + lax.rem(meta[0] + n_dp - k, n_dp)]
        total = 0.0
        for q in range(chunks):
            query = 0.0
            for s in range(n_dp):
                at = (s + n_dp - k) % n_dp * 2 * R
                query = query + shares[q * n_dp + s][:, at : at + 2 * R].astype(jnp.float32)
            query = query.astype(jnp.bfloat16)
            for j in range(g):
                rows = inputs[k][j * own_t + q * rc : j * own_t + (q + 1) * rc, :]
                total = total + fdot(query[j * rc : (j + 1) * rc], rows, TN)
        out_ref[tenant] = out_ref[tenant] + ADAPTER_SCALE * total


def in_outer(meta, shares, inputs, g):
    n_dp, chunks = len(inputs), len(shares)
    shares = [share for there in shares for share in there]
    rows, width = inputs[0].shape
    rc = shares[0].shape[0]
    low = n_dp * 2 * R
    tile = tile_of(width, 1024)
    return pl.pallas_call(
        functools.partial(in_outer_kernel, n_dp, chunks, g),
        out_shape=jax.ShapeDtypeStruct((TENANTS, 2 * R, width), jnp.float32),
        grid_spec=pltpu.PrefetchScalarGridSpec(
            num_scalar_prefetch=1,
            grid=(width // tile,),
            in_specs=[pl.BlockSpec((rc, low), lambda f, *_: (0, width // low))] * len(shares)
            + [pl.BlockSpec((rows, tile), lambda f, *_: (0, f))] * n_dp,
            out_specs=pl.BlockSpec((TENANTS, 2 * R, tile), lambda f, *_: (0, 0, f)),
        ),
        compiler_params=pltpu.CompilerParams(vmem_limit_bytes=VMEM_LIMIT),
        cost_estimate=NO_COST,
        name="in_outer",
    )(meta, *shares, *inputs)


def ring(n, by):
    return [(k, (k + by) % n) for k in range(n)]


def add32(*terms):
    return sum(term.astype(jnp.float32) for term in terms)


def after(value, *done):
    return lax.optimization_barrier((value,) + done)[0]


def per_device(
    layer_input,
    out_grad,
    gate_pre,
    up_pre,
    adapter_acts,
    gate_weight,
    up_weight,
    down_weight,
    adapter_a_gu,
    adapter_b_gu,
    adapter_a_down,
    adapter_b_down,
    block_tenant,
):
    n_dp, n_t = lax.axis_size("dp"), lax.axis_size("tensor")
    ny = n_t // 2
    z, t = lax.axis_index("dp"), lax.axis_index("tensor")
    own_rows, width = out_grad.shape
    own_t, hidden_width = gate_pre.shape
    tokens = adapter_acts.shape[0]
    g = own_rows // own_t
    assert own_rows == BLOCK and g * own_t == own_rows and n_t == 2 * ny and n_t == g * n_dp
    chunks, at = [], 0
    for share in SHARES:
        chunks.append((at, own_t * share // sum(SHARES)))
        at += chunks[-1][1]

    meta = jnp.concatenate([jnp.stack([z, t]).astype(jnp.int32), block_tenant])
    b_down = adapter_b_down.reshape(TENANTS * R, width)
    a_down = jnp.transpose(adapter_a_down, (0, 2, 1)).reshape(TENANTS * R, hidden_width)
    b_gu = adapter_b_gu.reshape(TENANTS * 2 * R, hidden_width)
    a_gu = jnp.transpose(adapter_a_gu, (0, 2, 1)).reshape(TENANTS * 2 * R, width)

    pair = [(k, k ^ 1) for k in range(n_t)]
    z_next = ring(n_dp, 1)

    grads = [[out_grad.reshape(g, own_t, width)[:, at : at + rc]] for at, rc in chunks]
    for _ in range(n_dp - 1):
        for pieces in grads:
            pieces.append(lax.ppermute(pieces[-1], "dp", z_next))
    stored = (gate_pre, up_pre)
    far_stored = [[lax.ppermute(x, "tensor", ring(n_t, 2 * s)) for x in stored] for s in range(1, ny)]
    pair_stored = [lax.ppermute(after(x, grads[0][2]), "tensor", pair) for x in stored]

    onehot = (
        jnp.arange(TENANTS, dtype=jnp.int32)[:, None] == jnp.repeat(block_tenant, BLOCK)[None, :]
    ).astype(jnp.bfloat16)
    acts = adapter_acts.T.reshape(3, 1, R, tokens) * onehot[None, :, None, :]
    acts = acts.reshape(3, TENANTS * R, n_t, own_t).transpose(0, 2, 1, 3)

    def factors_of(gate_pre, up_pre):
        gate_value = gate_pre.astype(jnp.float32)
        up_value = up_pre.astype(jnp.float32)
        sigmoid_value = jax.nn.sigmoid(gate_value)
        dgate = up_value * sigmoid_value * (1.0 + gate_value * (1.0 - sigmoid_value))
        dup = gate_value * sigmoid_value
        return [x.astype(jnp.bfloat16) for x in (dgate, dup, dup * up_value)]

    def first(q, done):
        pieces = [after(grads[q][0], *done)] + grads[q][1:]
        keep, send = hidden_partial(meta, pieces, down_weight, b_down, a_down, n_t, own_t)
        return keep, lax.ppermute(send, "tensor", pair)

    def exchange(keep, other):
        mine = add32(keep, other).astype(jnp.bfloat16)
        return mine, [lax.ppermute(mine, "tensor", ring(n_t, 2 * s)) for s in range(1, ny)]

    def total(mine, far):
        turned = [jnp.roll(there, -(s + 1), axis=0) for s, there in enumerate(far)]
        both = add32(mine, *turned).astype(jnp.bfloat16)
        return [both, lax.ppermute(both, "tensor", pair)]

    def second(q, sums, done):
        sums = [after(sums[0], *done), sums[1]]
        outs = input_partial(meta, factors, q, sums, gate_weight, up_weight, b_gu, a_gu, n_dp, own_t)
        return [outs[0]] + [lax.ppermute(outs[r], "dp", ring(n_dp, r)) for r in range(1, n_dp)]

    def finish(there, rc):
        return add32(*[x[:, :width] for x in there]).astype(jnp.bfloat16).reshape(g, rc, width)

    keep_a, other_a = first(0, (grads[1][n_dp - 2],))
    mine_a, far_a = exchange(keep_a, other_a)
    inputs = [after(layer_input, grads[-1][-1])]
    for _ in range(n_dp - 1):
        inputs.append(lax.ppermute(inputs[-1], "dp", z_next))
    *near, hidden = factors_of(*stored)
    factors = [near, factors_of(*pair_stored)[:2]]
    keep_b, other_b = first(1, (mine_a, near[0], factors[1][0]))
    mine_b, far_b = exchange(keep_b, other_b)
    for there in far_stored:
        there = [after(x, keep_a) for x in there]
        beside = [lax.ppermute(x, "tensor", pair) for x in there]
        there[0] = after(there[0], mine_b)
        factors += [factors_of(*there)[:2], factors_of(*beside)[:2]]
    grad_b_down = down_outer(meta, grads, after(acts[2:], *[pair[0] for pair in factors]))
    sums_a = total(after(mine_a, grad_b_down), far_a)
    there_a = second(0, sums_a, ())
    left = [acts[:2, :, :, at : at + rc] for at, rc in chunks]
    zeros = jnp.zeros((TENANTS, 2 * R, hidden_width), jnp.float32)
    grad_b_gu = gate_up_outer(meta, factors, 0, sums_a, after(left[0], there_a[0]), zeros)
    sums_b = total(after(mine_b, grad_b_gu, inputs[-1], there_a[1]), far_b)

    low = jnp.concatenate([sums_a[0][0], sums_b[0][0]], axis=0)
    low = low[:, hidden_width : hidden_width + TENANTS * R]
    a_part = fdot(low, hidden, TN).reshape(TENANTS, R, hidden_width).sum(0).astype(jnp.bfloat16)
    a_column = [a_part] + [lax.ppermute(a_part, "tensor", ring(n_t, 2 * s)) for s in range(1, ny)]
    there_b = second(1, sums_b, (a_part,))

    a_column = [after(a_column[0], there_b[0])] + a_column[1:]
    a_beside = lax.ppermute(jnp.concatenate(a_column, axis=0), "tensor", pair)
    half_a = finish([after(there_a[0], there_b[0])] + there_a[1:], chunks[0][1])
    grad_b_gu = gate_up_outer(meta, factors, 1, sums_b, after(left[1], half_a), grad_b_gu)

    def column_tenant(p, m):
        owner = lax.rem(m[1] // 2 + ny - p % ny, ny) * 2
        return tenant_of(m, owner + (m[1] % 2 if p < ny else 1 - m[1] % 2), own_t)

    a_column[0] = after(a_column[0], grad_b_gu)
    grad_a_down = spread(meta, a_column + [a_beside], column_tenant, R, "spread_a_down")
    there_b[0] = after(there_b[0], grad_a_down)
    grad_a_gu = in_outer(meta, [there_a, there_b], inputs, g)
    half_b = finish(there_b, chunks[1][1])
    block_input_grad = jnp.concatenate([half_a, half_b], axis=1).reshape(own_rows, width)
    return (
        block_input_grad,
        grad_a_gu.transpose(0, 2, 1),
        grad_b_gu,
        grad_a_down.transpose(0, 2, 1),
        grad_b_down,
    )


def solution(mesh):
    placed = (
        P(("groups", "dp"), "tensor"),
        P(("groups", "dp"), "tensor"),
        P(("groups", "tensor"), "dp"),
        P(("groups", "tensor"), "dp"),
        P("groups", None),
        P("tensor", "dp"),
        P("tensor", "dp"),
        P("dp", "tensor"),
        P(None, "tensor", None),
        P(None, None, "dp"),
        P(None, "dp", None),
        P(None, None, "tensor"),
        P("groups"),
    )
    return jax.shard_map(
        per_device,
        mesh=mesh,
        in_specs=placed,
        out_specs=(
            P(("groups", "dp"), "tensor"),
            P("groups", "tensor", None),
            P("groups", None, "dp"),
            P("groups", "dp", None),
            P("groups", None, "tensor"),
        ),
        check_vma=False,
    )
```

```python
import functools

import jax
import jax.numpy as jnp
from jax import lax
from jax.experimental import pallas as pl
from jax.experimental.pallas import tpu as pltpu
from jax.sharding import PartitionSpec as P

R = 16
TENANTS = 4
BLOCK = 128
SHARES = (1, 1)
LANES = 128
VMEM_LIMIT = 12 * 1024 * 1024
STREAM_LIMIT = 50 * 1024 * 1024

ADAPTER_SCALE = 2.0

NT = (((1,), (1,)), ((), ()))
NN = (((1,), (0,)), ((), ()))
TN = (((0,), (0,)), ((), ()))
ANY = pl.BlockSpec(memory_space=pl.ANY)
SMEM = pl.BlockSpec(memory_space=pltpu.SMEM)
VMEM = pl.BlockSpec(memory_space=pltpu.VMEM)
NO_COST = pl.CostEstimate(flops=1, bytes_accessed=1, transcendentals=0)


def fdot(lhs, rhs, dims):
    return lax.dot_general(lhs, rhs, dims, preferred_element_type=jnp.float32)


def tile_of(width, most):
    tile = most
    while width % tile:
        tile -= LANES
    return tile


def whole(shape):
    return pl.BlockSpec(shape, lambda *_: (0,) * len(shape))


def tenant_of(meta, owner, own_t):
    return meta[2 + (owner * own_t) // BLOCK]


def owner_of(p, y, c, ny):
    return lax.rem(y + ny - p // 2, ny) * 2 + (c if p % 2 == 0 else 1 - c)


def hidden_kernel(sizes, meta, *refs):
    n_dp, n_t, g, own_t, rc, tile = sizes
    ny = n_t // 2
    pieces, (w_ref, bd_ref, ad_ref, keep_ref, send_ref), refs = refs[:n_dp], refs[n_dp : n_dp + 5], refs[n_dp + 5 :]
    x_scr, p_scr, w_scr, w_sem = refs
    z, t = meta[0], meta[1]
    y, c = t // 2, t % 2
    hidden_width, width = w_ref.shape
    steps = hidden_width // tile

    def fetch(f):
        rows = pl.ds(pl.multiple_of(f * tile, LANES), tile)
        return pltpu.make_async_copy(w_ref.at[rows], w_scr.at[f], w_sem.at[f])

    for f in range(steps):
        fetch(f).start()

    for k in range(n_dp):
        for j in range(g):
            owner = lax.rem(z + (n_dp - k), n_dp) * g + j
            away = jnp.where(owner % 2 == c, 0, ny)
            x_scr[away + owner // 2] = pieces[k][j]
    proj = fdot(x_scr[...].reshape(n_t * rc, width), bd_ref[...], NT)
    lane = lax.broadcasted_iota(jnp.int32, (rc, TENANTS * R), 1) // R
    zeros = jnp.zeros((rc, LANES - TENANTS * R), jnp.bfloat16)
    for s in range(n_t):
        owner = (s % ny) * 2 + (c if s < ny else 1 - c)
        own = jnp.where(lane == tenant_of(meta, owner, own_t), proj[s * rc : (s + 1) * rc], 0.0)
        p_scr[s * rc : (s + 1) * rc, :] = (ADAPTER_SCALE * own).astype(jnp.bfloat16)
        out = keep_ref if s < ny else send_ref
        out[s % ny, :, hidden_width:] = jnp.concatenate([own.astype(jnp.bfloat16), zeros], axis=1)

    def body(step, carry):
        at = pl.ds(pl.multiple_of(step * tile, LANES), tile)
        fetch(step).wait()
        acc = fdot(x_scr[...].reshape(n_t * rc, width), w_scr[step], NT)
        acc = (acc + fdot(p_scr[...], ad_ref[:, at], NN)).astype(jnp.bfloat16).reshape(n_t, rc, tile)
        keep_ref[:, :, at] = acc[:ny]
        send_ref[:, :, at] = acc[ny:]
        return carry

    lax.fori_loop(0, steps, body, 0)


def hidden_partial(meta, pieces, down_weight, b_down, a_down, n_t, own_t):
    n_dp = len(pieces)
    g, rc, width = pieces[0].shape
    ny = n_t // 2
    hidden_width = down_weight.shape[0]
    tile = tile_of(hidden_width, 512)
    low = TENANTS * R
    out = jax.ShapeDtypeStruct((ny, rc, hidden_width + LANES), jnp.bfloat16)
    return pl.pallas_call(
        functools.partial(hidden_kernel, (n_dp, n_t, g, own_t, rc, tile)),
        out_shape=(out, out),
        in_specs=[SMEM] + [VMEM] * n_dp + [ANY] + [VMEM] * 2,
        out_specs=[VMEM] * 2,
        scratch_shapes=[
            pltpu.VMEM((n_t, rc, width), jnp.bfloat16),
            pltpu.VMEM((n_t * rc, low), jnp.bfloat16),
            pltpu.VMEM((hidden_width // tile, tile, width), jnp.bfloat16),
            pltpu.SemaphoreType.DMA((hidden_width // tile,)),
        ],
        compiler_params=pltpu.CompilerParams(vmem_limit_bytes=STREAM_LIMIT),
        cost_estimate=NO_COST,
        name="hidden_partial",
    )(meta, *pieces, down_weight, b_down, a_down)


def grads_of(total, factors):
    total = total.astype(jnp.float32)
    return [(total * factor[...].astype(jnp.float32)).astype(jnp.bfloat16) for factor in factors]


def input_kernel(sizes, meta, *refs):
    n_dp, n_t, g, own_t, rc, q, tile = sizes
    ny = n_t // 2
    factors, refs = [refs[2 * p : 2 * p + 2] for p in range(n_t)], refs[2 * n_t :]
    sums, (gw_ref, uw_ref, b_ref, a_ref) = refs[:2], refs[2:6]
    outs, (g_scr, u_scr, q_scr, w_scr, w_sem) = refs[6 : 6 + n_dp], refs[6 + n_dp :]
    z, t = meta[0], meta[1]
    y, c = t // 2, t % 2
    rows = n_t * rc
    width, hidden_width = gw_ref.shape
    steps = width // tile

    def fetch(f):
        at = pl.ds(pl.multiple_of(f * tile, LANES), tile)
        return [
            pltpu.make_async_copy(w.at[at], w_scr.at[f, k], w_sem.at[f, k]) for k, w in enumerate((gw_ref, uw_ref))
        ]

    for f in range(steps):
        for copy in fetch(f):
            copy.start()

    for p in range(n_t):
        owner = owner_of(p, y, c, ny)
        slot = lax.rem(owner // g + n_dp - z, n_dp) * g + owner % g
        mine = [factor[q * rc : (q + 1) * rc, :] for factor in factors[p]]
        g_scr[slot], u_scr[slot] = grads_of(sums[p % 2][owner // 2, :, :hidden_width], mine)
    q_gate = fdot(g_scr[...].reshape(rows, hidden_width), b_ref[...], NT)
    q_up = fdot(u_scr[...].reshape(rows, hidden_width), b_ref[...], NT)
    lane = lax.broadcasted_iota(jnp.int32, (rc, 2 * R * TENANTS), 1)
    shares = []
    for r in range(n_dp):
        share = []
        for j in range(g):
            at = slice((r * g + j) * rc, (r * g + j + 1) * rc)
            tenant = tenant_of(meta, lax.rem(z + r, n_dp) * g + j, own_t)
            mine = jnp.where(lane % (2 * R) < R, q_gate[at], q_up[at])
            mine = jnp.where(lane // (2 * R) == tenant, mine, 0.0)
            q_scr[at, :] = (ADAPTER_SCALE * mine).astype(jnp.bfloat16)
            share.append(sum(mine[:, e * 2 * R : (e + 1) * 2 * R] for e in range(TENANTS)))
        shares.append(jnp.concatenate(share, axis=0))
    share = jnp.concatenate(shares, axis=1).astype(jnp.bfloat16)
    for r in range(n_dp):
        outs[r][:, width:] = share

    def body(step, carry):
        at = pl.ds(pl.multiple_of(step * tile, LANES), tile)
        for copy in fetch(step):
            copy.wait()
        acc = fdot(g_scr[...].reshape(rows, hidden_width), w_scr[step, 0], NT)
        acc = acc + fdot(u_scr[...].reshape(rows, hidden_width), w_scr[step, 1], NT)
        acc = (acc + fdot(q_scr[...], a_ref[:, at], NN)).astype(jnp.bfloat16)
        for r in range(n_dp):
            outs[r][:, at] = acc[r * g * rc : (r + 1) * g * rc]
        return carry

    lax.fori_loop(0, steps, body, 0)


def input_partial(meta, factors, q, sums, gate_weight, up_weight, b_gu, a_gu, n_dp, own_t):
    n_t = len(factors)
    ny, rc, _ = sums[0].shape
    g = n_t // n_dp
    width, hidden_width = gate_weight.shape
    tile = tile_of(width, 256)
    low = 2 * R * TENANTS
    rows = n_t * rc
    outs = [jax.ShapeDtypeStruct((g * rc, width + n_dp * 2 * R), jnp.bfloat16)] * n_dp
    return pl.pallas_call(
        functools.partial(input_kernel, (n_dp, n_t, g, own_t, rc, q, tile)),
        out_shape=outs,
        in_specs=[SMEM] + [VMEM] * (2 * n_t + 2) + [ANY] * 2 + [VMEM] * 2,
        out_specs=[VMEM] * n_dp,
        scratch_shapes=[
            pltpu.VMEM((n_t, rc, hidden_width), jnp.bfloat16),
            pltpu.VMEM((n_t, rc, hidden_width), jnp.bfloat16),
            pltpu.VMEM((rows, low), jnp.bfloat16),
            pltpu.VMEM((width // tile, 2, tile, hidden_width), jnp.bfloat16),
            pltpu.SemaphoreType.DMA((width // tile, 2)),
        ],
        compiler_params=pltpu.CompilerParams(vmem_limit_bytes=STREAM_LIMIT),
        cost_estimate=NO_COST,
        name="input_partial",
    )(meta, *[x for pair in factors for x in pair], *sums, gate_weight, up_weight, b_gu, a_gu)


def left_of(left_ref, layer, owners):
    return jnp.concatenate([left_ref[layer, owner] for owner in owners], axis=1)


def down_outer_kernel(n_dp, g, chunks, meta, *refs):
    pieces, (left_ref, out_ref) = refs[: n_dp * chunks], refs[n_dp * chunks :]
    owners = [lax.rem(meta[0] + (n_dp - k), n_dp) * g + j for k in range(n_dp) for j in range(g)]
    right = [pieces[q * n_dp + k][j] for k in range(n_dp) for j in range(g) for q in range(chunks)]
    out = ADAPTER_SCALE * fdot(left_of(left_ref, 0, owners), jnp.concatenate(right, axis=0), NN)
    out_ref[...] = out.reshape(out_ref.shape)


def down_outer(meta, grads, left):
    n_dp, chunks = len(grads[0]), len(grads)
    pieces = [piece for pieces in grads for piece in pieces]
    g, _, width = pieces[0].shape
    tile = tile_of(width, 512)
    return pl.pallas_call(
        functools.partial(down_outer_kernel, n_dp, g, chunks),
        out_shape=jax.ShapeDtypeStruct((TENANTS, R, width), jnp.float32),
        grid_spec=pltpu.PrefetchScalarGridSpec(
            num_scalar_prefetch=1,
            grid=(width // tile,),
            in_specs=[
                pl.BlockSpec(piece.shape[:2] + (tile,), lambda f, *_: (0, 0, f)) for piece in pieces
            ]
            + [whole(left.shape)],
            out_specs=pl.BlockSpec((TENANTS, R, tile), lambda f, *_: (0, 0, f)),
        ),
        compiler_params=pltpu.CompilerParams(vmem_limit_bytes=VMEM_LIMIT),
        cost_estimate=NO_COST,
        name="down_outer",
    )(meta, *pieces, left)


def gate_up_outer_kernel(n_t, chunks, meta, *refs):
    ny = n_t // 2
    factors, refs = [refs[2 * p : 2 * p + 2] for p in range(n_t)], refs[2 * n_t :]
    sums, (left_ref, out_ref) = [refs[2 * q : 2 * q + 2] for q in range(chunks)], refs[2 * chunks :]
    y, c = meta[1] // 2, meta[1] % 2
    owners = [owner_of(p, y, c, ny) for p in range(n_t)]
    grads = []
    for p in range(n_t):
        total = jnp.concatenate([both[p % 2][owners[p] // 2] for both in sums], axis=0)
        grads.append(grads_of(total, factors[p]))
    for layer in range(2):
        right = jnp.concatenate([grad[layer] for grad in grads], axis=0)
        out = ADAPTER_SCALE * fdot(left_of(left_ref, layer, owners), right, NN)
        out_ref[:, layer * R : (layer + 1) * R, :] = out.reshape(TENANTS, R, out.shape[1])


def gate_up_outer(meta, factors, sums, left):
    n_t, chunks = len(factors), len(sums)
    rc = sums[0][0].shape[1]
    own_t, width = factors[0][0].shape
    tile = tile_of(width, 896)
    return pl.pallas_call(
        functools.partial(gate_up_outer_kernel, n_t, chunks),
        out_shape=jax.ShapeDtypeStruct((TENANTS, 2 * R, width), jnp.float32),
        grid_spec=pltpu.PrefetchScalarGridSpec(
            num_scalar_prefetch=1,
            grid=(width // tile,),
            in_specs=[pl.BlockSpec((own_t, tile), lambda f, *_: (0, f))] * (2 * n_t)
            + [pl.BlockSpec((n_t // 2, rc, tile), lambda f, *_: (0, 0, f))] * (2 * chunks)
            + [whole(left.shape)],
            out_specs=pl.BlockSpec((TENANTS, 2 * R, tile), lambda f, *_: (0, 0, f)),
        ),
        compiler_params=pltpu.CompilerParams(vmem_limit_bytes=2 * VMEM_LIMIT),
        cost_estimate=NO_COST,
        name="gate_up_outer",
    )(meta, *[x for pair in factors for x in pair], *[x for both in sums for x in both], left)


def down_part_kernel(chunks, meta, *refs):
    sums, (hidden_ref, out_ref) = refs[:chunks], refs[chunks:]
    width = hidden_ref.shape[1]
    low = jnp.concatenate([both[meta[1] // 2][:, width:] for both in sums], axis=0)
    part = fdot(low, hidden_ref[...], TN)
    out_ref[...] = sum(part[e * R : (e + 1) * R] for e in range(TENANTS)).astype(jnp.bfloat16)


def down_part(meta, sums, hidden):
    return pl.pallas_call(
        functools.partial(down_part_kernel, len(sums)),
        out_shape=jax.ShapeDtypeStruct((R, hidden.shape[1]), jnp.bfloat16),
        in_specs=[SMEM] + [VMEM] * (len(sums) + 1),
        out_specs=VMEM,
        compiler_params=pltpu.CompilerParams(vmem_limit_bytes=VMEM_LIMIT),
        cost_estimate=NO_COST,
        name="down_part",
    )(meta, *sums, hidden)


def spread_kernel(tenant_at, rows, meta, *refs):
    parts, out_ref = refs[:-1], refs[-1]
    out_ref[...] = jnp.zeros_like(out_ref)
    at = 0
    for part in parts:
        for k in range(part.shape[0] // rows):
            tenant = tenant_at(at, meta)
            term = part[k * rows : (k + 1) * rows].astype(jnp.float32)
            out_ref[tenant] = out_ref[tenant] + ADAPTER_SCALE * term
            at += 1


def spread(meta, parts, tenant_at, rows, name):
    width = parts[0].shape[1]
    out = jax.ShapeDtypeStruct((TENANTS, rows, width), jnp.float32)
    tile = tile_of(width, 1024)
    return pl.pallas_call(
        functools.partial(spread_kernel, tenant_at, rows),
        out_shape=out,
        grid_spec=pltpu.PrefetchScalarGridSpec(
            num_scalar_prefetch=1,
            grid=(width // tile,),
            in_specs=[pl.BlockSpec((part.shape[0], tile), lambda f, *_: (0, f)) for part in parts],
            out_specs=pl.BlockSpec((TENANTS, rows, tile), lambda f, *_: (0, 0, f)),
        ),
        compiler_params=pltpu.CompilerParams(vmem_limit_bytes=VMEM_LIMIT),
        cost_estimate=NO_COST,
        name=name,
    )(meta, *parts)


def in_outer_kernel(n_dp, chunks, g, meta, *refs):
    shares, inputs, out_ref = refs[: n_dp * chunks], refs[n_dp * chunks : -1], refs[-1]
    out_ref[...] = jnp.zeros_like(out_ref)
    own_t = inputs[0].shape[0] // g
    rc = own_t // chunks
    for k in range(n_dp):
        tenant = meta[2 + lax.rem(meta[0] + n_dp - k, n_dp)]
        total = 0.0
        for q in range(chunks):
            query = 0.0
            for s in range(n_dp):
                at = (s + n_dp - k) % n_dp * 2 * R
                query = query + shares[q * n_dp + s][:, at : at + 2 * R].astype(jnp.float32)
            query = query.astype(jnp.bfloat16)
            for j in range(g):
                rows = inputs[k][j * own_t + q * rc : j * own_t + (q + 1) * rc, :]
                total = total + fdot(query[j * rc : (j + 1) * rc], rows, TN)
        out_ref[tenant] = out_ref[tenant] + ADAPTER_SCALE * total


def in_outer(meta, shares, inputs, g):
    n_dp, chunks = len(inputs), len(shares)
    width = inputs[0].shape[1]
    shares = [share[:, width:] for there in shares for share in there]
    return pl.pallas_call(
        functools.partial(in_outer_kernel, n_dp, chunks, g),
        out_shape=jax.ShapeDtypeStruct((TENANTS, 2 * R, width), jnp.float32),
        in_specs=[SMEM] + [VMEM] * (len(shares) + n_dp),
        out_specs=VMEM,
        compiler_params=pltpu.CompilerParams(vmem_limit_bytes=VMEM_LIMIT),
        cost_estimate=NO_COST,
        name="in_outer",
    )(meta, *shares, *inputs)


def ring(n, by):
    return [(k, (k + by) % n) for k in range(n)]


def add32(*terms):
    return sum(term.astype(jnp.float32) for term in terms)


def after(value, *done):
    return lax.optimization_barrier((value,) + done)[0]


def per_device(
    layer_input,
    out_grad,
    gate_pre,
    up_pre,
    adapter_acts,
    gate_weight,
    up_weight,
    down_weight,
    adapter_a_gu,
    adapter_b_gu,
    adapter_a_down,
    adapter_b_down,
    block_tenant,
):
    n_dp, n_t = lax.axis_size("dp"), lax.axis_size("tensor")
    ny = n_t // 2
    z, t = lax.axis_index("dp"), lax.axis_index("tensor")
    own_rows, width = out_grad.shape
    own_t, hidden_width = gate_pre.shape
    tokens = adapter_acts.shape[0]
    g = own_rows // own_t
    assert own_rows == BLOCK and g * own_t == own_rows and n_t == 2 * ny and n_t == g * n_dp
    chunks, at = [], 0
    for share in SHARES:
        chunks.append((at, own_t * share // sum(SHARES)))
        at += chunks[-1][1]

    meta = jnp.concatenate([jnp.stack([z, t]).astype(jnp.int32), block_tenant])
    b_down = adapter_b_down.reshape(TENANTS * R, width)
    a_down = jnp.transpose(adapter_a_down, (0, 2, 1)).reshape(TENANTS * R, hidden_width)
    b_gu = adapter_b_gu.reshape(TENANTS * 2 * R, hidden_width)
    a_gu = jnp.transpose(adapter_a_gu, (0, 2, 1)).reshape(TENANTS * 2 * R, width)

    pair = [(k, k ^ 1) for k in range(n_t)]
    z_next = ring(n_dp, 1)

    stored = (gate_pre, up_pre)
    far_stored = [[lax.ppermute(x, "tensor", ring(n_t, 2 * s)) for x in stored] for s in range(1, ny)]
    grads = [[out_grad.reshape(g, own_t, width)[:, at : at + rc]] for at, rc in chunks]
    for step in range(n_dp - 1):
        for q, pieces in enumerate(grads):
            piece = pieces[-1]
            if q == 0 and step == n_dp - 2:
                piece = after(piece, *[there[0] for there in far_stored])
            pieces.append(lax.ppermute(piece, "dp", z_next))

    def first(q, done):
        pieces = [after(grads[q][0], *done)] + grads[q][1:]
        keep, send = hidden_partial(meta, pieces, down_weight, b_down, a_down, n_t, own_t)
        return keep, lax.ppermute(send, "tensor", pair)

    keep_a, other_a = first(0, (grads[1][1],))
    adapter_acts, gate_pre, up_pre = after((adapter_acts, gate_pre, up_pre), keep_a)
    onehot = (
        jnp.arange(TENANTS, dtype=jnp.int32)[:, None] == jnp.repeat(block_tenant, BLOCK)[None, :]
    ).astype(jnp.bfloat16)
    acts = adapter_acts.T.reshape(3, 1, R, tokens) * onehot[None, :, None, :]
    acts = acts.reshape(3, TENANTS * R, n_t, own_t).transpose(0, 2, 1, 3)

    def factors_of(gate_pre, up_pre):
        gate_value = gate_pre.astype(jnp.float32)
        up_value = up_pre.astype(jnp.float32)
        sigmoid_value = jax.nn.sigmoid(gate_value)
        dgate = up_value * sigmoid_value * (1.0 + gate_value * (1.0 - sigmoid_value))
        dup = gate_value * sigmoid_value
        return [x.astype(jnp.bfloat16) for x in (dgate, dup, dup * up_value)]

    def exchange(keep, other):
        mine = add32(keep, other).astype(jnp.bfloat16)
        return mine, [lax.ppermute(mine, "tensor", ring(n_t, 2 * s)) for s in range(1, ny)]

    def total(mine, far):
        both = add32(mine, *far).astype(jnp.bfloat16)
        return [both, lax.ppermute(both, "tensor", pair)]

    def second(q, sums, done):
        sums = [after(sums[0], *done), sums[1]]
        outs = input_partial(meta, factors, q, sums, gate_weight, up_weight, b_gu, a_gu, n_dp, own_t)
        return [outs[0]] + [lax.ppermute(outs[r], "dp", ring(n_dp, r)) for r in range(1, n_dp)]

    def finish(there, rc):
        return add32(*[x[:, :width] for x in there]).astype(jnp.bfloat16).reshape(g, rc, width)

    *near, hidden = factors_of(gate_pre, up_pre)
    beside = [lax.ppermute(x, "tensor", pair) for x in (gate_pre, up_pre)]
    mine_a, far_a = exchange(after(keep_a, near[0], *[there[1] for there in far_stored]), other_a)
    inputs = [after(layer_input, grads[-1][-1])]
    for _ in range(n_dp - 1):
        inputs.append(lax.ppermute(inputs[-1], "dp", z_next))
    keep_b, other_b = first(1, (mine_a,))
    factors = [near, factors_of(after(beside[0], keep_b), beside[1])[:2]]
    mine_b, far_b = exchange(after(keep_b, factors[1][0]), other_b)
    for there in far_stored:
        there = [after(x, keep_b) for x in there]
        beside = [lax.ppermute(x, "tensor", pair) for x in there]
        there[0] = after(there[0], mine_b)
        factors += [factors_of(*there)[:2], factors_of(*beside)[:2]]
    sums_a = total(after(mine_a, *[pair[0] for pair in factors]), far_a)
    there_a = second(0, sums_a, ())
    sums_b = total(after(mine_b, there_a[0], inputs[-1]), far_b)

    a_part = down_part(meta, [sums_a[0], sums_b[0]], hidden)
    a_column = [a_part] + [lax.ppermute(a_part, "tensor", ring(n_t, 2 * s)) for s in range(1, ny)]
    there_b = second(1, sums_b, (a_part,))

    a_column = [after(a_column[0], there_b[0])] + a_column[1:]
    a_beside = lax.ppermute(jnp.concatenate(a_column, axis=0), "tensor", pair)
    grad_b_down = down_outer(meta, grads, after(acts[2:], there_b[0]))
    grad_b_gu = gate_up_outer(meta, factors, [sums_a, sums_b], after(acts[:2], grad_b_down))

    def column_tenant(p, m):
        owner = lax.rem(m[1] // 2 + ny - p % ny, ny) * 2
        return tenant_of(m, owner + (m[1] % 2 if p < ny else 1 - m[1] % 2), own_t)

    a_column[0] = after(a_column[0], grad_b_gu)
    grad_a_down = spread(meta, a_column + [a_beside], column_tenant, R, "spread_a_down")
    there_b[0] = after(there_b[0], grad_a_down)
    grad_a_gu = in_outer(meta, [there_a, there_b], inputs, g)
    half_a = finish([after(there_a[0], grad_a_down)] + there_a[1:], chunks[0][1])
    half_b = finish(there_b, chunks[1][1])
    block_input_grad = jnp.concatenate([half_a, half_b], axis=1).reshape(own_rows, width)
    return (
        block_input_grad,
        grad_a_gu.transpose(0, 2, 1),
        grad_b_gu,
        grad_a_down.transpose(0, 2, 1),
        grad_b_down,
    )


def solution(mesh):
    placed = (
        P(("groups", "dp"), "tensor"),
        P(("groups", "dp"), "tensor"),
        P(("groups", "tensor"), "dp"),
        P(("groups", "tensor"), "dp"),
        P("groups", None),
        P("tensor", "dp"),
        P("tensor", "dp"),
        P("dp", "tensor"),
        P(None, "tensor", None),
        P(None, None, "dp"),
        P(None, "dp", None),
        P(None, None, "tensor"),
        P("groups"),
    )
    return jax.shard_map(
        per_device,
        mesh=mesh,
        in_specs=placed,
        out_specs=(
            P(("groups", "dp"), "tensor"),
            P("groups", "tensor", None),
            P("groups", None, "dp"),
            P("groups", "dp", None),
            P("groups", None, "tensor"),
        ),
        check_vma=False,
    )
```

```python
import functools

import jax
import jax.numpy as jnp
from jax import lax
from jax.experimental import pallas as pl
from jax.experimental.pallas import tpu as pltpu
from jax.sharding import PartitionSpec as P

R = 16
TENANTS = 4
BLOCK = 128
SHARES = (1, 1)
LANES = 128
VMEM_LIMIT = 12 * 1024 * 1024
STREAM_LIMIT = 50 * 1024 * 1024

ADAPTER_SCALE = 2.0

NT = (((1,), (1,)), ((), ()))
NN = (((1,), (0,)), ((), ()))
TN = (((0,), (0,)), ((), ()))
ANY = pl.BlockSpec(memory_space=pl.ANY)
SMEM = pl.BlockSpec(memory_space=pltpu.SMEM)
VMEM = pl.BlockSpec(memory_space=pltpu.VMEM)
NO_COST = pl.CostEstimate(flops=1, bytes_accessed=1, transcendentals=0)


def fdot(lhs, rhs, dims):
    return lax.dot_general(lhs, rhs, dims, preferred_element_type=jnp.float32)


def tile_of(width, most):
    tile = most
    while width % tile:
        tile -= LANES
    return tile


def whole(shape):
    return pl.BlockSpec(shape, lambda *_: (0,) * len(shape))


def tenant_of(meta, owner, own_t):
    return meta[2 + (owner * own_t) // BLOCK]


def owner_of(p, y, c, ny):
    return lax.rem(y + ny - p // 2, ny) * 2 + (c if p % 2 == 0 else 1 - c)


def hidden_kernel(sizes, meta, *refs):
    n_dp, n_t, g, own_t, rc, tile = sizes
    ny = n_t // 2
    pieces, (w_ref, bd_ref, ad_ref, keep_ref, send_ref), refs = refs[:n_dp], refs[n_dp : n_dp + 5], refs[n_dp + 5 :]
    x_scr, p_scr, w_scr, w_sem = refs
    z, t = meta[0], meta[1]
    y, c = t // 2, t % 2
    hidden_width, width = w_ref.shape
    steps = hidden_width // tile

    def fetch(f):
        rows = pl.ds(pl.multiple_of(f * tile, LANES), tile)
        return pltpu.make_async_copy(w_ref.at[rows], w_scr.at[f], w_sem.at[f])

    for f in range(steps):
        fetch(f).start()

    for k in range(n_dp):
        for j in range(g):
            owner = lax.rem(z + (n_dp - k), n_dp) * g + j
            away = jnp.where(owner % 2 == c, 0, ny)
            x_scr[away + owner // 2] = pieces[k][j]
    proj = fdot(x_scr[...].reshape(n_t * rc, width), bd_ref[...], NT)
    lane = lax.broadcasted_iota(jnp.int32, (rc, TENANTS * R), 1) // R
    zeros = jnp.zeros((rc, LANES - TENANTS * R), jnp.bfloat16)
    for s in range(n_t):
        owner = (s % ny) * 2 + (c if s < ny else 1 - c)
        own = jnp.where(lane == tenant_of(meta, owner, own_t), proj[s * rc : (s + 1) * rc], 0.0)
        p_scr[s * rc : (s + 1) * rc, :] = (ADAPTER_SCALE * own).astype(jnp.bfloat16)
        out = keep_ref if s < ny else send_ref
        out[s % ny, :, hidden_width:] = jnp.concatenate([own.astype(jnp.bfloat16), zeros], axis=1)

    def body(step, carry):
        at = pl.ds(pl.multiple_of(step * tile, LANES), tile)
        fetch(step).wait()
        acc = fdot(x_scr[...].reshape(n_t * rc, width), w_scr[step], NT)
        acc = (acc + fdot(p_scr[...], ad_ref[:, at], NN)).astype(jnp.bfloat16).reshape(n_t, rc, tile)
        keep_ref[:, :, at] = acc[:ny]
        send_ref[:, :, at] = acc[ny:]
        return carry

    lax.fori_loop(0, steps, body, 0)


def hidden_partial(meta, pieces, down_weight, b_down, a_down, n_t, own_t):
    n_dp = len(pieces)
    g, rc, width = pieces[0].shape
    ny = n_t // 2
    hidden_width = down_weight.shape[0]
    tile = tile_of(hidden_width, 512)
    low = TENANTS * R
    out = jax.ShapeDtypeStruct((ny, rc, hidden_width + LANES), jnp.bfloat16)
    return pl.pallas_call(
        functools.partial(hidden_kernel, (n_dp, n_t, g, own_t, rc, tile)),
        out_shape=(out, out),
        in_specs=[SMEM] + [VMEM] * n_dp + [ANY] + [VMEM] * 2,
        out_specs=[VMEM] * 2,
        scratch_shapes=[
            pltpu.VMEM((n_t, rc, width), jnp.bfloat16),
            pltpu.VMEM((n_t * rc, low), jnp.bfloat16),
            pltpu.VMEM((hidden_width // tile, tile, width), jnp.bfloat16),
            pltpu.SemaphoreType.DMA((hidden_width // tile,)),
        ],
        compiler_params=pltpu.CompilerParams(vmem_limit_bytes=STREAM_LIMIT),
        cost_estimate=NO_COST,
        name="hidden_partial",
    )(meta, *pieces, down_weight, b_down, a_down)


def grads_of(total, factors):
    total = total.astype(jnp.float32)
    return [(total * factor[...].astype(jnp.float32)).astype(jnp.bfloat16) for factor in factors]


def input_kernel(sizes, meta, *refs):
    n_dp, n_t, g, own_t, rc, q, tile = sizes
    ny = n_t // 2
    factors, refs = [refs[2 * p : 2 * p + 2] for p in range(n_t)], refs[2 * n_t :]
    sums, (gw_ref, uw_ref, b_ref, a_ref) = refs[:2], refs[2:6]
    outs, (g_scr, u_scr, q_scr, w_scr, w_sem) = refs[6 : 6 + n_dp], refs[6 + n_dp :]
    z, t = meta[0], meta[1]
    y, c = t // 2, t % 2
    rows = n_t * rc
    width, hidden_width = gw_ref.shape
    steps = width // tile

    def fetch(f):
        at = pl.ds(pl.multiple_of(f * tile, LANES), tile)
        return [
            pltpu.make_async_copy(w.at[at], w_scr.at[f, k], w_sem.at[f, k]) for k, w in enumerate((gw_ref, uw_ref))
        ]

    for f in range(steps):
        for copy in fetch(f):
            copy.start()

    for p in range(n_t):
        owner = owner_of(p, y, c, ny)
        slot = lax.rem(owner // g + n_dp - z, n_dp) * g + owner % g
        mine = [factor[q * rc : (q + 1) * rc, :] for factor in factors[p]]
        g_scr[slot], u_scr[slot] = grads_of(sums[p % 2][owner // 2, :, :hidden_width], mine)
    q_gate = fdot(g_scr[...].reshape(rows, hidden_width), b_ref[...], NT)
    q_up = fdot(u_scr[...].reshape(rows, hidden_width), b_ref[...], NT)
    lane = lax.broadcasted_iota(jnp.int32, (rc, 2 * R * TENANTS), 1)
    shares = []
    for r in range(n_dp):
        share = []
        for j in range(g):
            at = slice((r * g + j) * rc, (r * g + j + 1) * rc)
            tenant = tenant_of(meta, lax.rem(z + r, n_dp) * g + j, own_t)
            mine = jnp.where(lane % (2 * R) < R, q_gate[at], q_up[at])
            mine = jnp.where(lane // (2 * R) == tenant, mine, 0.0)
            q_scr[at, :] = (ADAPTER_SCALE * mine).astype(jnp.bfloat16)
            share.append(sum(mine[:, e * 2 * R : (e + 1) * 2 * R] for e in range(TENANTS)))
        shares.append(jnp.concatenate(share, axis=0))
    share = jnp.concatenate(shares, axis=1).astype(jnp.bfloat16)
    for r in range(n_dp):
        outs[r][:, width:] = share

    def body(step, carry):
        at = pl.ds(pl.multiple_of(step * tile, LANES), tile)
        for copy in fetch(step):
            copy.wait()
        acc = fdot(g_scr[...].reshape(rows, hidden_width), w_scr[step, 0], NT)
        acc = acc + fdot(u_scr[...].reshape(rows, hidden_width), w_scr[step, 1], NT)
        acc = (acc + fdot(q_scr[...], a_ref[:, at], NN)).astype(jnp.bfloat16)
        for r in range(n_dp):
            outs[r][:, at] = acc[r * g * rc : (r + 1) * g * rc]
        return carry

    lax.fori_loop(0, steps, body, 0)


def input_partial(meta, factors, q, sums, gate_weight, up_weight, b_gu, a_gu, n_dp, own_t):
    n_t = len(factors)
    ny, rc, _ = sums[0].shape
    g = n_t // n_dp
    width, hidden_width = gate_weight.shape
    tile = tile_of(width, 256)
    low = 2 * R * TENANTS
    rows = n_t * rc
    outs = [jax.ShapeDtypeStruct((g * rc, width + n_dp * 2 * R), jnp.bfloat16)] * n_dp
    return pl.pallas_call(
        functools.partial(input_kernel, (n_dp, n_t, g, own_t, rc, q, tile)),
        out_shape=outs,
        in_specs=[SMEM] + [VMEM] * (2 * n_t + 2) + [ANY] * 2 + [VMEM] * 2,
        out_specs=[VMEM] * n_dp,
        scratch_shapes=[
            pltpu.VMEM((n_t, rc, hidden_width), jnp.bfloat16),
            pltpu.VMEM((n_t, rc, hidden_width), jnp.bfloat16),
            pltpu.VMEM((rows, low), jnp.bfloat16),
            pltpu.VMEM((width // tile, 2, tile, hidden_width), jnp.bfloat16),
            pltpu.SemaphoreType.DMA((width // tile, 2)),
        ],
        compiler_params=pltpu.CompilerParams(vmem_limit_bytes=STREAM_LIMIT),
        cost_estimate=NO_COST,
        name="input_partial",
    )(meta, *[x for pair in factors for x in pair], *sums, gate_weight, up_weight, b_gu, a_gu)


def acts_kernel(meta, acts_ref, out_ref):
    layers, n_t, _, own_t = out_ref.shape
    for owner in range(n_t):
        tenant = tenant_of(meta, owner, own_t)
        for layer in range(layers):
            mine = acts_ref[layer * R : (layer + 1) * R, owner * own_t : (owner + 1) * own_t]
            for e in range(TENANTS):
                chosen = jnp.where(tenant == e, mine.astype(jnp.float32), 0.0)
                out_ref[layer, owner, e * R : (e + 1) * R, :] = chosen.astype(jnp.bfloat16)


def masked_acts(meta, acts, n_t):
    return pl.pallas_call(
        acts_kernel,
        out_shape=jax.ShapeDtypeStruct((3, n_t, TENANTS * R, acts.shape[1] // n_t), jnp.bfloat16),
        in_specs=[SMEM, VMEM],
        out_specs=VMEM,
        compiler_params=pltpu.CompilerParams(vmem_limit_bytes=VMEM_LIMIT),
        cost_estimate=NO_COST,
        name="masked_acts",
    )(meta, acts)


def left_of(left_ref, layer, owners):
    return jnp.concatenate([left_ref[layer, owner] for owner in owners], axis=1)


def down_outer_kernel(n_dp, g, chunks, meta, *refs):
    pieces, (left_ref, out_ref) = refs[: n_dp * chunks], refs[n_dp * chunks :]
    owners = [lax.rem(meta[0] + (n_dp - k), n_dp) * g + j for k in range(n_dp) for j in range(g)]
    right = [pieces[q * n_dp + k][j] for k in range(n_dp) for j in range(g) for q in range(chunks)]
    out = ADAPTER_SCALE * fdot(left_of(left_ref, 2, owners), jnp.concatenate(right, axis=0), NN)
    out_ref[...] = out.reshape(out_ref.shape)


def down_outer(meta, grads, left):
    n_dp, chunks = len(grads[0]), len(grads)
    pieces = [piece for pieces in grads for piece in pieces]
    g, _, width = pieces[0].shape
    tile = tile_of(width, 512)
    return pl.pallas_call(
        functools.partial(down_outer_kernel, n_dp, g, chunks),
        out_shape=jax.ShapeDtypeStruct((TENANTS, R, width), jnp.float32),
        grid_spec=pltpu.PrefetchScalarGridSpec(
            num_scalar_prefetch=1,
            grid=(width // tile,),
            in_specs=[
                pl.BlockSpec(piece.shape[:2] + (tile,), lambda f, *_: (0, 0, f)) for piece in pieces
            ]
            + [whole(left.shape)],
            out_specs=pl.BlockSpec((TENANTS, R, tile), lambda f, *_: (0, 0, f)),
        ),
        compiler_params=pltpu.CompilerParams(vmem_limit_bytes=VMEM_LIMIT),
        cost_estimate=NO_COST,
        name="down_outer",
    )(meta, *pieces, left)


def gate_up_outer_kernel(n_t, chunks, meta, *refs):
    ny = n_t // 2
    factors, refs = [refs[2 * p : 2 * p + 2] for p in range(n_t)], refs[2 * n_t :]
    sums, (left_ref, out_ref) = [refs[2 * q : 2 * q + 2] for q in range(chunks)], refs[2 * chunks :]
    y, c = meta[1] // 2, meta[1] % 2
    owners = [owner_of(p, y, c, ny) for p in range(n_t)]
    grads = []
    for p in range(n_t):
        total = jnp.concatenate([both[p % 2][owners[p] // 2] for both in sums], axis=0)
        grads.append(grads_of(total, factors[p]))
    for layer in range(2):
        right = jnp.concatenate([grad[layer] for grad in grads], axis=0)
        out = ADAPTER_SCALE * fdot(left_of(left_ref, layer, owners), right, NN)
        out_ref[:, layer * R : (layer + 1) * R, :] = out.reshape(TENANTS, R, out.shape[1])


def gate_up_outer(meta, factors, sums, left):
    n_t, chunks = len(factors), len(sums)
    rc = sums[0][0].shape[1]
    own_t, width = factors[0][0].shape
    tile = tile_of(width, 896)
    return pl.pallas_call(
        functools.partial(gate_up_outer_kernel, n_t, chunks),
        out_shape=jax.ShapeDtypeStruct((TENANTS, 2 * R, width), jnp.float32),
        grid_spec=pltpu.PrefetchScalarGridSpec(
            num_scalar_prefetch=1,
            grid=(width // tile,),
            in_specs=[pl.BlockSpec((own_t, tile), lambda f, *_: (0, f))] * (2 * n_t)
            + [pl.BlockSpec((n_t // 2, rc, tile), lambda f, *_: (0, 0, f))] * (2 * chunks)
            + [whole(left.shape)],
            out_specs=pl.BlockSpec((TENANTS, 2 * R, tile), lambda f, *_: (0, 0, f)),
        ),
        compiler_params=pltpu.CompilerParams(vmem_limit_bytes=2 * VMEM_LIMIT),
        cost_estimate=NO_COST,
        name="gate_up_outer",
    )(meta, *[x for pair in factors for x in pair], *[x for both in sums for x in both], left)


def down_part_kernel(chunks, meta, *refs):
    sums, (hidden_ref, out_ref) = refs[:chunks], refs[chunks:]
    width = hidden_ref.shape[1]
    low = jnp.concatenate([both[meta[1] // 2][:, width:] for both in sums], axis=0)
    part = fdot(low, hidden_ref[...], TN)
    out_ref[...] = sum(part[e * R : (e + 1) * R] for e in range(TENANTS)).astype(jnp.bfloat16)


def down_part(meta, sums, hidden):
    return pl.pallas_call(
        functools.partial(down_part_kernel, len(sums)),
        out_shape=jax.ShapeDtypeStruct((R, hidden.shape[1]), jnp.bfloat16),
        in_specs=[SMEM] + [VMEM] * (len(sums) + 1),
        out_specs=VMEM,
        compiler_params=pltpu.CompilerParams(vmem_limit_bytes=VMEM_LIMIT),
        cost_estimate=NO_COST,
        name="down_part",
    )(meta, *sums, hidden)


def spread_kernel(tenant_at, rows, meta, *refs):
    parts, out_ref = refs[:-1], refs[-1]
    out_ref[...] = jnp.zeros_like(out_ref)
    at = 0
    for part in parts:
        for k in range(part.shape[0] // rows):
            tenant = tenant_at(at, meta)
            term = part[k * rows : (k + 1) * rows].astype(jnp.float32)
            out_ref[tenant] = out_ref[tenant] + ADAPTER_SCALE * term
            at += 1


def spread(meta, parts, tenant_at, rows, name):
    width = parts[0].shape[1]
    out = jax.ShapeDtypeStruct((TENANTS, rows, width), jnp.float32)
    tile = tile_of(width, 1024)
    return pl.pallas_call(
        functools.partial(spread_kernel, tenant_at, rows),
        out_shape=out,
        grid_spec=pltpu.PrefetchScalarGridSpec(
            num_scalar_prefetch=1,
            grid=(width // tile,),
            in_specs=[pl.BlockSpec((part.shape[0], tile), lambda f, *_: (0, f)) for part in parts],
            out_specs=pl.BlockSpec((TENANTS, rows, tile), lambda f, *_: (0, 0, f)),
        ),
        compiler_params=pltpu.CompilerParams(vmem_limit_bytes=VMEM_LIMIT),
        cost_estimate=NO_COST,
        name=name,
    )(meta, *parts)


def in_outer_kernel(n_dp, chunks, g, meta, *refs):
    shares, inputs_ref, out_ref = refs[: n_dp * chunks], refs[-2], refs[-1]
    out_ref[...] = jnp.zeros_like(out_ref)
    _, rows, width = inputs_ref.shape
    own_t = rows // g
    rc = own_t // chunks
    for k in range(n_dp):
        block = lax.rem(meta[0] + n_dp - k, n_dp)
        queries = []
        for q in range(chunks):
            query = 0.0
            for s in range(n_dp):
                at = width + (s + n_dp - k) % n_dp * 2 * R
                query = query + shares[q * n_dp + s][:, at : at + 2 * R].astype(jnp.float32)
            queries.append(query.astype(jnp.bfloat16))
        low = [queries[q][j * rc : (j + 1) * rc] for j in range(g) for q in range(chunks)]
        total = fdot(jnp.concatenate(low, axis=0), inputs_ref[block], TN)
        tenant = meta[2 + block]
        out_ref[tenant] = out_ref[tenant] + ADAPTER_SCALE * total


def in_outer(meta, shares, inputs, g):
    n_dp, _, width = inputs.shape
    chunks = len(shares)
    shares = [share for there in shares for share in there]
    return pl.pallas_call(
        functools.partial(in_outer_kernel, n_dp, chunks, g),
        out_shape=jax.ShapeDtypeStruct((TENANTS, 2 * R, width), jnp.float32),
        in_specs=[SMEM] + [VMEM] * (len(shares) + 1),
        out_specs=VMEM,
        compiler_params=pltpu.CompilerParams(vmem_limit_bytes=VMEM_LIMIT),
        cost_estimate=NO_COST,
        name="in_outer",
    )(meta, *shares, inputs)


def ring(n, by):
    return [(k, (k + by) % n) for k in range(n)]


def add32(*terms):
    return sum(term.astype(jnp.float32) for term in terms)


def after(value, *done):
    return lax.optimization_barrier((value,) + done)[0]


def per_device(
    layer_input,
    out_grad,
    gate_pre,
    up_pre,
    adapter_acts,
    gate_weight,
    up_weight,
    down_weight,
    adapter_a_gu,
    adapter_b_gu,
    adapter_a_down,
    adapter_b_down,
    block_tenant,
):
    n_dp, n_t = lax.axis_size("dp"), lax.axis_size("tensor")
    ny = n_t // 2
    z, t = lax.axis_index("dp"), lax.axis_index("tensor")
    own_rows, width = out_grad.shape
    own_t, hidden_width = gate_pre.shape
    tokens = adapter_acts.shape[0]
    g = own_rows // own_t
    assert own_rows == BLOCK and g * own_t == own_rows and n_t == 2 * ny and n_t == g * n_dp
    chunks, at = [], 0
    for share in SHARES:
        chunks.append((at, own_t * share // sum(SHARES)))
        at += chunks[-1][1]

    meta = jnp.concatenate([jnp.stack([z, t]).astype(jnp.int32), block_tenant])
    b_down = adapter_b_down.reshape(TENANTS * R, width)
    a_down = jnp.transpose(adapter_a_down, (0, 2, 1)).reshape(TENANTS * R, hidden_width)
    b_gu = adapter_b_gu.reshape(TENANTS * 2 * R, hidden_width)
    a_gu = jnp.transpose(adapter_a_gu, (0, 2, 1)).reshape(TENANTS * 2 * R, width)

    pair = [(k, k ^ 1) for k in range(n_t)]
    z_next = ring(n_dp, 1)

    stored = [gate_pre, up_pre]
    far_stored = [[lax.ppermute(x, "tensor", ring(n_t, 2 * s)) for x in stored] for s in range(1, ny)]
    grads = [[out_grad.reshape(g, own_t, width)[:, at : at + rc]] for at, rc in chunks]
    for _ in range(n_dp - 1):
        grads[0].append(lax.ppermute(grads[0][-1], "dp", z_next))
    stored[0] = after(stored[0], grads[0][1])
    beside_stored = [lax.ppermute(x, "tensor", pair) for x in stored]
    grads[1][0] = after(grads[1][0], grads[0][2])
    for _ in range(n_dp - 2):
        grads[1].append(lax.ppermute(grads[1][-1], "dp", z_next))

    def first(q, done):
        pieces = [after(grads[q][0], *done)] + grads[q][1:]
        keep, send = hidden_partial(meta, pieces, down_weight, b_down, a_down, n_t, own_t)
        return keep, send

    def factors_of(stored):
        gate_value, up_value = [x.astype(jnp.float32) for x in stored]
        sigmoid_value = jax.nn.sigmoid(gate_value)
        dgate = up_value * sigmoid_value * (1.0 + gate_value * (1.0 - sigmoid_value))
        dup = gate_value * sigmoid_value
        return [x.astype(jnp.bfloat16) for x in (dgate, dup, dup * up_value)]

    def exchange(keep, other):
        mine = add32(keep, other).astype(jnp.bfloat16)
        return mine, [lax.ppermute(mine, "tensor", ring(n_t, 2 * s)) for s in range(1, ny)]

    def total(mine, far):
        both = add32(mine, *far).astype(jnp.bfloat16)
        return [both, lax.ppermute(both, "tensor", pair)]

    def second(q, sums, done):
        sums = [after(sums[0], *done), sums[1]]
        outs = input_partial(meta, factors, q, sums, gate_weight, up_weight, b_gu, a_gu, n_dp, own_t)
        return [outs[0]] + [lax.ppermute(outs[r], "dp", ring(n_dp, r)) for r in range(1, n_dp)]

    def finish(there, rc):
        return add32(*[x[:, :width] for x in there]).astype(jnp.bfloat16).reshape(g, rc, width)

    *near, hidden = factors_of(stored)
    factors = [near, factors_of(beside_stored)[:2]]
    keep_a, send_a = first(0, (grads[1][1], near[0], factors[1][0]))
    other_a = lax.ppermute(after(send_a, *[x for there in far_stored for x in there]), "tensor", pair)
    mine_a, far_a = exchange(keep_a, other_a)
    grads[1].append(lax.ppermute(after(grads[1][-1], mine_a), "dp", z_next))
    inputs = lax.all_gather(after(layer_input, grads[0][-1]), "dp")
    keep_b, send_b = first(1, (mine_a,))
    other_b = lax.ppermute(send_b, "tensor", pair)
    mine_b, far_b = exchange(keep_b, other_b)
    for there in far_stored:
        beside = [lax.ppermute(x, "tensor", pair) for x in (after(there[0], mine_a), there[1])]
        for both in (there, beside):
            factors.append(factors_of([after(both[0], keep_b), both[1]])[:2])
    sums_a = total(after(mine_a, mine_b, *[pair[0] for pair in factors]), far_a)
    there_a = second(0, sums_a, ())
    sums_b = total(after(mine_b, there_a[0]), far_b)
    a_part = down_part(meta, [sums_a[0], sums_b[0]], hidden)
    a_parts = [a_part] + [lax.ppermute(a_part, "tensor", ring(n_t, 2 * s)) for s in range(1, ny)]
    there_b = second(1, sums_b, (a_part, inputs))

    half_a = finish([after(x, there_b[0]) for x in there_a], chunks[0][1])
    acts = masked_acts(meta, after(adapter_acts.T, half_a), n_t)
    grad_b_down = down_outer(meta, grads, acts)
    a_parts = [after(x, half_a) for x in a_parts]
    a_parts += [lax.ppermute(x, "tensor", pair) for x in a_parts]
    grad_b_gu = gate_up_outer(meta, factors, [sums_a, sums_b], after(acts, grad_b_down))

    def column_tenant(p, m):
        owner = lax.rem(m[1] // 2 + ny - p % ny, ny) * 2
        return tenant_of(m, owner + (m[1] % 2 if p < ny else 1 - m[1] % 2), own_t)

    a_parts[0] = after(a_parts[0], grad_b_gu)
    grad_a_down = spread(meta, a_parts, column_tenant, R, "spread_a_down")
    there_b[0] = after(there_b[0], grad_a_down)
    grad_a_gu = in_outer(meta, [there_a, there_b], inputs, g)
    half_b = finish(there_b, chunks[1][1])
    block_input_grad = jnp.concatenate([half_a, half_b], axis=1).reshape(own_rows, width)
    return (
        block_input_grad,
        grad_a_gu.transpose(0, 2, 1),
        grad_b_gu,
        grad_a_down.transpose(0, 2, 1),
        grad_b_down,
    )


def solution(mesh):
    placed = (
        P(("groups", "dp"), "tensor"),
        P(("groups", "dp"), "tensor"),
        P(("groups", "tensor"), "dp"),
        P(("groups", "tensor"), "dp"),
        P("groups", None),
        P("tensor", "dp"),
        P("tensor", "dp"),
        P("dp", "tensor"),
        P(None, "tensor", None),
        P(None, None, "dp"),
        P(None, "dp", None),
        P(None, None, "tensor"),
        P("groups"),
    )
    return jax.shard_map(
        per_device,
        mesh=mesh,
        in_specs=placed,
        out_specs=(
            P(("groups", "dp"), "tensor"),
            P("groups", "tensor", None),
            P("groups", None, "dp"),
            P("groups", "dp", None),
            P("groups", None, "tensor"),
        ),
        check_vma=False,
    )
```

```python
import functools

import jax
import jax.numpy as jnp
from jax import lax
from jax.experimental import pallas as pl
from jax.experimental.pallas import tpu as pltpu
from jax.sharding import PartitionSpec as P

R = 16
TENANTS = 4
BLOCK = 128
SHARES = (1, 1)
LANES = 128
VMEM_LIMIT = 12 * 1024 * 1024
STREAM_LIMIT = 50 * 1024 * 1024

ADAPTER_SCALE = 2.0

NT = (((1,), (1,)), ((), ()))
NN = (((1,), (0,)), ((), ()))
TN = (((0,), (0,)), ((), ()))
ANY = pl.BlockSpec(memory_space=pl.ANY)
SMEM = pl.BlockSpec(memory_space=pltpu.SMEM)
VMEM = pl.BlockSpec(memory_space=pltpu.VMEM)
NO_COST = pl.CostEstimate(flops=1, bytes_accessed=1, transcendentals=0)


def fdot(lhs, rhs, dims):
    return lax.dot_general(lhs, rhs, dims, preferred_element_type=jnp.float32)


def tile_of(width, most):
    tile = most
    while width % tile:
        tile -= LANES
    return tile


def whole(shape):
    return pl.BlockSpec(shape, lambda *_: (0,) * len(shape))


def tenant_of(meta, owner, own_t):
    return meta[2 + (owner * own_t) // BLOCK]


def owner_of(p, y, c, ny):
    return lax.rem(y + ny - p // 2, ny) * 2 + (c if p % 2 == 0 else 1 - c)


def hidden_kernel(sizes, meta, *refs):
    n_dp, n_t, g, own_t, rc, tile = sizes
    ny = n_t // 2
    pieces, (w_ref, bd_ref, ad_ref, keep_ref, send_ref), refs = refs[:n_dp], refs[n_dp : n_dp + 5], refs[n_dp + 5 :]
    x_scr, xt_scr, p_scr, w_scr, w_sem = refs
    z, t = meta[0], meta[1]
    y, c = t // 2, t % 2
    hidden_width, width = w_ref.shape
    steps = hidden_width // tile

    def fetch(f):
        rows = pl.ds(pl.multiple_of(f * tile, LANES), tile)
        return pltpu.make_async_copy(w_ref.at[rows], w_scr.at[f], w_sem.at[f])

    for f in range(steps):
        fetch(f).start()

    for k in range(n_dp):
        for j in range(g):
            owner = lax.rem(z + (n_dp - k), n_dp) * g + j
            away = jnp.where(owner % 2 == c, 0, ny)
            x_scr[away + owner // 2] = pieces[k][j]
    xt_scr[...] = x_scr[...].reshape(n_t * rc, width).T
    proj = fdot(x_scr[...].reshape(n_t * rc, width), bd_ref[...], NT)
    lane = lax.broadcasted_iota(jnp.int32, (rc, TENANTS * R), 1) // R
    zeros = jnp.zeros((rc, LANES - TENANTS * R), jnp.bfloat16)
    for s in range(n_t):
        owner = (s % ny) * 2 + (c if s < ny else 1 - c)
        own = jnp.where(lane == tenant_of(meta, owner, own_t), proj[s * rc : (s + 1) * rc], 0.0)
        p_scr[s * rc : (s + 1) * rc, :] = (ADAPTER_SCALE * own).astype(jnp.bfloat16)
        out = keep_ref if s < ny else send_ref
        out[s % ny, :, hidden_width:] = jnp.concatenate([own.astype(jnp.bfloat16), zeros], axis=1)

    def body(step, carry):
        at = pl.ds(pl.multiple_of(step * tile, LANES), tile)
        fetch(step).wait()
        acc = fdot(w_scr[step], xt_scr[...], NN).T
        acc = (acc + fdot(p_scr[...], ad_ref[:, at], NN)).astype(jnp.bfloat16).reshape(n_t, rc, tile)
        keep_ref[:, :, at] = acc[:ny]
        send_ref[:, :, at] = acc[ny:]
        return carry

    lax.fori_loop(0, steps, body, 0)


def hidden_partial(meta, pieces, down_weight, b_down, a_down, n_t, own_t):
    n_dp = len(pieces)
    g, rc, width = pieces[0].shape
    ny = n_t // 2
    hidden_width = down_weight.shape[0]
    tile = tile_of(hidden_width, 512)
    low = TENANTS * R
    out = jax.ShapeDtypeStruct((ny, rc, hidden_width + LANES), jnp.bfloat16)
    return pl.pallas_call(
        functools.partial(hidden_kernel, (n_dp, n_t, g, own_t, rc, tile)),
        out_shape=(out, out),
        in_specs=[SMEM] + [VMEM] * n_dp + [ANY] + [VMEM] * 2,
        out_specs=[VMEM] * 2,
        scratch_shapes=[
            pltpu.VMEM((n_t, rc, width), jnp.bfloat16),
            pltpu.VMEM((width, n_t * rc), jnp.bfloat16),
            pltpu.VMEM((n_t * rc, low), jnp.bfloat16),
            pltpu.VMEM((hidden_width // tile, tile, width), jnp.bfloat16),
            pltpu.SemaphoreType.DMA((hidden_width // tile,)),
        ],
        compiler_params=pltpu.CompilerParams(vmem_limit_bytes=STREAM_LIMIT),
        cost_estimate=NO_COST,
        name="hidden_partial",
    )(meta, *pieces, down_weight, b_down, a_down)


def grads_of(total, factors):
    total = total.astype(jnp.float32)
    return [(total * factor[...].astype(jnp.float32)).astype(jnp.bfloat16) for factor in factors]


def input_kernel(sizes, meta, *refs):
    n_dp, n_t, g, own_t, rc, q, tile = sizes
    ny = n_t // 2
    factors, refs = [refs[2 * p : 2 * p + 2] for p in range(n_t)], refs[2 * n_t :]
    sums, (gw_ref, uw_ref, b_ref, a_ref) = refs[:2], refs[2:6]
    outs, (g_scr, u_scr, q_scr, w_scr, w_sem) = refs[6 : 6 + n_dp], refs[6 + n_dp :]
    z, t = meta[0], meta[1]
    y, c = t // 2, t % 2
    rows = n_t * rc
    width, hidden_width = gw_ref.shape
    steps = width // tile

    def fetch(f):
        at = pl.ds(pl.multiple_of(f * tile, LANES), tile)
        return [
            pltpu.make_async_copy(w.at[at], w_scr.at[f, k], w_sem.at[f, k]) for k, w in enumerate((gw_ref, uw_ref))
        ]

    for f in range(steps):
        for copy in fetch(f):
            copy.start()

    for p in range(n_t):
        owner = owner_of(p, y, c, ny)
        slot = lax.rem(owner // g + n_dp - z, n_dp) * g + owner % g
        mine = [factor[q * rc : (q + 1) * rc, :] for factor in factors[p]]
        g_scr[slot], u_scr[slot] = grads_of(sums[p % 2][owner // 2, :, :hidden_width], mine)
    q_gate = fdot(g_scr[...].reshape(rows, hidden_width), b_ref[...], NT)
    q_up = fdot(u_scr[...].reshape(rows, hidden_width), b_ref[...], NT)
    lane = lax.broadcasted_iota(jnp.int32, (rc, 2 * R * TENANTS), 1)
    shares = []
    for r in range(n_dp):
        share = []
        for j in range(g):
            at = slice((r * g + j) * rc, (r * g + j + 1) * rc)
            tenant = tenant_of(meta, lax.rem(z + r, n_dp) * g + j, own_t)
            mine = jnp.where(lane % (2 * R) < R, q_gate[at], q_up[at])
            mine = jnp.where(lane // (2 * R) == tenant, mine, 0.0)
            q_scr[at, :] = (ADAPTER_SCALE * mine).astype(jnp.bfloat16)
            share.append(sum(mine[:, e * 2 * R : (e + 1) * 2 * R] for e in range(TENANTS)))
        shares.append(jnp.concatenate(share, axis=0))
    share = jnp.concatenate(shares, axis=1).astype(jnp.bfloat16)
    for r in range(n_dp):
        outs[r][:, width:] = share

    def body(step, carry):
        at = pl.ds(pl.multiple_of(step * tile, LANES), tile)
        for copy in fetch(step):
            copy.wait()
        acc = fdot(g_scr[...].reshape(rows, hidden_width), w_scr[step, 0], NT)
        acc = acc + fdot(u_scr[...].reshape(rows, hidden_width), w_scr[step, 1], NT)
        acc = (acc + fdot(q_scr[...], a_ref[:, at], NN)).astype(jnp.bfloat16)
        for r in range(n_dp):
            outs[r][:, at] = acc[r * g * rc : (r + 1) * g * rc]
        return carry

    lax.fori_loop(0, steps, body, 0)


def input_partial(meta, factors, q, sums, gate_weight, up_weight, b_gu, a_gu, n_dp, own_t):
    n_t = len(factors)
    ny, rc, _ = sums[0].shape
    g = n_t // n_dp
    width, hidden_width = gate_weight.shape
    tile = tile_of(width, 256)
    low = 2 * R * TENANTS
    rows = n_t * rc
    outs = [jax.ShapeDtypeStruct((g * rc, width + n_dp * 2 * R), jnp.bfloat16)] * n_dp
    return pl.pallas_call(
        functools.partial(input_kernel, (n_dp, n_t, g, own_t, rc, q, tile)),
        out_shape=outs,
        in_specs=[SMEM] + [VMEM] * (2 * n_t + 2) + [ANY] * 2 + [VMEM] * 2,
        out_specs=[VMEM] * n_dp,
        scratch_shapes=[
            pltpu.VMEM((n_t, rc, hidden_width), jnp.bfloat16),
            pltpu.VMEM((n_t, rc, hidden_width), jnp.bfloat16),
            pltpu.VMEM((rows, low), jnp.bfloat16),
            pltpu.VMEM((width // tile, 2, tile, hidden_width), jnp.bfloat16),
            pltpu.SemaphoreType.DMA((width // tile, 2)),
        ],
        compiler_params=pltpu.CompilerParams(vmem_limit_bytes=STREAM_LIMIT),
        cost_estimate=NO_COST,
        name="input_partial",
    )(meta, *[x for pair in factors for x in pair], *sums, gate_weight, up_weight, b_gu, a_gu)


def acts_kernel(meta, acts_ref, out_ref):
    layers, n_t, _, own_t = out_ref.shape
    for owner in range(n_t):
        tenant = tenant_of(meta, owner, own_t)
        for layer in range(layers):
            mine = acts_ref[layer * R : (layer + 1) * R, owner * own_t : (owner + 1) * own_t]
            for e in range(TENANTS):
                chosen = jnp.where(tenant == e, mine.astype(jnp.float32), 0.0)
                out_ref[layer, owner, e * R : (e + 1) * R, :] = chosen.astype(jnp.bfloat16)


def masked_acts(meta, acts, n_t):
    return pl.pallas_call(
        acts_kernel,
        out_shape=jax.ShapeDtypeStruct((3, n_t, TENANTS * R, acts.shape[1] // n_t), jnp.bfloat16),
        in_specs=[SMEM, VMEM],
        out_specs=VMEM,
        compiler_params=pltpu.CompilerParams(vmem_limit_bytes=VMEM_LIMIT),
        cost_estimate=NO_COST,
        name="masked_acts",
    )(meta, acts)


def left_of(left_ref, layer, owners):
    return jnp.concatenate([left_ref[layer, owner] for owner in owners], axis=1)


def down_outer_kernel(n_dp, g, chunks, meta, *refs):
    pieces, (left_ref, out_ref) = refs[: n_dp * chunks], refs[n_dp * chunks :]
    owners = [lax.rem(meta[0] + (n_dp - k), n_dp) * g + j for k in range(n_dp) for j in range(g)]
    right = [pieces[q * n_dp + k][j] for k in range(n_dp) for j in range(g) for q in range(chunks)]
    out = ADAPTER_SCALE * fdot(left_of(left_ref, 2, owners), jnp.concatenate(right, axis=0), NN)
    out_ref[...] = out.reshape(out_ref.shape)


def down_outer(meta, grads, left):
    n_dp, chunks = len(grads[0]), len(grads)
    pieces = [piece for pieces in grads for piece in pieces]
    g, _, width = pieces[0].shape
    tile = tile_of(width, 512)
    return pl.pallas_call(
        functools.partial(down_outer_kernel, n_dp, g, chunks),
        out_shape=jax.ShapeDtypeStruct((TENANTS, R, width), jnp.float32),
        grid_spec=pltpu.PrefetchScalarGridSpec(
            num_scalar_prefetch=1,
            grid=(width // tile,),
            in_specs=[
                pl.BlockSpec(piece.shape[:2] + (tile,), lambda f, *_: (0, 0, f)) for piece in pieces
            ]
            + [whole(left.shape)],
            out_specs=pl.BlockSpec((TENANTS, R, tile), lambda f, *_: (0, 0, f)),
        ),
        compiler_params=pltpu.CompilerParams(vmem_limit_bytes=VMEM_LIMIT),
        cost_estimate=NO_COST,
        name="down_outer",
    )(meta, *pieces, left)


def gate_up_outer_kernel(n_t, chunks, meta, *refs):
    ny = n_t // 2
    factors, refs = [refs[2 * p : 2 * p + 2] for p in range(n_t)], refs[2 * n_t :]
    sums, (left_ref, out_ref) = [refs[2 * q : 2 * q + 2] for q in range(chunks)], refs[2 * chunks :]
    y, c = meta[1] // 2, meta[1] % 2
    owners = [owner_of(p, y, c, ny) for p in range(n_t)]
    grads = []
    for p in range(n_t):
        total = jnp.concatenate([both[p % 2][owners[p] // 2] for both in sums], axis=0)
        grads.append(grads_of(total, factors[p]))
    for layer in range(2):
        right = jnp.concatenate([grad[layer] for grad in grads], axis=0)
        out = ADAPTER_SCALE * fdot(left_of(left_ref, layer, owners), right, NN)
        out_ref[:, layer * R : (layer + 1) * R, :] = out.reshape(TENANTS, R, out.shape[1])


def gate_up_outer(meta, factors, sums, left):
    n_t, chunks = len(factors), len(sums)
    rc = sums[0][0].shape[1]
    own_t, width = factors[0][0].shape
    tile = tile_of(width, 896)
    return pl.pallas_call(
        functools.partial(gate_up_outer_kernel, n_t, chunks),
        out_shape=jax.ShapeDtypeStruct((TENANTS, 2 * R, width), jnp.float32),
        grid_spec=pltpu.PrefetchScalarGridSpec(
            num_scalar_prefetch=1,
            grid=(width // tile,),
            in_specs=[pl.BlockSpec((own_t, tile), lambda f, *_: (0, f))] * (2 * n_t)
            + [pl.BlockSpec((n_t // 2, rc, tile), lambda f, *_: (0, 0, f))] * (2 * chunks)
            + [whole(left.shape)],
            out_specs=pl.BlockSpec((TENANTS, 2 * R, tile), lambda f, *_: (0, 0, f)),
        ),
        compiler_params=pltpu.CompilerParams(vmem_limit_bytes=2 * VMEM_LIMIT),
        cost_estimate=NO_COST,
        name="gate_up_outer",
    )(meta, *[x for pair in factors for x in pair], *[x for both in sums for x in both], left)


def down_part_kernel(chunks, meta, *refs):
    sums, (hidden_ref, out_ref) = refs[:chunks], refs[chunks:]
    width = hidden_ref.shape[1]
    low = jnp.concatenate([both[meta[1] // 2][:, width:] for both in sums], axis=0)
    part = fdot(low, hidden_ref[...], TN)
    out_ref[...] = sum(part[e * R : (e + 1) * R] for e in range(TENANTS)).astype(jnp.bfloat16)


def down_part(meta, sums, hidden):
    return pl.pallas_call(
        functools.partial(down_part_kernel, len(sums)),
        out_shape=jax.ShapeDtypeStruct((R, hidden.shape[1]), jnp.bfloat16),
        in_specs=[SMEM] + [VMEM] * (len(sums) + 1),
        out_specs=VMEM,
        compiler_params=pltpu.CompilerParams(vmem_limit_bytes=VMEM_LIMIT),
        cost_estimate=NO_COST,
        name="down_part",
    )(meta, *sums, hidden)


def spread_kernel(tenant_at, rows, meta, *refs):
    parts, out_ref = refs[:-1], refs[-1]
    out_ref[...] = jnp.zeros_like(out_ref)
    at = 0
    for part in parts:
        for k in range(part.shape[0] // rows):
            tenant = tenant_at(at, meta)
            term = part[k * rows : (k + 1) * rows].astype(jnp.float32)
            out_ref[tenant] = out_ref[tenant] + ADAPTER_SCALE * term
            at += 1


def spread(meta, parts, tenant_at, rows, name):
    width = parts[0].shape[1]
    out = jax.ShapeDtypeStruct((TENANTS, rows, width), jnp.float32)
    tile = tile_of(width, 1024)
    return pl.pallas_call(
        functools.partial(spread_kernel, tenant_at, rows),
        out_shape=out,
        grid_spec=pltpu.PrefetchScalarGridSpec(
            num_scalar_prefetch=1,
            grid=(width // tile,),
            in_specs=[pl.BlockSpec((part.shape[0], tile), lambda f, *_: (0, f)) for part in parts],
            out_specs=pl.BlockSpec((TENANTS, rows, tile), lambda f, *_: (0, 0, f)),
        ),
        compiler_params=pltpu.CompilerParams(vmem_limit_bytes=VMEM_LIMIT),
        cost_estimate=NO_COST,
        name=name,
    )(meta, *parts)


def in_outer_kernel(n_dp, chunks, g, meta, *refs):
    shares, inputs, out_ref = refs[: n_dp * chunks], refs[n_dp * chunks : -1], refs[-1]
    out_ref[...] = jnp.zeros_like(out_ref)
    rows, width = inputs[0].shape
    own_t = rows // g
    rc = own_t // chunks
    for k in range(n_dp):
        block = lax.rem(meta[0] + n_dp - k, n_dp)
        queries = []
        for q in range(chunks):
            query = 0.0
            for s in range(n_dp):
                at = width + (s + n_dp - k) % n_dp * 2 * R
                query = query + shares[q * n_dp + s][:, at : at + 2 * R].astype(jnp.float32)
            queries.append(query.astype(jnp.bfloat16))
        low = [queries[q][j * rc : (j + 1) * rc] for j in range(g) for q in range(chunks)]
        total = fdot(jnp.concatenate(low, axis=0), inputs[k][...], TN)
        tenant = meta[2 + block]
        out_ref[tenant] = out_ref[tenant] + ADAPTER_SCALE * total


def in_outer(meta, shares, inputs, g):
    n_dp, width = len(inputs), inputs[0].shape[1]
    chunks = len(shares)
    shares = [share for there in shares for share in there]
    return pl.pallas_call(
        functools.partial(in_outer_kernel, n_dp, chunks, g),
        out_shape=jax.ShapeDtypeStruct((TENANTS, 2 * R, width), jnp.float32),
        in_specs=[SMEM] + [VMEM] * (len(shares) + n_dp),
        out_specs=VMEM,
        compiler_params=pltpu.CompilerParams(vmem_limit_bytes=VMEM_LIMIT),
        cost_estimate=NO_COST,
        name="in_outer",
    )(meta, *shares, *inputs)


def ring(n, by):
    return [(k, (k + by) % n) for k in range(n)]


def add32(*terms):
    return sum(term.astype(jnp.float32) for term in terms)


def after(value, *done):
    return lax.optimization_barrier((value,) + done)[0]


def per_device(
    layer_input,
    out_grad,
    gate_pre,
    up_pre,
    adapter_acts,
    gate_weight,
    up_weight,
    down_weight,
    adapter_a_gu,
    adapter_b_gu,
    adapter_a_down,
    adapter_b_down,
    block_tenant,
):
    n_dp, n_t = lax.axis_size("dp"), lax.axis_size("tensor")
    ny = n_t // 2
    z, t = lax.axis_index("dp"), lax.axis_index("tensor")
    own_rows, width = out_grad.shape
    own_t, hidden_width = gate_pre.shape
    tokens = adapter_acts.shape[0]
    g = own_rows // own_t
    assert own_rows == BLOCK and g * own_t == own_rows and n_t == 2 * ny and n_t == g * n_dp
    chunks, at = [], 0
    for share in SHARES:
        chunks.append((at, own_t * share // sum(SHARES)))
        at += chunks[-1][1]

    meta = jnp.concatenate([jnp.stack([z, t]).astype(jnp.int32), block_tenant])
    b_down = adapter_b_down.reshape(TENANTS * R, width)
    a_down = jnp.transpose(adapter_a_down, (0, 2, 1)).reshape(TENANTS * R, hidden_width)
    b_gu = adapter_b_gu.reshape(TENANTS * 2 * R, hidden_width)
    a_gu = jnp.transpose(adapter_a_gu, (0, 2, 1)).reshape(TENANTS * 2 * R, width)

    pair = [(k, k ^ 1) for k in range(n_t)]
    z_next = ring(n_dp, 1)

    stored = [gate_pre, up_pre]
    far_stored = [[lax.ppermute(x, "tensor", ring(n_t, 2 * s)) for x in stored] for s in range(1, ny)]
    grads = [[out_grad.reshape(g, own_t, width)[:, at : at + rc]] for at, rc in chunks]
    for _ in range(n_dp - 1):
        grads[0].append(lax.ppermute(grads[0][-1], "dp", z_next))
    grads[1][0] = after(grads[1][0], grads[0][2])
    for _ in range(n_dp - 2):
        grads[1].append(lax.ppermute(grads[1][-1], "dp", z_next))

    def first(q, done):
        pieces = [after(grads[q][0], *done)] + grads[q][1:]
        keep, send = hidden_partial(meta, pieces, down_weight, b_down, a_down, n_t, own_t)
        return keep, send

    def factors_of(stored):
        gate_value, up_value = [x.astype(jnp.float32) for x in stored]
        sigmoid_value = jax.nn.sigmoid(gate_value)
        dgate = up_value * sigmoid_value * (1.0 + gate_value * (1.0 - sigmoid_value))
        dup = gate_value * sigmoid_value
        return [x.astype(jnp.bfloat16) for x in (dgate, dup, dup * up_value)]

    def exchange(keep, other):
        mine = add32(keep, other).astype(jnp.bfloat16)
        return mine, [lax.ppermute(mine, "tensor", ring(n_t, 2 * s)) for s in range(1, ny)]

    def total(mine, far):
        both = add32(mine, *far).astype(jnp.bfloat16)
        return [both, lax.ppermute(both, "tensor", pair)]

    def second(q, sums, done):
        sums = [after(sums[0], *done), sums[1]]
        outs = input_partial(meta, factors, q, sums, gate_weight, up_weight, b_gu, a_gu, n_dp, own_t)
        return [outs[0]] + [lax.ppermute(outs[r], "dp", ring(n_dp, r)) for r in range(1, n_dp)]

    def finish(there, rc):
        return add32(*[x[:, :width] for x in there]).astype(jnp.bfloat16).reshape(g, rc, width)

    keep_a, send_a = first(0, (grads[1][1],))
    stored[0] = after(stored[0], keep_a)
    beside_stored = [lax.ppermute(x, "tensor", pair) for x in stored]
    *near, hidden = factors_of(stored)
    other_a = lax.ppermute(after(send_a, *[x for there in far_stored for x in there]), "tensor", pair)
    mine_a, far_a = exchange(after(keep_a, near[0]), other_a)
    grads[1].append(lax.ppermute(after(grads[1][-1], mine_a), "dp", z_next))
    keep_b, send_b = first(1, (mine_a,))
    other_b = lax.ppermute(send_b, "tensor", pair)
    mine_b, far_b = exchange(keep_b, other_b)
    beside_stored[0] = after(beside_stored[0], keep_b)
    factors = [near, factors_of(beside_stored)[:2]]
    for there in far_stored:
        beside = [lax.ppermute(x, "tensor", pair) for x in (after(there[0], mine_a), there[1])]
        for both in (there, beside):
            factors.append(factors_of([after(both[0], keep_b), both[1]])[:2])
    inputs = [layer_input, lax.ppermute(after(layer_input, grads[1][-1]), "dp", z_next)]
    inputs.append(lax.ppermute(after(inputs[-1], mine_b), "dp", z_next))
    sums_a = total(after(mine_a, mine_b, inputs[1], *[pair[0] for pair in factors]), far_a)
    there_a = second(0, sums_a, ())
    for step in range(n_dp - 3):
        inputs.append(lax.ppermute(after(inputs[-1], there_a[0]), "dp", z_next))
    sums_b = total(after(mine_b, there_a[0], inputs[2]), far_b)
    there_b = second(1, sums_b, ())

    half_a = finish([after(x, there_b[0], inputs[-1]) for x in there_a], chunks[0][1])
    acts = masked_acts(meta, after(adapter_acts.T, half_a), n_t)
    grad_b_down = down_outer(meta, grads, acts)
    a_part = down_part(meta, [sums_a[0], after(sums_b[0], half_a)], hidden)
    a_parts = [a_part] + [lax.ppermute(a_part, "tensor", ring(n_t, 2 * s)) for s in range(1, ny)]
    a_parts = [after(x, grad_b_down) for x in a_parts]
    a_parts += [lax.ppermute(x, "tensor", pair) for x in a_parts]
    grad_b_gu = gate_up_outer(meta, factors, [sums_a, sums_b], after(acts, grad_b_down))

    def column_tenant(p, m):
        owner = lax.rem(m[1] // 2 + ny - p % ny, ny) * 2
        return tenant_of(m, owner + (m[1] % 2 if p < ny else 1 - m[1] % 2), own_t)

    a_parts[0] = after(a_parts[0], grad_b_gu)
    grad_a_down = spread(meta, a_parts, column_tenant, R, "spread_a_down")
    there_b[0] = after(there_b[0], grad_a_down)
    grad_a_gu = in_outer(meta, [there_a, there_b], inputs, g)
    half_b = finish(there_b, chunks[1][1])
    block_input_grad = jnp.concatenate([half_a, half_b], axis=1).reshape(own_rows, width)
    return (
        block_input_grad,
        grad_a_gu.transpose(0, 2, 1),
        grad_b_gu,
        grad_a_down.transpose(0, 2, 1),
        grad_b_down,
    )


def solution(mesh):
    placed = (
        P(("groups", "dp"), "tensor"),
        P(("groups", "dp"), "tensor"),
        P(("groups", "tensor"), "dp"),
        P(("groups", "tensor"), "dp"),
        P("groups", None),
        P("tensor", "dp"),
        P("tensor", "dp"),
        P("dp", "tensor"),
        P(None, "tensor", None),
        P(None, None, "dp"),
        P(None, "dp", None),
        P(None, None, "tensor"),
        P("groups"),
    )
    return jax.shard_map(
        per_device,
        mesh=mesh,
        in_specs=placed,
        out_specs=(
            P(("groups", "dp"), "tensor"),
            P("groups", "tensor", None),
            P("groups", None, "dp"),
            P("groups", "dp", None),
            P("groups", None, "tensor"),
        ),
        check_vma=False,
    )
```

```python
import functools

import jax
import jax.numpy as jnp
from jax import lax
from jax.experimental import pallas as pl
from jax.experimental.pallas import tpu as pltpu
from jax.sharding import PartitionSpec as P

R = 16
TENANTS = 4
BLOCK = 128
SHARES = (1, 1)
LANES = 128
VMEM_LIMIT = 12 * 1024 * 1024
STREAM_LIMIT = 50 * 1024 * 1024

ADAPTER_SCALE = 2.0

NT = (((1,), (1,)), ((), ()))
NN = (((1,), (0,)), ((), ()))
TN = (((0,), (0,)), ((), ()))
ANY = pl.BlockSpec(memory_space=pl.ANY)
SMEM = pl.BlockSpec(memory_space=pltpu.SMEM)
VMEM = pl.BlockSpec(memory_space=pltpu.VMEM)
NO_COST = pl.CostEstimate(flops=1, bytes_accessed=1, transcendentals=0)


def fdot(lhs, rhs, dims):
    return lax.dot_general(lhs, rhs, dims, preferred_element_type=jnp.float32)


def tile_of(width, most):
    tile = most
    while width % tile:
        tile -= LANES
    return tile


def whole(shape):
    return pl.BlockSpec(shape, lambda *_: (0,) * len(shape))


def tenant_of(meta, owner, own_t):
    return meta[2 + (owner * own_t) // BLOCK]


def owner_of(p, y, c, ny):
    return lax.rem(y + ny - p // 2, ny) * 2 + (c if p % 2 == 0 else 1 - c)


def hidden_kernel(sizes, meta, *refs):
    n_dp, n_t, g, own_t, rc, tile = sizes
    ny = n_t // 2
    pieces, (w_ref, bd_ref, ad_ref, keep_ref, send_ref), refs = refs[:n_dp], refs[n_dp : n_dp + 5], refs[n_dp + 5 :]
    x_scr, p_scr, w_scr, w_sem = refs
    z, t = meta[0], meta[1]
    y, c = t // 2, t % 2
    hidden_width, width = w_ref.shape
    steps = hidden_width // tile

    def fetch(f):
        rows = pl.ds(pl.multiple_of(f * tile, LANES), tile)
        return pltpu.make_async_copy(w_ref.at[rows], w_scr.at[f], w_sem.at[f])

    for f in range(steps):
        fetch(f).start()

    for k in range(n_dp):
        for j in range(g):
            owner = lax.rem(z + (n_dp - k), n_dp) * g + j
            away = jnp.where(owner % 2 == c, 0, ny)
            x_scr[away + owner // 2] = pieces[k][j]
    proj = fdot(x_scr[...].reshape(n_t * rc, width), bd_ref[...], NT)
    lane = lax.broadcasted_iota(jnp.int32, (rc, TENANTS * R), 1) // R
    zeros = jnp.zeros((rc, LANES - TENANTS * R), jnp.bfloat16)
    for s in range(n_t):
        owner = (s % ny) * 2 + (c if s < ny else 1 - c)
        own = jnp.where(lane == tenant_of(meta, owner, own_t), proj[s * rc : (s + 1) * rc], 0.0)
        p_scr[s * rc : (s + 1) * rc, :] = (ADAPTER_SCALE * own).astype(jnp.bfloat16)
        out = keep_ref if s < ny else send_ref
        out[s % ny, :, hidden_width:] = jnp.concatenate([own.astype(jnp.bfloat16), zeros], axis=1)

    def body(step, carry):
        at = pl.ds(pl.multiple_of(step * tile, LANES), tile)
        fetch(step).wait()
        acc = fdot(x_scr[...].reshape(n_t * rc, width), w_scr[step], NT)
        acc = (acc + fdot(p_scr[...], ad_ref[:, at], NN)).astype(jnp.bfloat16).reshape(n_t, rc, tile)
        keep_ref[:, :, at] = acc[:ny]
        send_ref[:, :, at] = acc[ny:]
        return carry

    lax.fori_loop(0, steps, body, 0)


def hidden_partial(meta, pieces, down_weight, b_down, a_down, n_t, own_t):
    n_dp = len(pieces)
    g, rc, width = pieces[0].shape
    ny = n_t // 2
    hidden_width = down_weight.shape[0]
    tile = tile_of(hidden_width, 512)
    low = TENANTS * R
    out = jax.ShapeDtypeStruct((ny, rc, hidden_width + LANES), jnp.bfloat16)
    return pl.pallas_call(
        functools.partial(hidden_kernel, (n_dp, n_t, g, own_t, rc, tile)),
        out_shape=(out, out),
        in_specs=[SMEM] + [VMEM] * n_dp + [ANY] + [VMEM] * 2,
        out_specs=[VMEM] * 2,
        scratch_shapes=[
            pltpu.VMEM((n_t, rc, width), jnp.bfloat16),
            pltpu.VMEM((n_t * rc, low), jnp.bfloat16),
            pltpu.VMEM((hidden_width // tile, tile, width), jnp.bfloat16),
            pltpu.SemaphoreType.DMA((hidden_width // tile,)),
        ],
        compiler_params=pltpu.CompilerParams(vmem_limit_bytes=STREAM_LIMIT),
        cost_estimate=NO_COST,
        name="hidden_partial",
    )(meta, *pieces, down_weight, b_down, a_down)


def grads_of(total, factors):
    total = total.astype(jnp.float32)
    return [(total * factor[...].astype(jnp.float32)).astype(jnp.bfloat16) for factor in factors]


def input_kernel(sizes, meta, *refs):
    n_dp, n_t, g, own_t, rc, q, tile = sizes
    ny = n_t // 2
    factors, refs = [refs[2 * p : 2 * p + 2] for p in range(n_t)], refs[2 * n_t :]
    sums, (gw_ref, uw_ref, b_ref, a_ref) = refs[:2], refs[2:6]
    outs, (g_scr, u_scr, q_scr, w_scr, w_sem) = refs[6 : 6 + n_dp], refs[6 + n_dp :]
    z, t = meta[0], meta[1]
    y, c = t // 2, t % 2
    rows = n_t * rc
    width, hidden_width = gw_ref.shape
    steps = width // tile

    def fetch(f):
        at = pl.ds(pl.multiple_of(f * tile, LANES), tile)
        return [
            pltpu.make_async_copy(w.at[at], w_scr.at[f, k], w_sem.at[f, k]) for k, w in enumerate((gw_ref, uw_ref))
        ]

    for f in range(steps):
        for copy in fetch(f):
            copy.start()

    for p in range(n_t):
        owner = owner_of(p, y, c, ny)
        slot = lax.rem(owner // g + n_dp - z, n_dp) * g + owner % g
        mine = [factor[q * rc : (q + 1) * rc, :] for factor in factors[p]]
        g_scr[slot], u_scr[slot] = grads_of(sums[p % 2][owner // 2, :, :hidden_width], mine)
    q_gate = fdot(g_scr[...].reshape(rows, hidden_width), b_ref[...], NT)
    q_up = fdot(u_scr[...].reshape(rows, hidden_width), b_ref[...], NT)
    lane = lax.broadcasted_iota(jnp.int32, (rc, 2 * R * TENANTS), 1)
    shares = []
    for r in range(n_dp):
        share = []
        for j in range(g):
            at = slice((r * g + j) * rc, (r * g + j + 1) * rc)
            tenant = tenant_of(meta, lax.rem(z + r, n_dp) * g + j, own_t)
            mine = jnp.where(lane % (2 * R) < R, q_gate[at], q_up[at])
            mine = jnp.where(lane // (2 * R) == tenant, mine, 0.0)
            q_scr[at, :] = (ADAPTER_SCALE * mine).astype(jnp.bfloat16)
            share.append(sum(mine[:, e * 2 * R : (e + 1) * 2 * R] for e in range(TENANTS)))
        shares.append(jnp.concatenate(share, axis=0))
    share = jnp.concatenate(shares, axis=1).astype(jnp.bfloat16)
    for r in range(n_dp):
        outs[r][:, width:] = share

    def body(step, carry):
        at = pl.ds(pl.multiple_of(step * tile, LANES), tile)
        for copy in fetch(step):
            copy.wait()
        acc = fdot(g_scr[...].reshape(rows, hidden_width), w_scr[step, 0], NT)
        acc = acc + fdot(u_scr[...].reshape(rows, hidden_width), w_scr[step, 1], NT)
        acc = (acc + fdot(q_scr[...], a_ref[:, at], NN)).astype(jnp.bfloat16)
        for r in range(n_dp):
            outs[r][:, at] = acc[r * g * rc : (r + 1) * g * rc]
        return carry

    lax.fori_loop(0, steps, body, 0)


def input_partial(meta, factors, q, sums, gate_weight, up_weight, b_gu, a_gu, n_dp, own_t):
    n_t = len(factors)
    ny, rc, _ = sums[0].shape
    g = n_t // n_dp
    width, hidden_width = gate_weight.shape
    tile = tile_of(width, 256)
    low = 2 * R * TENANTS
    rows = n_t * rc
    outs = [jax.ShapeDtypeStruct((g * rc, width + n_dp * 2 * R), jnp.bfloat16)] * n_dp
    return pl.pallas_call(
        functools.partial(input_kernel, (n_dp, n_t, g, own_t, rc, q, tile)),
        out_shape=outs,
        in_specs=[SMEM] + [VMEM] * (2 * n_t + 2) + [ANY] * 2 + [VMEM] * 2,
        out_specs=[VMEM] * n_dp,
        scratch_shapes=[
            pltpu.VMEM((n_t, rc, hidden_width), jnp.bfloat16),
            pltpu.VMEM((n_t, rc, hidden_width), jnp.bfloat16),
            pltpu.VMEM((rows, low), jnp.bfloat16),
            pltpu.VMEM((width // tile, 2, tile, hidden_width), jnp.bfloat16),
            pltpu.SemaphoreType.DMA((width // tile, 2)),
        ],
        compiler_params=pltpu.CompilerParams(vmem_limit_bytes=STREAM_LIMIT),
        cost_estimate=NO_COST,
        name="input_partial",
    )(meta, *[x for pair in factors for x in pair], *sums, gate_weight, up_weight, b_gu, a_gu)


def acts_kernel(meta, acts_ref, out_ref):
    layers, n_t, _, own_t = out_ref.shape
    for owner in range(n_t):
        tenant = tenant_of(meta, owner, own_t)
        for layer in range(layers):
            mine = acts_ref[layer * R : (layer + 1) * R, owner * own_t : (owner + 1) * own_t]
            for e in range(TENANTS):
                chosen = jnp.where(tenant == e, mine.astype(jnp.float32), 0.0)
                out_ref[layer, owner, e * R : (e + 1) * R, :] = chosen.astype(jnp.bfloat16)


def masked_acts(meta, acts, n_t):
    return pl.pallas_call(
        acts_kernel,
        out_shape=jax.ShapeDtypeStruct((3, n_t, TENANTS * R, acts.shape[1] // n_t), jnp.bfloat16),
        in_specs=[SMEM, VMEM],
        out_specs=VMEM,
        compiler_params=pltpu.CompilerParams(vmem_limit_bytes=VMEM_LIMIT),
        cost_estimate=NO_COST,
        name="masked_acts",
    )(meta, acts)


def left_of(left_ref, layer, owners):
    return jnp.concatenate([left_ref[layer, owner] for owner in owners], axis=1)


def down_outer_kernel(n_dp, g, chunks, meta, *refs):
    pieces, (left_ref, out_ref) = refs[: n_dp * chunks], refs[n_dp * chunks :]
    owners = [lax.rem(meta[0] + (n_dp - k), n_dp) * g + j for k in range(n_dp) for j in range(g)]
    right = [pieces[q * n_dp + k][j] for k in range(n_dp) for j in range(g) for q in range(chunks)]
    out = ADAPTER_SCALE * fdot(left_of(left_ref, 2, owners), jnp.concatenate(right, axis=0), NN)
    out_ref[...] = out.reshape(out_ref.shape)


def down_outer(meta, grads, left):
    n_dp, chunks = len(grads[0]), len(grads)
    pieces = [piece for pieces in grads for piece in pieces]
    g, _, width = pieces[0].shape
    tile = tile_of(width, 512)
    return pl.pallas_call(
        functools.partial(down_outer_kernel, n_dp, g, chunks),
        out_shape=jax.ShapeDtypeStruct((TENANTS, R, width), jnp.float32),
        grid_spec=pltpu.PrefetchScalarGridSpec(
            num_scalar_prefetch=1,
            grid=(width // tile,),
            in_specs=[
                pl.BlockSpec(piece.shape[:2] + (tile,), lambda f, *_: (0, 0, f)) for piece in pieces
            ]
            + [whole(left.shape)],
            out_specs=pl.BlockSpec((TENANTS, R, tile), lambda f, *_: (0, 0, f)),
        ),
        compiler_params=pltpu.CompilerParams(vmem_limit_bytes=VMEM_LIMIT),
        cost_estimate=NO_COST,
        name="down_outer",
    )(meta, *pieces, left)


def gate_up_outer_kernel(n_t, chunks, meta, *refs):
    ny = n_t // 2
    factors, refs = [refs[2 * p : 2 * p + 2] for p in range(n_t)], refs[2 * n_t :]
    sums, (left_ref, out_ref) = [refs[2 * q : 2 * q + 2] for q in range(chunks)], refs[2 * chunks :]
    y, c = meta[1] // 2, meta[1] % 2
    owners = [owner_of(p, y, c, ny) for p in range(n_t)]
    grads = []
    for p in range(n_t):
        total = jnp.concatenate([both[p % 2][owners[p] // 2] for both in sums], axis=0)
        grads.append(grads_of(total, factors[p]))
    for layer in range(2):
        right = jnp.concatenate([grad[layer] for grad in grads], axis=0)
        out = ADAPTER_SCALE * fdot(left_of(left_ref, layer, owners), right, NN)
        out_ref[:, layer * R : (layer + 1) * R, :] = out.reshape(TENANTS, R, out.shape[1])


def gate_up_outer(meta, factors, sums, left):
    n_t, chunks = len(factors), len(sums)
    rc = sums[0][0].shape[1]
    own_t, width = factors[0][0].shape
    tile = tile_of(width, 896)
    return pl.pallas_call(
        functools.partial(gate_up_outer_kernel, n_t, chunks),
        out_shape=jax.ShapeDtypeStruct((TENANTS, 2 * R, width), jnp.float32),
        grid_spec=pltpu.PrefetchScalarGridSpec(
            num_scalar_prefetch=1,
            grid=(width // tile,),
            in_specs=[pl.BlockSpec((own_t, tile), lambda f, *_: (0, f))] * (2 * n_t)
            + [pl.BlockSpec((n_t // 2, rc, tile), lambda f, *_: (0, 0, f))] * (2 * chunks)
            + [whole(left.shape)],
            out_specs=pl.BlockSpec((TENANTS, 2 * R, tile), lambda f, *_: (0, 0, f)),
        ),
        compiler_params=pltpu.CompilerParams(vmem_limit_bytes=2 * VMEM_LIMIT),
        cost_estimate=NO_COST,
        name="gate_up_outer",
    )(meta, *[x for pair in factors for x in pair], *[x for both in sums for x in both], left)


def down_part_kernel(chunks, meta, *refs):
    sums, (hidden_ref, out_ref) = refs[:chunks], refs[chunks:]
    width = hidden_ref.shape[1]
    low = jnp.concatenate([both[meta[1] // 2][:, width:] for both in sums], axis=0)
    part = fdot(low, hidden_ref[...], TN)
    out_ref[...] = sum(part[e * R : (e + 1) * R] for e in range(TENANTS)).astype(jnp.bfloat16)


def down_part(meta, sums, hidden):
    return pl.pallas_call(
        functools.partial(down_part_kernel, len(sums)),
        out_shape=jax.ShapeDtypeStruct((R, hidden.shape[1]), jnp.bfloat16),
        in_specs=[SMEM] + [VMEM] * (len(sums) + 1),
        out_specs=VMEM,
        compiler_params=pltpu.CompilerParams(vmem_limit_bytes=VMEM_LIMIT),
        cost_estimate=NO_COST,
        name="down_part",
    )(meta, *sums, hidden)


def spread_kernel(tenant_at, rows, meta, *refs):
    parts, out_ref = refs[:-1], refs[-1]
    out_ref[...] = jnp.zeros_like(out_ref)
    at = 0
    for part in parts:
        for k in range(part.shape[0] // rows):
            tenant = tenant_at(at, meta)
            term = part[k * rows : (k + 1) * rows].astype(jnp.float32)
            out_ref[tenant] = out_ref[tenant] + ADAPTER_SCALE * term
            at += 1


def spread(meta, parts, tenant_at, rows, name):
    width = parts[0].shape[1]
    out = jax.ShapeDtypeStruct((TENANTS, rows, width), jnp.float32)
    tile = tile_of(width, 1024)
    return pl.pallas_call(
        functools.partial(spread_kernel, tenant_at, rows),
        out_shape=out,
        grid_spec=pltpu.PrefetchScalarGridSpec(
            num_scalar_prefetch=1,
            grid=(width // tile,),
            in_specs=[pl.BlockSpec((part.shape[0], tile), lambda f, *_: (0, f)) for part in parts],
            out_specs=pl.BlockSpec((TENANTS, rows, tile), lambda f, *_: (0, 0, f)),
        ),
        compiler_params=pltpu.CompilerParams(vmem_limit_bytes=VMEM_LIMIT),
        cost_estimate=NO_COST,
        name=name,
    )(meta, *parts)


def in_outer_kernel(n_dp, chunks, g, meta, *refs):
    shares, inputs, out_ref = refs[: n_dp * chunks], refs[n_dp * chunks : -1], refs[-1]
    out_ref[...] = jnp.zeros_like(out_ref)
    rows, width = inputs[0].shape
    own_t = rows // g
    rc = own_t // chunks
    for k in range(n_dp):
        block = lax.rem(meta[0] + n_dp - k, n_dp)
        queries = []
        for q in range(chunks):
            query = 0.0
            for s in range(n_dp):
                at = width + (s + n_dp - k) % n_dp * 2 * R
                query = query + shares[q * n_dp + s][:, at : at + 2 * R].astype(jnp.float32)
            queries.append(query.astype(jnp.bfloat16))
        low = [queries[q][j * rc : (j + 1) * rc] for j in range(g) for q in range(chunks)]
        total = fdot(jnp.concatenate(low, axis=0), inputs[k][...], TN)
        tenant = meta[2 + block]
        out_ref[tenant] = out_ref[tenant] + ADAPTER_SCALE * total


def in_outer(meta, shares, inputs, g):
    n_dp, width = len(inputs), inputs[0].shape[1]
    chunks = len(shares)
    shares = [share for there in shares for share in there]
    return pl.pallas_call(
        functools.partial(in_outer_kernel, n_dp, chunks, g),
        out_shape=jax.ShapeDtypeStruct((TENANTS, 2 * R, width), jnp.float32),
        in_specs=[SMEM] + [VMEM] * (len(shares) + n_dp),
        out_specs=VMEM,
        compiler_params=pltpu.CompilerParams(vmem_limit_bytes=VMEM_LIMIT),
        cost_estimate=NO_COST,
        name="in_outer",
    )(meta, *shares, *inputs)


def ring(n, by):
    return [(k, (k + by) % n) for k in range(n)]


def add32(*terms):
    return sum(term.astype(jnp.float32) for term in terms)


def after(value, *done):
    return lax.optimization_barrier((value,) + done)[0]


def per_device(
    layer_input,
    out_grad,
    gate_pre,
    up_pre,
    adapter_acts,
    gate_weight,
    up_weight,
    down_weight,
    adapter_a_gu,
    adapter_b_gu,
    adapter_a_down,
    adapter_b_down,
    block_tenant,
):
    n_dp, n_t = lax.axis_size("dp"), lax.axis_size("tensor")
    ny = n_t // 2
    z, t = lax.axis_index("dp"), lax.axis_index("tensor")
    own_rows, width = out_grad.shape
    own_t, hidden_width = gate_pre.shape
    tokens = adapter_acts.shape[0]
    g = own_rows // own_t
    assert own_rows == BLOCK and g * own_t == own_rows and n_t == 2 * ny and n_t == g * n_dp
    chunks, at = [], 0
    for share in SHARES:
        chunks.append((at, own_t * share // sum(SHARES)))
        at += chunks[-1][1]

    meta = jnp.concatenate([jnp.stack([z, t]).astype(jnp.int32), block_tenant])
    b_down = adapter_b_down.reshape(TENANTS * R, width)
    a_down = jnp.transpose(adapter_a_down, (0, 2, 1)).reshape(TENANTS * R, hidden_width)
    b_gu = adapter_b_gu.reshape(TENANTS * 2 * R, hidden_width)
    a_gu = jnp.transpose(adapter_a_gu, (0, 2, 1)).reshape(TENANTS * 2 * R, width)

    pair = [(k, k ^ 1) for k in range(n_t)]
    z_next = ring(n_dp, 1)

    stored = [gate_pre, up_pre]
    far_stored = [[lax.ppermute(x, "tensor", ring(n_t, 2 * s)) for x in stored] for s in range(1, ny)]
    grads = [[out_grad.reshape(g, own_t, width)[:, at : at + rc]] for at, rc in chunks]
    for _ in range(n_dp - 1):
        grads[0].append(lax.ppermute(grads[0][-1], "dp", z_next))
    grads[1][0] = after(grads[1][0], grads[0][2])
    for _ in range(n_dp - 1):
        grads[1].append(lax.ppermute(grads[1][-1], "dp", z_next))

    def first(q, done):
        pieces = [after(grads[q][0], *done)] + grads[q][1:]
        keep, send = hidden_partial(meta, pieces, down_weight, b_down, a_down, n_t, own_t)
        return keep, send

    def factors_of(stored):
        gate_value, up_value = [x.astype(jnp.float32) for x in stored]
        sigmoid_value = jax.nn.sigmoid(gate_value)
        dgate = up_value * sigmoid_value * (1.0 + gate_value * (1.0 - sigmoid_value))
        dup = gate_value * sigmoid_value
        return [x.astype(jnp.bfloat16) for x in (dgate, dup, dup * up_value)]

    def exchange(keep, other):
        mine = add32(keep, other).astype(jnp.bfloat16)
        return mine, [lax.ppermute(mine, "tensor", ring(n_t, 2 * s)) for s in range(1, ny)]

    def total(mine, far):
        both = add32(mine, *far).astype(jnp.bfloat16)
        return [both, lax.ppermute(both, "tensor", pair)]

    def second(q, sums, done):
        sums = [after(sums[0], *done), sums[1]]
        outs = input_partial(meta, factors, q, sums, gate_weight, up_weight, b_gu, a_gu, n_dp, own_t)
        return [outs[0]] + [lax.ppermute(outs[r], "dp", ring(n_dp, r)) for r in range(1, n_dp)]

    def finish(there, rc):
        return add32(*[x[:, :width] for x in there]).astype(jnp.bfloat16).reshape(g, rc, width)

    keep_a, send_a = first(0, (grads[1][n_dp - 2],))
    stored[0] = after(stored[0], keep_a)
    *near, hidden = factors_of(stored)
    other_a = lax.ppermute(after(send_a, *[x for there in far_stored for x in there]), "tensor", pair)
    mine_a, far_a = exchange(after(keep_a, near[0]), other_a)
    beside_stored = [lax.ppermute(after(x, mine_a), "tensor", pair) for x in stored]
    keep_b, send_b = first(1, (mine_a,))
    other_b = lax.ppermute(send_b, "tensor", pair)
    mine_b, far_b = exchange(keep_b, other_b)
    beside_stored[0] = after(beside_stored[0], keep_b)
    factors = [near, factors_of(beside_stored)[:2]]
    for there in far_stored:
        beside = [lax.ppermute(x, "tensor", pair) for x in [after(x, *beside_stored) for x in there]]
        for both in (there, beside):
            factors.append(factors_of([after(both[0], keep_b), both[1]])[:2])
    inputs = [after(layer_input, grads[1][-1], mine_a)] + [None] * (n_dp - 1)
    inputs[1] = lax.ppermute(inputs[0], "dp", z_next)
    inputs[-1] = lax.ppermute(inputs[0], "dp", ring(n_dp, -1))
    for k in range(2, n_dp // 2 + 1):
        inputs[k] = lax.ppermute(inputs[k - 1], "dp", z_next)
    for k in range(2, (n_dp + 1) // 2):
        inputs[-k] = lax.ppermute(inputs[1 - k], "dp", ring(n_dp, -1))
    sums_a = total(after(mine_a, mine_b, inputs[1], inputs[-1], *[pair[0] for pair in factors]), far_a)
    there_a = second(0, sums_a, ())
    sums_b = total(after(mine_b, there_a[0], inputs[n_dp // 2]), far_b)
    there_b = second(1, sums_b, ())

    half_a = finish([after(x, there_b[0]) for x in there_a], chunks[0][1])
    acts = masked_acts(meta, after(adapter_acts.T, half_a), n_t)
    grad_b_down = down_outer(meta, grads, acts)
    a_part = down_part(meta, [sums_a[0], after(sums_b[0], half_a)], hidden)
    a_parts = [a_part] + [lax.ppermute(a_part, "tensor", ring(n_t, 2 * s)) for s in range(1, ny)]
    a_parts = [after(x, grad_b_down) for x in a_parts]
    a_parts += [lax.ppermute(x, "tensor", pair) for x in a_parts]
    grad_b_gu = gate_up_outer(meta, factors, [sums_a, sums_b], after(acts, grad_b_down))

    def column_tenant(p, m):
        owner = lax.rem(m[1] // 2 + ny - p % ny, ny) * 2
        return tenant_of(m, owner + (m[1] % 2 if p < ny else 1 - m[1] % 2), own_t)

    a_parts[0] = after(a_parts[0], grad_b_gu)
    grad_a_down = spread(meta, a_parts, column_tenant, R, "spread_a_down")
    there_b[0] = after(there_b[0], grad_a_down)
    grad_a_gu = in_outer(meta, [there_a, there_b], inputs, g)
    half_b = finish(there_b, chunks[1][1])
    block_input_grad = jnp.concatenate([half_a, half_b], axis=1).reshape(own_rows, width)
    return (
        block_input_grad,
        grad_a_gu.transpose(0, 2, 1),
        grad_b_gu,
        grad_a_down.transpose(0, 2, 1),
        grad_b_down,
    )


def solution(mesh):
    placed = (
        P(("groups", "dp"), "tensor"),
        P(("groups", "dp"), "tensor"),
        P(("groups", "tensor"), "dp"),
        P(("groups", "tensor"), "dp"),
        P("groups", None),
        P("tensor", "dp"),
        P("tensor", "dp"),
        P("dp", "tensor"),
        P(None, "tensor", None),
        P(None, None, "dp"),
        P(None, "dp", None),
        P(None, None, "tensor"),
        P("groups"),
    )
    return jax.shard_map(
        per_device,
        mesh=mesh,
        in_specs=placed,
        out_specs=(
            P(("groups", "dp"), "tensor"),
            P("groups", "tensor", None),
            P("groups", None, "dp"),
            P("groups", "dp", None),
            P("groups", None, "tensor"),
        ),
        check_vma=False,
    )
```

```python
import functools

import jax
import jax.numpy as jnp
from jax import lax
from jax.experimental import pallas as pl
from jax.experimental.pallas import tpu as pltpu
from jax.sharding import PartitionSpec as P

R = 16
TENANTS = 4
BLOCK = 128
SHARES = (1, 1)
LANES = 128
VMEM_LIMIT = 12 * 1024 * 1024
STREAM_LIMIT = 50 * 1024 * 1024

ADAPTER_SCALE = 2.0

NT = (((1,), (1,)), ((), ()))
NN = (((1,), (0,)), ((), ()))
TN = (((0,), (0,)), ((), ()))
ANY = pl.BlockSpec(memory_space=pl.ANY)
SMEM = pl.BlockSpec(memory_space=pltpu.SMEM)
VMEM = pl.BlockSpec(memory_space=pltpu.VMEM)
NO_COST = pl.CostEstimate(flops=1, bytes_accessed=1, transcendentals=0)


def fdot(lhs, rhs, dims):
    return lax.dot_general(lhs, rhs, dims, preferred_element_type=jnp.float32)


def tile_of(width, most):
    tile = most
    while width % tile:
        tile -= LANES
    return tile


def whole(shape):
    return pl.BlockSpec(shape, lambda *_: (0,) * len(shape))


def tenant_of(meta, owner, own_t):
    return meta[2 + (owner * own_t) // BLOCK]


def owner_of(p, y, c, ny):
    return lax.rem(y + ny - p // 2, ny) * 2 + (c if p % 2 == 0 else 1 - c)


def hidden_kernel(sizes, meta, *refs):
    n_dp, n_t, g, own_t, rc, tile = sizes
    ny = n_t // 2
    pieces, (w_ref, bd_ref, ad_ref, keep_ref, send_ref), refs = refs[:n_dp], refs[n_dp : n_dp + 5], refs[n_dp + 5 :]
    x_scr, p_scr, w_scr, w_sem = refs
    z, t = meta[0], meta[1]
    y, c = t // 2, t % 2
    hidden_width, width = w_ref.shape
    steps = hidden_width // tile

    def fetch(f):
        rows = pl.ds(pl.multiple_of(f * tile, LANES), tile)
        return pltpu.make_async_copy(w_ref.at[rows], w_scr.at[f], w_sem.at[f])

    for f in range(steps):
        fetch(f).start()

    for k in range(n_dp):
        for j in range(g):
            owner = lax.rem(z + (n_dp - k), n_dp) * g + j
            away = jnp.where(owner % 2 == c, 0, ny)
            x_scr[away + owner // 2] = pieces[k][j]
    proj = fdot(x_scr[...].reshape(n_t * rc, width), bd_ref[...], NT)
    lane = lax.broadcasted_iota(jnp.int32, (rc, TENANTS * R), 1) // R
    zeros = jnp.zeros((rc, LANES - TENANTS * R), jnp.bfloat16)
    for s in range(n_t):
        owner = (s % ny) * 2 + (c if s < ny else 1 - c)
        own = jnp.where(lane == tenant_of(meta, owner, own_t), proj[s * rc : (s + 1) * rc], 0.0)
        p_scr[s * rc : (s + 1) * rc, :] = (ADAPTER_SCALE * own).astype(jnp.bfloat16)
        out = keep_ref if s < ny else send_ref
        out[s % ny, :, hidden_width:] = jnp.concatenate([own.astype(jnp.bfloat16), zeros], axis=1)

    def body(step, carry):
        at = pl.ds(pl.multiple_of(step * tile, LANES), tile)
        fetch(step).wait()
        acc = fdot(x_scr[...].reshape(n_t * rc, width), w_scr[step], NT)
        acc = (acc + fdot(p_scr[...], ad_ref[:, at], NN)).astype(jnp.bfloat16).reshape(n_t, rc, tile)
        keep_ref[:, :, at] = acc[:ny]
        send_ref[:, :, at] = acc[ny:]
        return carry

    lax.fori_loop(0, steps, body, 0)


def hidden_partial(meta, pieces, down_weight, b_down, a_down, n_t, own_t):
    n_dp = len(pieces)
    g, rc, width = pieces[0].shape
    ny = n_t // 2
    hidden_width = down_weight.shape[0]
    tile = tile_of(hidden_width, 512)
    low = TENANTS * R
    out = jax.ShapeDtypeStruct((ny, rc, hidden_width + LANES), jnp.bfloat16)
    return pl.pallas_call(
        functools.partial(hidden_kernel, (n_dp, n_t, g, own_t, rc, tile)),
        out_shape=(out, out),
        in_specs=[SMEM] + [VMEM] * n_dp + [ANY] + [VMEM] * 2,
        out_specs=[VMEM] * 2,
        scratch_shapes=[
            pltpu.VMEM((n_t, rc, width), jnp.bfloat16),
            pltpu.VMEM((n_t * rc, low), jnp.bfloat16),
            pltpu.VMEM((hidden_width // tile, tile, width), jnp.bfloat16),
            pltpu.SemaphoreType.DMA((hidden_width // tile,)),
        ],
        compiler_params=pltpu.CompilerParams(vmem_limit_bytes=STREAM_LIMIT),
        cost_estimate=NO_COST,
        name="hidden_partial",
    )(meta, *pieces, down_weight, b_down, a_down)


def grads_of(total, factors):
    total = total.astype(jnp.float32)
    return [(total * factor[...].astype(jnp.float32)).astype(jnp.bfloat16) for factor in factors]


def input_kernel(sizes, meta, *refs):
    n_dp, n_t, g, own_t, rc, q, tile = sizes
    ny = n_t // 2
    factors, refs = [refs[2 * p : 2 * p + 2] for p in range(n_t)], refs[2 * n_t :]
    sums, (gw_ref, uw_ref, b_ref, a_ref) = refs[:2], refs[2:6]
    outs, (g_scr, u_scr, q_scr, w_scr, w_sem) = refs[6 : 6 + n_dp], refs[6 + n_dp :]
    z, t = meta[0], meta[1]
    y, c = t // 2, t % 2
    rows = n_t * rc
    width, hidden_width = gw_ref.shape
    steps = width // tile

    def fetch(f):
        at = pl.ds(pl.multiple_of(f * tile, LANES), tile)
        return [
            pltpu.make_async_copy(w.at[at], w_scr.at[f, k], w_sem.at[f, k]) for k, w in enumerate((gw_ref, uw_ref))
        ]

    for f in range(steps):
        for copy in fetch(f):
            copy.start()

    for p in range(n_t):
        owner = owner_of(p, y, c, ny)
        slot = lax.rem(owner // g + n_dp - z, n_dp) * g + owner % g
        mine = [factor[q * rc : (q + 1) * rc, :] for factor in factors[p]]
        g_scr[slot], u_scr[slot] = grads_of(sums[p % 2][owner // 2, :, :hidden_width], mine)
    q_gate = fdot(g_scr[...].reshape(rows, hidden_width), b_ref[...], NT)
    q_up = fdot(u_scr[...].reshape(rows, hidden_width), b_ref[...], NT)
    lane = lax.broadcasted_iota(jnp.int32, (rc, 2 * R * TENANTS), 1)
    shares = []
    for r in range(n_dp):
        share = []
        for j in range(g):
            at = slice((r * g + j) * rc, (r * g + j + 1) * rc)
            tenant = tenant_of(meta, lax.rem(z + r, n_dp) * g + j, own_t)
            mine = jnp.where(lane % (2 * R) < R, q_gate[at], q_up[at])
            mine = jnp.where(lane // (2 * R) == tenant, mine, 0.0)
            q_scr[at, :] = (ADAPTER_SCALE * mine).astype(jnp.bfloat16)
            share.append(sum(mine[:, e * 2 * R : (e + 1) * 2 * R] for e in range(TENANTS)))
        shares.append(jnp.concatenate(share, axis=0))
    share = jnp.concatenate(shares, axis=1).astype(jnp.bfloat16)
    for r in range(n_dp):
        outs[r][:, width:] = share

    def body(step, carry):
        at = pl.ds(pl.multiple_of(step * tile, LANES), tile)
        for copy in fetch(step):
            copy.wait()
        acc = fdot(g_scr[...].reshape(rows, hidden_width), w_scr[step, 0], NT)
        acc = acc + fdot(u_scr[...].reshape(rows, hidden_width), w_scr[step, 1], NT)
        acc = (acc + fdot(q_scr[...], a_ref[:, at], NN)).astype(jnp.bfloat16)
        for r in range(n_dp):
            outs[r][:, at] = acc[r * g * rc : (r + 1) * g * rc]
        return carry

    lax.fori_loop(0, steps, body, 0)


def input_partial(meta, factors, q, sums, gate_weight, up_weight, b_gu, a_gu, n_dp, own_t):
    n_t = len(factors)
    ny, rc, _ = sums[0].shape
    g = n_t // n_dp
    width, hidden_width = gate_weight.shape
    tile = tile_of(width, 256)
    low = 2 * R * TENANTS
    rows = n_t * rc
    outs = [jax.ShapeDtypeStruct((g * rc, width + n_dp * 2 * R), jnp.bfloat16)] * n_dp
    return pl.pallas_call(
        functools.partial(input_kernel, (n_dp, n_t, g, own_t, rc, q, tile)),
        out_shape=outs,
        in_specs=[SMEM] + [VMEM] * (2 * n_t + 2) + [ANY] * 2 + [VMEM] * 2,
        out_specs=[VMEM] * n_dp,
        scratch_shapes=[
            pltpu.VMEM((n_t, rc, hidden_width), jnp.bfloat16),
            pltpu.VMEM((n_t, rc, hidden_width), jnp.bfloat16),
            pltpu.VMEM((rows, low), jnp.bfloat16),
            pltpu.VMEM((width // tile, 2, tile, hidden_width), jnp.bfloat16),
            pltpu.SemaphoreType.DMA((width // tile, 2)),
        ],
        compiler_params=pltpu.CompilerParams(vmem_limit_bytes=STREAM_LIMIT),
        cost_estimate=NO_COST,
        name="input_partial",
    )(meta, *[x for pair in factors for x in pair], *sums, gate_weight, up_weight, b_gu, a_gu)


def acts_kernel(meta, acts_ref, out_ref):
    layers, n_t, _, own_t = out_ref.shape
    for owner in range(n_t):
        tenant = tenant_of(meta, owner, own_t)
        for layer in range(layers):
            mine = acts_ref[layer * R : (layer + 1) * R, owner * own_t : (owner + 1) * own_t]
            for e in range(TENANTS):
                chosen = jnp.where(tenant == e, mine.astype(jnp.float32), 0.0)
                out_ref[layer, owner, e * R : (e + 1) * R, :] = chosen.astype(jnp.bfloat16)


def masked_acts(meta, acts, n_t):
    return pl.pallas_call(
        acts_kernel,
        out_shape=jax.ShapeDtypeStruct((3, n_t, TENANTS * R, acts.shape[1] // n_t), jnp.bfloat16),
        in_specs=[SMEM, VMEM],
        out_specs=VMEM,
        compiler_params=pltpu.CompilerParams(vmem_limit_bytes=VMEM_LIMIT),
        cost_estimate=NO_COST,
        name="masked_acts",
    )(meta, acts)


def left_of(left_ref, layer, owners):
    return jnp.concatenate([left_ref[layer, owner] for owner in owners], axis=1)


def down_outer_kernel(n_dp, g, chunks, meta, *refs):
    pieces, (left_ref, out_ref) = refs[: n_dp * chunks], refs[n_dp * chunks :]
    owners = [lax.rem(meta[0] + (n_dp - k), n_dp) * g + j for k in range(n_dp) for j in range(g)]
    right = [pieces[q * n_dp + k][j] for k in range(n_dp) for j in range(g) for q in range(chunks)]
    out = ADAPTER_SCALE * fdot(left_of(left_ref, 2, owners), jnp.concatenate(right, axis=0), NN)
    out_ref[...] = out.reshape(out_ref.shape)


def down_outer(meta, grads, left):
    n_dp, chunks = len(grads[0]), len(grads)
    pieces = [piece for pieces in grads for piece in pieces]
    g, _, width = pieces[0].shape
    tile = tile_of(width, 512)
    return pl.pallas_call(
        functools.partial(down_outer_kernel, n_dp, g, chunks),
        out_shape=jax.ShapeDtypeStruct((TENANTS, R, width), jnp.float32),
        grid_spec=pltpu.PrefetchScalarGridSpec(
            num_scalar_prefetch=1,
            grid=(width // tile,),
            in_specs=[
                pl.BlockSpec(piece.shape[:2] + (tile,), lambda f, *_: (0, 0, f)) for piece in pieces
            ]
            + [whole(left.shape)],
            out_specs=pl.BlockSpec((TENANTS, R, tile), lambda f, *_: (0, 0, f)),
        ),
        compiler_params=pltpu.CompilerParams(vmem_limit_bytes=VMEM_LIMIT),
        cost_estimate=NO_COST,
        name="down_outer",
    )(meta, *pieces, left)


def gate_up_outer_kernel(n_t, chunks, meta, *refs):
    ny = n_t // 2
    factors, refs = [refs[2 * p : 2 * p + 2] for p in range(n_t)], refs[2 * n_t :]
    sums, (left_ref, out_ref) = [refs[2 * q : 2 * q + 2] for q in range(chunks)], refs[2 * chunks :]
    y, c = meta[1] // 2, meta[1] % 2
    owners = [owner_of(p, y, c, ny) for p in range(n_t)]
    grads = []
    for p in range(n_t):
        total = jnp.concatenate([both[p % 2][owners[p] // 2] for both in sums], axis=0)
        grads.append(grads_of(total, factors[p]))
    for layer in range(2):
        right = jnp.concatenate([grad[layer] for grad in grads], axis=0)
        out = ADAPTER_SCALE * fdot(left_of(left_ref, layer, owners), right, NN)
        out_ref[:, layer * R : (layer + 1) * R, :] = out.reshape(TENANTS, R, out.shape[1])


def gate_up_outer(meta, factors, sums, left):
    n_t, chunks = len(factors), len(sums)
    rc = sums[0][0].shape[1]
    own_t, width = factors[0][0].shape
    tile = tile_of(width, 896)
    return pl.pallas_call(
        functools.partial(gate_up_outer_kernel, n_t, chunks),
        out_shape=jax.ShapeDtypeStruct((TENANTS, 2 * R, width), jnp.float32),
        grid_spec=pltpu.PrefetchScalarGridSpec(
            num_scalar_prefetch=1,
            grid=(width // tile,),
            in_specs=[pl.BlockSpec((own_t, tile), lambda f, *_: (0, f))] * (2 * n_t)
            + [pl.BlockSpec((n_t // 2, rc, tile), lambda f, *_: (0, 0, f))] * (2 * chunks)
            + [whole(left.shape)],
            out_specs=pl.BlockSpec((TENANTS, 2 * R, tile), lambda f, *_: (0, 0, f)),
        ),
        compiler_params=pltpu.CompilerParams(vmem_limit_bytes=2 * VMEM_LIMIT),
        cost_estimate=NO_COST,
        name="gate_up_outer",
    )(meta, *[x for pair in factors for x in pair], *[x for both in sums for x in both], left)


def down_part_kernel(chunks, meta, *refs):
    sums, (hidden_ref, out_ref) = refs[:chunks], refs[chunks:]
    width = hidden_ref.shape[1]
    low = jnp.concatenate([both[meta[1] // 2][:, width:] for both in sums], axis=0)
    part = fdot(low, hidden_ref[...], TN)
    out_ref[...] = sum(part[e * R : (e + 1) * R] for e in range(TENANTS)).astype(jnp.bfloat16)


def down_part(meta, sums, hidden):
    return pl.pallas_call(
        functools.partial(down_part_kernel, len(sums)),
        out_shape=jax.ShapeDtypeStruct((R, hidden.shape[1]), jnp.bfloat16),
        in_specs=[SMEM] + [VMEM] * (len(sums) + 1),
        out_specs=VMEM,
        compiler_params=pltpu.CompilerParams(vmem_limit_bytes=VMEM_LIMIT),
        cost_estimate=NO_COST,
        name="down_part",
    )(meta, *sums, hidden)


def spread_kernel(tenant_at, rows, meta, *refs):
    parts, out_ref = refs[:-1], refs[-1]
    out_ref[...] = jnp.zeros_like(out_ref)
    at = 0
    for part in parts:
        for k in range(part.shape[0] // rows):
            tenant = tenant_at(at, meta)
            term = part[k * rows : (k + 1) * rows].astype(jnp.float32)
            out_ref[tenant] = out_ref[tenant] + ADAPTER_SCALE * term
            at += 1


def spread(meta, parts, tenant_at, rows, name):
    width = parts[0].shape[1]
    out = jax.ShapeDtypeStruct((TENANTS, rows, width), jnp.float32)
    tile = tile_of(width, 1024)
    return pl.pallas_call(
        functools.partial(spread_kernel, tenant_at, rows),
        out_shape=out,
        grid_spec=pltpu.PrefetchScalarGridSpec(
            num_scalar_prefetch=1,
            grid=(width // tile,),
            in_specs=[pl.BlockSpec((part.shape[0], tile), lambda f, *_: (0, f)) for part in parts],
            out_specs=pl.BlockSpec((TENANTS, rows, tile), lambda f, *_: (0, 0, f)),
        ),
        compiler_params=pltpu.CompilerParams(vmem_limit_bytes=VMEM_LIMIT),
        cost_estimate=NO_COST,
        name=name,
    )(meta, *parts)


def in_outer_kernel(n_dp, chunks, g, meta, *refs):
    shares, inputs, out_ref = refs[: n_dp * chunks], refs[n_dp * chunks : -1], refs[-1]
    out_ref[...] = jnp.zeros_like(out_ref)
    rows, width = inputs[0].shape
    own_t = rows // g
    rc = own_t // chunks
    for k in range(n_dp):
        block = lax.rem(meta[0] + n_dp - k, n_dp)
        queries = []
        for q in range(chunks):
            query = 0.0
            for s in range(n_dp):
                at = width + (s + n_dp - k) % n_dp * 2 * R
                query = query + shares[q * n_dp + s][:, at : at + 2 * R].astype(jnp.float32)
            queries.append(query.astype(jnp.bfloat16))
        low = [queries[q][j * rc : (j + 1) * rc] for j in range(g) for q in range(chunks)]
        total = fdot(jnp.concatenate(low, axis=0), inputs[k][...], TN)
        tenant = meta[2 + block]
        out_ref[tenant] = out_ref[tenant] + ADAPTER_SCALE * total


def in_outer(meta, shares, inputs, g):
    n_dp, width = len(inputs), inputs[0].shape[1]
    chunks = len(shares)
    shares = [share for there in shares for share in there]
    return pl.pallas_call(
        functools.partial(in_outer_kernel, n_dp, chunks, g),
        out_shape=jax.ShapeDtypeStruct((TENANTS, 2 * R, width), jnp.float32),
        in_specs=[SMEM] + [VMEM] * (len(shares) + n_dp),
        out_specs=VMEM,
        compiler_params=pltpu.CompilerParams(vmem_limit_bytes=VMEM_LIMIT),
        cost_estimate=NO_COST,
        name="in_outer",
    )(meta, *shares, *inputs)


def ring(n, by):
    return [(k, (k + by) % n) for k in range(n)]


def add32(*terms):
    return sum(term.astype(jnp.float32) for term in terms)


def after(value, *done):
    return lax.optimization_barrier((value,) + done)[0]


def per_device(
    layer_input,
    out_grad,
    gate_pre,
    up_pre,
    adapter_acts,
    gate_weight,
    up_weight,
    down_weight,
    adapter_a_gu,
    adapter_b_gu,
    adapter_a_down,
    adapter_b_down,
    block_tenant,
):
    n_dp, n_t = lax.axis_size("dp"), lax.axis_size("tensor")
    ny = n_t // 2
    z, t = lax.axis_index("dp"), lax.axis_index("tensor")
    own_rows, width = out_grad.shape
    own_t, hidden_width = gate_pre.shape
    tokens = adapter_acts.shape[0]
    g = own_rows // own_t
    assert own_rows == BLOCK and g * own_t == own_rows and n_t == 2 * ny and n_t == g * n_dp
    chunks, at = [], 0
    for share in SHARES:
        chunks.append((at, own_t * share // sum(SHARES)))
        at += chunks[-1][1]

    meta = jnp.concatenate([jnp.stack([z, t]).astype(jnp.int32), block_tenant])
    b_down = adapter_b_down.reshape(TENANTS * R, width)
    a_down = jnp.transpose(adapter_a_down, (0, 2, 1)).reshape(TENANTS * R, hidden_width)
    b_gu = adapter_b_gu.reshape(TENANTS * 2 * R, hidden_width)
    a_gu = jnp.transpose(adapter_a_gu, (0, 2, 1)).reshape(TENANTS * 2 * R, width)

    pair = [(k, k ^ 1) for k in range(n_t)]
    z_next = ring(n_dp, 1)

    stored = [gate_pre, up_pre]
    far_stored = [[lax.ppermute(x, "tensor", ring(n_t, 2 * s)) for x in stored] for s in range(1, ny)]
    grads = [[out_grad.reshape(g, own_t, width)[:, at : at + rc]] for at, rc in chunks]
    for _ in range(n_dp - 1):
        grads[0].append(lax.ppermute(grads[0][-1], "dp", z_next))
    grads[1][0] = after(grads[1][0], grads[0][2])
    for _ in range(n_dp - 1):
        grads[1].append(lax.ppermute(grads[1][-1], "dp", z_next))

    def first(q, done):
        pieces = [after(grads[q][0], *done)] + grads[q][1:]
        keep, send = hidden_partial(meta, pieces, down_weight, b_down, a_down, n_t, own_t)
        return keep, send

    def factors_of(stored):
        gate_value, up_value = [x.astype(jnp.float32) for x in stored]
        sigmoid_value = jax.nn.sigmoid(gate_value)
        dgate = up_value * sigmoid_value * (1.0 + gate_value * (1.0 - sigmoid_value))
        dup = gate_value * sigmoid_value
        return [x.astype(jnp.bfloat16) for x in (dgate, dup, dup * up_value)]

    def exchange(keep, other):
        mine = add32(keep, other).astype(jnp.bfloat16)
        return mine, [lax.ppermute(mine, "tensor", ring(n_t, 2 * s)) for s in range(1, ny)]

    def total(mine, far):
        both = add32(mine, *far).astype(jnp.bfloat16)
        return [both, lax.ppermute(both, "tensor", pair)]

    def second(q, sums, done):
        sums = [after(sums[0], *done), sums[1]]
        outs = input_partial(meta, factors, q, sums, gate_weight, up_weight, b_gu, a_gu, n_dp, own_t)
        return [outs[0]] + [lax.ppermute(outs[r], "dp", ring(n_dp, r)) for r in range(1, n_dp)]

    def finish(there, rc):
        return add32(*[x[:, :width] for x in there]).astype(jnp.bfloat16).reshape(g, rc, width)

    keep_a, send_a = first(0, (grads[1][1],))
    stored[0] = after(stored[0], keep_a)
    *near, hidden = factors_of(stored)
    other_a = lax.ppermute(after(send_a, grads[1][n_dp - 2], *[x for there in far_stored for x in there]), "tensor", pair)
    mine_a, far_a = exchange(after(keep_a, near[0], grads[1][-1]), other_a)
    beside_stored = [lax.ppermute(after(x, mine_a), "tensor", pair) for x in stored]
    keep_b, send_b = first(1, (mine_a,))
    other_b = lax.ppermute(send_b, "tensor", pair)
    beside_stored[0] = after(beside_stored[0], keep_b)
    factors = [near, factors_of(beside_stored)[:2]]
    for there in far_stored:
        beside = [lax.ppermute(x, "tensor", pair) for x in [after(x, *beside_stored) for x in there]]
        for both in (there, beside):
            factors.append(factors_of([after(both[0], keep_b), both[1]])[:2])
    mine_b, far_b = exchange(after(keep_b, *far_a, *[pair[0] for pair in factors]), other_b)
    inputs = [after(layer_input, grads[1][-1], mine_a)] + [None] * (n_dp - 1)
    inputs[1] = lax.ppermute(inputs[0], "dp", z_next)
    inputs[-1] = lax.ppermute(inputs[0], "dp", ring(n_dp, -1))
    for k in range(2, n_dp // 2 + 1):
        inputs[k] = lax.ppermute(inputs[k - 1], "dp", z_next)
    for k in range(2, (n_dp + 1) // 2):
        inputs[-k] = lax.ppermute(inputs[1 - k], "dp", ring(n_dp, -1))
    sums_a = total(after(mine_a, mine_b), far_a)
    there_a = second(0, sums_a, (inputs[1],))
    sums_b = total(after(mine_b, there_a[0], inputs[n_dp // 2], inputs[-1]), far_b)
    there_b = second(1, sums_b, ())

    half_a = finish([after(x, there_b[0]) for x in there_a], chunks[0][1])
    acts = masked_acts(meta, after(adapter_acts.T, half_a), n_t)
    grad_b_down = down_outer(meta, grads, acts)
    a_part = down_part(meta, [sums_a[0], after(sums_b[0], half_a)], hidden)
    a_parts = [a_part] + [lax.ppermute(a_part, "tensor", ring(n_t, 2 * s)) for s in range(1, ny)]
    a_parts = [after(x, grad_b_down) for x in a_parts]
    a_parts += [lax.ppermute(x, "tensor", pair) for x in a_parts]
    grad_b_gu = gate_up_outer(meta, factors, [sums_a, sums_b], after(acts, grad_b_down))

    def column_tenant(p, m):
        owner = lax.rem(m[1] // 2 + ny - p % ny, ny) * 2
        return tenant_of(m, owner + (m[1] % 2 if p < ny else 1 - m[1] % 2), own_t)

    a_parts[0] = after(a_parts[0], grad_b_gu)
    grad_a_down = spread(meta, a_parts, column_tenant, R, "spread_a_down")
    there_b[0] = after(there_b[0], grad_a_down)
    grad_a_gu = in_outer(meta, [there_a, there_b], inputs, g)
    half_b = finish(there_b, chunks[1][1])
    block_input_grad = jnp.concatenate([half_a, half_b], axis=1).reshape(own_rows, width)
    return (
        block_input_grad,
        grad_a_gu.transpose(0, 2, 1),
        grad_b_gu,
        grad_a_down.transpose(0, 2, 1),
        grad_b_down,
    )


def solution(mesh):
    placed = (
        P(("groups", "dp"), "tensor"),
        P(("groups", "dp"), "tensor"),
        P(("groups", "tensor"), "dp"),
        P(("groups", "tensor"), "dp"),
        P("groups", None),
        P("tensor", "dp"),
        P("tensor", "dp"),
        P("dp", "tensor"),
        P(None, "tensor", None),
        P(None, None, "dp"),
        P(None, "dp", None),
        P(None, None, "tensor"),
        P("groups"),
    )
    return jax.shard_map(
        per_device,
        mesh=mesh,
        in_specs=placed,
        out_specs=(
            P(("groups", "dp"), "tensor"),
            P("groups", "tensor", None),
            P("groups", None, "dp"),
            P("groups", "dp", None),
            P("groups", None, "tensor"),
        ),
        check_vma=False,
    )
```

```python
import functools

import jax
import jax.numpy as jnp
from jax import lax
from jax.experimental import pallas as pl
from jax.experimental.pallas import tpu as pltpu
from jax.sharding import PartitionSpec as P

R = 16
TENANTS = 4
BLOCK = 128
SHARES = (1, 1)
LANES = 128
VMEM_LIMIT = 12 * 1024 * 1024
STREAM_LIMIT = 50 * 1024 * 1024

ADAPTER_SCALE = 2.0

NT = (((1,), (1,)), ((), ()))
NN = (((1,), (0,)), ((), ()))
TN = (((0,), (0,)), ((), ()))
ANY = pl.BlockSpec(memory_space=pl.ANY)
SMEM = pl.BlockSpec(memory_space=pltpu.SMEM)
VMEM = pl.BlockSpec(memory_space=pltpu.VMEM)
NO_COST = pl.CostEstimate(flops=1, bytes_accessed=1, transcendentals=0)


def fdot(lhs, rhs, dims):
    return lax.dot_general(lhs, rhs, dims, preferred_element_type=jnp.float32)


def tile_of(width, most):
    tile = most
    while width % tile:
        tile -= LANES
    return tile


def whole(shape):
    return pl.BlockSpec(shape, lambda *_: (0,) * len(shape))


def tenant_of(meta, owner, own_t):
    return meta[2 + (owner * own_t) // BLOCK]


def owner_of(p, y, c, ny):
    return lax.rem(y + ny - p // 2, ny) * 2 + (c if p % 2 == 0 else 1 - c)


def hidden_kernel(sizes, chunks, meta, *refs):
    n_dp, n_t, g, own_t, tile = sizes
    ny = n_t // 2
    pieces, (w_ref, bd_ref, ad_ref), refs = refs[:n_dp], refs[n_dp : n_dp + 3], refs[n_dp + 3 :]
    outs, (x_scr, p_scr, w_scr, w_sem) = refs[: 2 * len(chunks)], refs[2 * len(chunks) :]
    keeps, sends = outs[: len(chunks)], outs[len(chunks) :]
    z, t = meta[0], meta[1]
    y, c = t // 2, t % 2
    hidden_width, width = w_ref.shape
    steps = hidden_width // tile

    def fetch(f):
        rows = pl.ds(pl.multiple_of(f * tile, LANES), tile)
        return pltpu.make_async_copy(w_ref.at[rows], w_scr.at[f], w_sem.at[f])

    for f in range(steps):
        fetch(f).start()

    for k in range(n_dp):
        for j in range(g):
            owner = lax.rem(z + (n_dp - k), n_dp) * g + j
            away = jnp.where(owner % 2 == c, 0, ny)
            x_scr[away + owner // 2] = pieces[k][j]
    proj = fdot(x_scr[...].reshape(n_t * own_t, width), bd_ref[...], NT)
    lane = lax.broadcasted_iota(jnp.int32, (own_t, TENANTS * R), 1) // R
    zeros = jnp.zeros((own_t, LANES - TENANTS * R), jnp.bfloat16)
    for s in range(n_t):
        owner = (s % ny) * 2 + (c if s < ny else 1 - c)
        own = jnp.where(lane == tenant_of(meta, owner, own_t), proj[s * own_t : (s + 1) * own_t], 0.0)
        p_scr[s * own_t : (s + 1) * own_t, :] = (ADAPTER_SCALE * own).astype(jnp.bfloat16)
        padded = jnp.concatenate([own.astype(jnp.bfloat16), zeros], axis=1)
        for (first, rc), out in zip(chunks, keeps if s < ny else sends):
            out[s % ny, :, hidden_width:] = padded[first : first + rc]

    def body(step, carry):
        at = pl.ds(pl.multiple_of(step * tile, LANES), tile)
        fetch(step).wait()
        acc = fdot(x_scr[...].reshape(n_t * own_t, width), w_scr[step], NT)
        acc = (acc + fdot(p_scr[...], ad_ref[:, at], NN)).astype(jnp.bfloat16).reshape(n_t, own_t, tile)
        for (first, rc), keep, send in zip(chunks, keeps, sends):
            keep[:, :, at] = acc[:ny, first : first + rc]
            send[:, :, at] = acc[ny:, first : first + rc]
        return carry

    lax.fori_loop(0, steps, body, 0)


def hidden_partial(meta, pieces, down_weight, b_down, a_down, n_t, chunks):
    n_dp = len(pieces)
    g, own_t, width = pieces[0].shape
    ny = n_t // 2
    hidden_width = down_weight.shape[0]
    tile = tile_of(hidden_width, 512)
    low = TENANTS * R
    outs = [jax.ShapeDtypeStruct((ny, rc, hidden_width + LANES), jnp.bfloat16) for _, rc in chunks]
    result = pl.pallas_call(
        functools.partial(hidden_kernel, (n_dp, n_t, g, own_t, tile), chunks),
        out_shape=outs * 2,
        in_specs=[SMEM] + [VMEM] * n_dp + [ANY] + [VMEM] * 2,
        out_specs=[VMEM] * (2 * len(chunks)),
        scratch_shapes=[
            pltpu.VMEM((n_t, own_t, width), jnp.bfloat16),
            pltpu.VMEM((n_t * own_t, low), jnp.bfloat16),
            pltpu.VMEM((hidden_width // tile, tile, width), jnp.bfloat16),
            pltpu.SemaphoreType.DMA((hidden_width // tile,)),
        ],
        compiler_params=pltpu.CompilerParams(vmem_limit_bytes=STREAM_LIMIT),
        cost_estimate=NO_COST,
        name="hidden_partial",
    )(meta, *pieces, down_weight, b_down, a_down)
    return list(result[: len(chunks)]), list(result[len(chunks) :])


def grads_of(total, factors):
    total = total.astype(jnp.float32)
    return [(total * factor[...].astype(jnp.float32)).astype(jnp.bfloat16) for factor in factors]


def input_kernel(sizes, meta, *refs):
    n_dp, n_t, g, own_t, rc, q, tile = sizes
    ny = n_t // 2
    factors, refs = [refs[2 * p : 2 * p + 2] for p in range(n_t)], refs[2 * n_t :]
    sums, (gw_ref, uw_ref, b_ref, a_ref) = refs[:2], refs[2:6]
    outs, (g_scr, u_scr, q_scr, w_scr, w_sem) = refs[6 : 6 + n_dp], refs[6 + n_dp :]
    z, t = meta[0], meta[1]
    y, c = t // 2, t % 2
    rows = n_t * rc
    width, hidden_width = gw_ref.shape
    steps = width // tile

    def fetch(f):
        at = pl.ds(pl.multiple_of(f * tile, LANES), tile)
        return [
            pltpu.make_async_copy(w.at[at], w_scr.at[f, k], w_sem.at[f, k]) for k, w in enumerate((gw_ref, uw_ref))
        ]

    for f in range(steps):
        for copy in fetch(f):
            copy.start()

    for p in range(n_t):
        owner = owner_of(p, y, c, ny)
        slot = lax.rem(owner // g + n_dp - z, n_dp) * g + owner % g
        mine = [factor[q * rc : (q + 1) * rc, :] for factor in factors[p]]
        g_scr[slot], u_scr[slot] = grads_of(sums[p % 2][owner // 2, :, :hidden_width], mine)
    q_gate = fdot(g_scr[...].reshape(rows, hidden_width), b_ref[...], NT)
    q_up = fdot(u_scr[...].reshape(rows, hidden_width), b_ref[...], NT)
    lane = lax.broadcasted_iota(jnp.int32, (rc, 2 * R * TENANTS), 1)
    shares = []
    for r in range(n_dp):
        share = []
        for j in range(g):
            at = slice((r * g + j) * rc, (r * g + j + 1) * rc)
            tenant = tenant_of(meta, lax.rem(z + r, n_dp) * g + j, own_t)
            mine = jnp.where(lane % (2 * R) < R, q_gate[at], q_up[at])
            mine = jnp.where(lane // (2 * R) == tenant, mine, 0.0)
            q_scr[at, :] = (ADAPTER_SCALE * mine).astype(jnp.bfloat16)
            share.append(sum(mine[:, e * 2 * R : (e + 1) * 2 * R] for e in range(TENANTS)))
        shares.append(jnp.concatenate(share, axis=0))
    share = jnp.concatenate(shares, axis=1).astype(jnp.bfloat16)
    for r in range(n_dp):
        outs[r][:, width:] = share

    def body(step, carry):
        at = pl.ds(pl.multiple_of(step * tile, LANES), tile)
        for copy in fetch(step):
            copy.wait()
        acc = fdot(g_scr[...].reshape(rows, hidden_width), w_scr[step, 0], NT)
        acc = acc + fdot(u_scr[...].reshape(rows, hidden_width), w_scr[step, 1], NT)
        acc = (acc + fdot(q_scr[...], a_ref[:, at], NN)).astype(jnp.bfloat16)
        for r in range(n_dp):
            outs[r][:, at] = acc[r * g * rc : (r + 1) * g * rc]
        return carry

    lax.fori_loop(0, steps, body, 0)


def input_partial(meta, factors, q, sums, gate_weight, up_weight, b_gu, a_gu, n_dp, own_t):
    n_t = len(factors)
    ny, rc, _ = sums[0].shape
    g = n_t // n_dp
    width, hidden_width = gate_weight.shape
    tile = tile_of(width, 256)
    low = 2 * R * TENANTS
    rows = n_t * rc
    outs = [jax.ShapeDtypeStruct((g * rc, width + n_dp * 2 * R), jnp.bfloat16)] * n_dp
    return pl.pallas_call(
        functools.partial(input_kernel, (n_dp, n_t, g, own_t, rc, q, tile)),
        out_shape=outs,
        in_specs=[SMEM] + [VMEM] * (2 * n_t + 2) + [ANY] * 2 + [VMEM] * 2,
        out_specs=[VMEM] * n_dp,
        scratch_shapes=[
            pltpu.VMEM((n_t, rc, hidden_width), jnp.bfloat16),
            pltpu.VMEM((n_t, rc, hidden_width), jnp.bfloat16),
            pltpu.VMEM((rows, low), jnp.bfloat16),
            pltpu.VMEM((width // tile, 2, tile, hidden_width), jnp.bfloat16),
            pltpu.SemaphoreType.DMA((width // tile, 2)),
        ],
        compiler_params=pltpu.CompilerParams(vmem_limit_bytes=STREAM_LIMIT),
        cost_estimate=NO_COST,
        name="input_partial",
    )(meta, *[x for pair in factors for x in pair], *sums, gate_weight, up_weight, b_gu, a_gu)


def acts_kernel(meta, acts_ref, out_ref):
    layers, n_t, _, own_t = out_ref.shape
    for owner in range(n_t):
        tenant = tenant_of(meta, owner, own_t)
        for layer in range(layers):
            mine = acts_ref[layer * R : (layer + 1) * R, owner * own_t : (owner + 1) * own_t]
            for e in range(TENANTS):
                chosen = jnp.where(tenant == e, mine.astype(jnp.float32), 0.0)
                out_ref[layer, owner, e * R : (e + 1) * R, :] = chosen.astype(jnp.bfloat16)


def masked_acts(meta, acts, n_t):
    return pl.pallas_call(
        acts_kernel,
        out_shape=jax.ShapeDtypeStruct((3, n_t, TENANTS * R, acts.shape[1] // n_t), jnp.bfloat16),
        in_specs=[SMEM, VMEM],
        out_specs=VMEM,
        compiler_params=pltpu.CompilerParams(vmem_limit_bytes=VMEM_LIMIT),
        cost_estimate=NO_COST,
        name="masked_acts",
    )(meta, acts)


def left_of(left_ref, layer, owners):
    return jnp.concatenate([left_ref[layer, owner] for owner in owners], axis=1)


def down_outer_kernel(n_dp, g, meta, *refs):
    pieces, (left_ref, out_ref) = refs[:n_dp], refs[n_dp:]
    owners = [lax.rem(meta[0] + (n_dp - k), n_dp) * g + j for k in range(n_dp) for j in range(g)]
    right = [pieces[k][j] for k in range(n_dp) for j in range(g)]
    out = ADAPTER_SCALE * fdot(left_of(left_ref, 2, owners), jnp.concatenate(right, axis=0), NN)
    out_ref[...] = out.reshape(out_ref.shape)


def down_outer(meta, grads, left):
    n_dp = len(grads)
    g, _, width = grads[0].shape
    tile = tile_of(width, 512)
    return pl.pallas_call(
        functools.partial(down_outer_kernel, n_dp, g),
        out_shape=jax.ShapeDtypeStruct((TENANTS, R, width), jnp.float32),
        grid_spec=pltpu.PrefetchScalarGridSpec(
            num_scalar_prefetch=1,
            grid=(width // tile,),
            in_specs=[
                pl.BlockSpec(piece.shape[:2] + (tile,), lambda f, *_: (0, 0, f)) for piece in grads
            ]
            + [whole(left.shape)],
            out_specs=pl.BlockSpec((TENANTS, R, tile), lambda f, *_: (0, 0, f)),
        ),
        compiler_params=pltpu.CompilerParams(vmem_limit_bytes=VMEM_LIMIT),
        cost_estimate=NO_COST,
        name="down_outer",
    )(meta, *grads, left)


def gate_up_outer_kernel(n_t, chunks, meta, *refs):
    ny = n_t // 2
    factors, refs = [refs[2 * p : 2 * p + 2] for p in range(n_t)], refs[2 * n_t :]
    sums, (left_ref, out_ref) = [refs[2 * q : 2 * q + 2] for q in range(chunks)], refs[2 * chunks :]
    y, c = meta[1] // 2, meta[1] % 2
    owners = [owner_of(p, y, c, ny) for p in range(n_t)]
    grads = []
    for p in range(n_t):
        total = jnp.concatenate([both[p % 2][owners[p] // 2] for both in sums], axis=0)
        grads.append(grads_of(total, factors[p]))
    for layer in range(2):
        right = jnp.concatenate([grad[layer] for grad in grads], axis=0)
        out = ADAPTER_SCALE * fdot(left_of(left_ref, layer, owners), right, NN)
        out_ref[:, layer * R : (layer + 1) * R, :] = out.reshape(TENANTS, R, out.shape[1])


def gate_up_outer(meta, factors, sums, left):
    n_t, chunks = len(factors), len(sums)
    rc = sums[0][0].shape[1]
    own_t, width = factors[0][0].shape
    tile = tile_of(width, 896)
    return pl.pallas_call(
        functools.partial(gate_up_outer_kernel, n_t, chunks),
        out_shape=jax.ShapeDtypeStruct((TENANTS, 2 * R, width), jnp.float32),
        grid_spec=pltpu.PrefetchScalarGridSpec(
            num_scalar_prefetch=1,
            grid=(width // tile,),
            in_specs=[pl.BlockSpec((own_t, tile), lambda f, *_: (0, f))] * (2 * n_t)
            + [pl.BlockSpec((n_t // 2, rc, tile), lambda f, *_: (0, 0, f))] * (2 * chunks)
            + [whole(left.shape)],
            out_specs=pl.BlockSpec((TENANTS, 2 * R, tile), lambda f, *_: (0, 0, f)),
        ),
        compiler_params=pltpu.CompilerParams(vmem_limit_bytes=2 * VMEM_LIMIT),
        cost_estimate=NO_COST,
        name="gate_up_outer",
    )(meta, *[x for pair in factors for x in pair], *[x for both in sums for x in both], left)


def down_part_kernel(chunks, meta, *refs):
    sums, (hidden_ref, out_ref) = refs[:chunks], refs[chunks:]
    width = hidden_ref.shape[1]
    low = jnp.concatenate([both[meta[1] // 2][:, width:] for both in sums], axis=0)
    part = fdot(low, hidden_ref[...], TN)
    out_ref[...] = sum(part[e * R : (e + 1) * R] for e in range(TENANTS)).astype(jnp.bfloat16)


def down_part(meta, sums, hidden):
    return pl.pallas_call(
        functools.partial(down_part_kernel, len(sums)),
        out_shape=jax.ShapeDtypeStruct((R, hidden.shape[1]), jnp.bfloat16),
        in_specs=[SMEM] + [VMEM] * (len(sums) + 1),
        out_specs=VMEM,
        compiler_params=pltpu.CompilerParams(vmem_limit_bytes=VMEM_LIMIT),
        cost_estimate=NO_COST,
        name="down_part",
    )(meta, *sums, hidden)


def spread_kernel(tenant_at, rows, meta, *refs):
    parts, out_ref = refs[:-1], refs[-1]
    out_ref[...] = jnp.zeros_like(out_ref)
    at = 0
    for part in parts:
        for k in range(part.shape[0] // rows):
            tenant = tenant_at(at, meta)
            term = part[k * rows : (k + 1) * rows].astype(jnp.float32)
            out_ref[tenant] = out_ref[tenant] + ADAPTER_SCALE * term
            at += 1


def spread(meta, parts, tenant_at, rows, name):
    width = parts[0].shape[1]
    out = jax.ShapeDtypeStruct((TENANTS, rows, width), jnp.float32)
    tile = tile_of(width, 1024)
    return pl.pallas_call(
        functools.partial(spread_kernel, tenant_at, rows),
        out_shape=out,
        grid_spec=pltpu.PrefetchScalarGridSpec(
            num_scalar_prefetch=1,
            grid=(width // tile,),
            in_specs=[pl.BlockSpec((part.shape[0], tile), lambda f, *_: (0, f)) for part in parts],
            out_specs=pl.BlockSpec((TENANTS, rows, tile), lambda f, *_: (0, 0, f)),
        ),
        compiler_params=pltpu.CompilerParams(vmem_limit_bytes=VMEM_LIMIT),
        cost_estimate=NO_COST,
        name=name,
    )(meta, *parts)


def in_outer_kernel(n_dp, chunks, g, meta, *refs):
    shares, inputs, out_ref = refs[: n_dp * chunks], refs[n_dp * chunks : -1], refs[-1]
    out_ref[...] = jnp.zeros_like(out_ref)
    rows, width = inputs[0].shape
    own_t = rows // g
    rc = own_t // chunks
    for k in range(n_dp):
        block = lax.rem(meta[0] + n_dp - k, n_dp)
        queries = []
        for q in range(chunks):
            query = 0.0
            for s in range(n_dp):
                at = width + (s + n_dp - k) % n_dp * 2 * R
                query = query + shares[q * n_dp + s][:, at : at + 2 * R].astype(jnp.float32)
            queries.append(query.astype(jnp.bfloat16))
        low = [queries[q][j * rc : (j + 1) * rc] for j in range(g) for q in range(chunks)]
        total = fdot(jnp.concatenate(low, axis=0), inputs[k][...], TN)
        tenant = meta[2 + block]
        out_ref[tenant] = out_ref[tenant] + ADAPTER_SCALE * total


def in_outer(meta, shares, inputs, g):
    n_dp, width = len(inputs), inputs[0].shape[1]
    chunks = len(shares)
    shares = [share for there in shares for share in there]
    return pl.pallas_call(
        functools.partial(in_outer_kernel, n_dp, chunks, g),
        out_shape=jax.ShapeDtypeStruct((TENANTS, 2 * R, width), jnp.float32),
        in_specs=[SMEM] + [VMEM] * (len(shares) + n_dp),
        out_specs=VMEM,
        compiler_params=pltpu.CompilerParams(vmem_limit_bytes=VMEM_LIMIT),
        cost_estimate=NO_COST,
        name="in_outer",
    )(meta, *shares, *inputs)


def ring(n, by):
    return [(k, (k + by) % n) for k in range(n)]


def add32(*terms):
    return sum(term.astype(jnp.float32) for term in terms)


def after(value, *done):
    return lax.optimization_barrier((value,) + done)[0]


def per_device(
    layer_input,
    out_grad,
    gate_pre,
    up_pre,
    adapter_acts,
    gate_weight,
    up_weight,
    down_weight,
    adapter_a_gu,
    adapter_b_gu,
    adapter_a_down,
    adapter_b_down,
    block_tenant,
):
    n_dp, n_t = lax.axis_size("dp"), lax.axis_size("tensor")
    ny = n_t // 2
    z, t = lax.axis_index("dp"), lax.axis_index("tensor")
    own_rows, width = out_grad.shape
    own_t, hidden_width = gate_pre.shape
    tokens = adapter_acts.shape[0]
    g = own_rows // own_t
    assert own_rows == BLOCK and g * own_t == own_rows and n_t == 2 * ny and n_t == g * n_dp
    chunks, at = [], 0
    for share in SHARES:
        chunks.append((at, own_t * share // sum(SHARES)))
        at += chunks[-1][1]

    meta = jnp.concatenate([jnp.stack([z, t]).astype(jnp.int32), block_tenant])
    b_down = adapter_b_down.reshape(TENANTS * R, width)
    a_down = jnp.transpose(adapter_a_down, (0, 2, 1)).reshape(TENANTS * R, hidden_width)
    b_gu = adapter_b_gu.reshape(TENANTS * 2 * R, hidden_width)
    a_gu = jnp.transpose(adapter_a_gu, (0, 2, 1)).reshape(TENANTS * 2 * R, width)

    pair = [(k, k ^ 1) for k in range(n_t)]
    z_next = ring(n_dp, 1)

    stored = [gate_pre, up_pre]
    far_gates = [lax.ppermute(gate_pre, "tensor", ring(n_t, 2 * s)) for s in range(1, ny)]
    late_up = after(up_pre, *far_gates)
    far_stored = [[x, lax.ppermute(late_up, "tensor", ring(n_t, 2 * s + 2))] for s, x in enumerate(far_gates)]
    grads = [out_grad.reshape(g, own_t, width)]
    for step in range(n_dp - 1):
        piece = grads[-1] if step < n_dp - 2 else after(grads[-1], *far_gates)
        grads.append(lax.ppermute(piece, "dp", z_next))

    def factors_of(stored):
        gate_value, up_value = [x.astype(jnp.float32) for x in stored]
        sigmoid_value = jax.nn.sigmoid(gate_value)
        dgate = up_value * sigmoid_value * (1.0 + gate_value * (1.0 - sigmoid_value))
        dup = gate_value * sigmoid_value
        return [x.astype(jnp.bfloat16) for x in (dgate, dup, dup * up_value)]

    def exchange(keep, other):
        mine = add32(keep, other).astype(jnp.bfloat16)
        return mine, [lax.ppermute(mine, "tensor", ring(n_t, 2 * s)) for s in range(1, ny)]

    def total(mine, far):
        both = add32(mine, *far).astype(jnp.bfloat16)
        return [both, lax.ppermute(both, "tensor", pair)]

    def second(q, sums, done):
        sums = [after(sums[0], *done), sums[1]]
        outs = input_partial(meta, factors, q, sums, gate_weight, up_weight, b_gu, a_gu, n_dp, own_t)
        return [outs[0]] + [lax.ppermute(outs[r], "dp", ring(n_dp, r)) for r in range(1, n_dp)]

    def finish(there, rc):
        return add32(*[x[:, :width] for x in there]).astype(jnp.bfloat16).reshape(g, rc, width)

    (keep_a, keep_b), sends = hidden_partial(meta, grads, down_weight, b_down, a_down, n_t, chunks)
    inputs = [after(layer_input, grads[-1])]
    inputs.append(lax.ppermute(inputs[0], "dp", z_next))
    *near, hidden = factors_of([after(stored[0], keep_a), stored[1]])
    sends[0] = after(sends[0], *[x for there in far_stored for x in there])
    other_a, other_b = [lax.ppermute(send, "tensor", pair) for send in sends]
    mine_a, far_a = exchange(after(keep_a, near[0]), other_a)
    beside_stored = [lax.ppermute(after(x, mine_a), "tensor", pair) for x in stored]
    factors = [near, factors_of(beside_stored)[:2]]
    inputs.append(lax.ppermute(after(inputs[1], factors[1][0]), "dp", z_next))
    for there in far_stored:
        beside = [lax.ppermute(after(x, *beside_stored), "tensor", pair) for x in there]
        for both in (there, beside):
            factors.append(factors_of([after(both[0], mine_a, inputs[1]), both[1]])[:2])
    mine_b, far_b = exchange(after(keep_b, *far_a, *[pair[0] for pair in factors]), other_b)
    inputs[2] = after(inputs[2], mine_b)
    sums_a = total(after(mine_a, mine_b), far_a)
    for _ in range(n_dp - 3):
        inputs.append(lax.ppermute(after(inputs[-1], sums_a[0]), "dp", z_next))
    there_a = second(0, sums_a, (inputs[2],))
    sums_b = total(after(mine_b, there_a[0], inputs[-1]), far_b)
    there_b = second(1, sums_b, ())

    half_a = finish([after(x, there_b[0]) for x in there_a], chunks[0][1])
    acts = masked_acts(meta, after(adapter_acts.T, half_a), n_t)
    grad_b_down = down_outer(meta, grads, acts)
    a_part = down_part(meta, [sums_a[0], after(sums_b[0], half_a)], hidden)
    a_parts = [a_part] + [lax.ppermute(a_part, "tensor", ring(n_t, 2 * s)) for s in range(1, ny)]
    a_parts = [after(x, grad_b_down) for x in a_parts]
    a_parts += [lax.ppermute(x, "tensor", pair) for x in a_parts]
    grad_b_gu = gate_up_outer(meta, factors, [sums_a, sums_b], after(acts, grad_b_down))

    def column_tenant(p, m):
        owner = lax.rem(m[1] // 2 + ny - p % ny, ny) * 2
        return tenant_of(m, owner + (m[1] % 2 if p < ny else 1 - m[1] % 2), own_t)

    a_parts[0] = after(a_parts[0], grad_b_gu)
    grad_a_down = spread(meta, a_parts, column_tenant, R, "spread_a_down")
    there_b[0] = after(there_b[0], grad_a_down)
    grad_a_gu = in_outer(meta, [there_a, there_b], inputs, g)
    half_b = finish(there_b, chunks[1][1])
    block_input_grad = jnp.concatenate([half_a, half_b], axis=1).reshape(own_rows, width)
    return (
        block_input_grad,
        grad_a_gu.transpose(0, 2, 1),
        grad_b_gu,
        grad_a_down.transpose(0, 2, 1),
        grad_b_down,
    )


def solution(mesh):
    placed = (
        P(("groups", "dp"), "tensor"),
        P(("groups", "dp"), "tensor"),
        P(("groups", "tensor"), "dp"),
        P(("groups", "tensor"), "dp"),
        P("groups", None),
        P("tensor", "dp"),
        P("tensor", "dp"),
        P("dp", "tensor"),
        P(None, "tensor", None),
        P(None, None, "dp"),
        P(None, "dp", None),
        P(None, None, "tensor"),
        P("groups"),
    )
    return jax.shard_map(
        per_device,
        mesh=mesh,
        in_specs=placed,
        out_specs=(
            P(("groups", "dp"), "tensor"),
            P("groups", "tensor", None),
            P("groups", None, "dp"),
            P("groups", "dp", None),
            P("groups", None, "tensor"),
        ),
        check_vma=False,
    )
```

```python
import functools

import jax
import jax.numpy as jnp
from jax import lax
from jax.experimental import pallas as pl
from jax.experimental.pallas import tpu as pltpu
from jax.sharding import PartitionSpec as P

R = 16
TENANTS = 4
BLOCK = 128
SHARES = (1, 1)
LANES = 128
VMEM_LIMIT = 12 * 1024 * 1024
STREAM_LIMIT = 50 * 1024 * 1024

ADAPTER_SCALE = 2.0

NT = (((1,), (1,)), ((), ()))
NN = (((1,), (0,)), ((), ()))
TN = (((0,), (0,)), ((), ()))
ANY = pl.BlockSpec(memory_space=pl.ANY)
SMEM = pl.BlockSpec(memory_space=pltpu.SMEM)
VMEM = pl.BlockSpec(memory_space=pltpu.VMEM)
NO_COST = pl.CostEstimate(flops=1, bytes_accessed=1, transcendentals=0)


def fdot(lhs, rhs, dims):
    return lax.dot_general(lhs, rhs, dims, preferred_element_type=jnp.float32)


def tile_of(width, most):
    tile = most
    while width % tile:
        tile -= LANES
    return tile


def whole(shape):
    return pl.BlockSpec(shape, lambda *_: (0,) * len(shape))


def tenant_of(meta, owner, own_t):
    return meta[2 + (owner * own_t) // BLOCK]


def owner_of(p, y, c, ny):
    return lax.rem(y + ny - p // 2, ny) * 2 + (c if p % 2 == 0 else 1 - c)


def hidden_kernel(sizes, meta, *refs):
    n_dp, n_t, g, own_t, rc, tile = sizes
    ny = n_t // 2
    pieces, (w_ref, bd_ref, ad_ref, keep_ref, send_ref), refs = refs[:n_dp], refs[n_dp : n_dp + 5], refs[n_dp + 5 :]
    x_scr, p_scr, w_scr, w_sem = refs
    z, t = meta[0], meta[1]
    y, c = t // 2, t % 2
    hidden_width, width = w_ref.shape
    steps = hidden_width // tile

    def fetch(f):
        rows = pl.ds(pl.multiple_of(f * tile, LANES), tile)
        return pltpu.make_async_copy(w_ref.at[rows], w_scr.at[f], w_sem.at[f])

    for f in range(steps):
        fetch(f).start()

    for k in range(n_dp):
        for j in range(g):
            owner = lax.rem(z + (n_dp - k), n_dp) * g + j
            away = jnp.where(owner % 2 == c, 0, ny)
            x_scr[away + owner // 2] = pieces[k][j]
    proj = fdot(x_scr[...].reshape(n_t * rc, width), bd_ref[...], NT)
    lane = lax.broadcasted_iota(jnp.int32, (rc, TENANTS * R), 1) // R
    zeros = jnp.zeros((rc, LANES - TENANTS * R), jnp.bfloat16)
    for s in range(n_t):
        owner = (s % ny) * 2 + (c if s < ny else 1 - c)
        own = jnp.where(lane == tenant_of(meta, owner, own_t), proj[s * rc : (s + 1) * rc], 0.0)
        p_scr[s * rc : (s + 1) * rc, :] = (ADAPTER_SCALE * own).astype(jnp.bfloat16)
        out = keep_ref if s < ny else send_ref
        out[s % ny, :, hidden_width:] = jnp.concatenate([own.astype(jnp.bfloat16), zeros], axis=1)

    def body(step, carry):
        at = pl.ds(pl.multiple_of(step * tile, LANES), tile)
        fetch(step).wait()
        acc = fdot(x_scr[...].reshape(n_t * rc, width), w_scr[step], NT)
        acc = (acc + fdot(p_scr[...], ad_ref[:, at], NN)).astype(jnp.bfloat16).reshape(n_t, rc, tile)
        keep_ref[:, :, at] = acc[:ny]
        send_ref[:, :, at] = acc[ny:]
        return carry

    lax.fori_loop(0, steps, body, 0)


def hidden_partial(meta, pieces, down_weight, b_down, a_down, n_t, own_t):
    n_dp = len(pieces)
    g, rc, width = pieces[0].shape
    ny = n_t // 2
    hidden_width = down_weight.shape[0]
    tile = tile_of(hidden_width, 512)
    low = TENANTS * R
    out = jax.ShapeDtypeStruct((ny, rc, hidden_width + LANES), jnp.bfloat16)
    return pl.pallas_call(
        functools.partial(hidden_kernel, (n_dp, n_t, g, own_t, rc, tile)),
        out_shape=(out, out),
        in_specs=[SMEM] + [VMEM] * n_dp + [ANY] + [VMEM] * 2,
        out_specs=[VMEM] * 2,
        scratch_shapes=[
            pltpu.VMEM((n_t, rc, width), jnp.bfloat16),
            pltpu.VMEM((n_t * rc, low), jnp.bfloat16),
            pltpu.VMEM((hidden_width // tile, tile, width), jnp.bfloat16),
            pltpu.SemaphoreType.DMA((hidden_width // tile,)),
        ],
        compiler_params=pltpu.CompilerParams(vmem_limit_bytes=STREAM_LIMIT),
        cost_estimate=NO_COST,
        name="hidden_partial",
    )(meta, *pieces, down_weight, b_down, a_down)


def grads_of(total, factors):
    total = total.astype(jnp.float32)
    return [(total * factor[...].astype(jnp.float32)).astype(jnp.bfloat16) for factor in factors]


def input_kernel(sizes, meta, *refs):
    n_dp, n_t, g, own_t, rc, q, tile = sizes
    ny = n_t // 2
    factors, refs = [refs[2 * p : 2 * p + 2] for p in range(n_t)], refs[2 * n_t :]
    sums, (gw_ref, uw_ref, b_ref, a_ref) = refs[:2], refs[2:6]
    outs, (g_scr, u_scr, q_scr, w_scr, w_sem) = refs[6 : 6 + n_dp], refs[6 + n_dp :]
    z, t = meta[0], meta[1]
    y, c = t // 2, t % 2
    rows = n_t * rc
    width, hidden_width = gw_ref.shape
    steps = width // tile

    def fetch(f):
        at = pl.ds(pl.multiple_of(f * tile, LANES), tile)
        return [
            pltpu.make_async_copy(w.at[at], w_scr.at[f, k], w_sem.at[f, k]) for k, w in enumerate((gw_ref, uw_ref))
        ]

    for f in range(steps):
        for copy in fetch(f):
            copy.start()

    for p in range(n_t):
        owner = owner_of(p, y, c, ny)
        slot = lax.rem(owner // g + n_dp - z, n_dp) * g + owner % g
        mine = [factor[q * rc : (q + 1) * rc, :] for factor in factors[p]]
        g_scr[slot], u_scr[slot] = grads_of(sums[p % 2][owner // 2, :, :hidden_width], mine)
    q_gate = fdot(g_scr[...].reshape(rows, hidden_width), b_ref[...], NT)
    q_up = fdot(u_scr[...].reshape(rows, hidden_width), b_ref[...], NT)
    lane = lax.broadcasted_iota(jnp.int32, (rc, 2 * R * TENANTS), 1)
    shares = []
    for r in range(n_dp):
        share = []
        for j in range(g):
            at = slice((r * g + j) * rc, (r * g + j + 1) * rc)
            tenant = tenant_of(meta, lax.rem(z + r, n_dp) * g + j, own_t)
            mine = jnp.where(lane % (2 * R) < R, q_gate[at], q_up[at])
            mine = jnp.where(lane // (2 * R) == tenant, mine, 0.0)
            q_scr[at, :] = (ADAPTER_SCALE * mine).astype(jnp.bfloat16)
            share.append(sum(mine[:, e * 2 * R : (e + 1) * 2 * R] for e in range(TENANTS)))
        shares.append(jnp.concatenate(share, axis=0))
    share = jnp.concatenate(shares, axis=1).astype(jnp.bfloat16)
    for r in range(n_dp):
        outs[r][:, width:] = share

    def body(step, carry):
        at = pl.ds(pl.multiple_of(step * tile, LANES), tile)
        for copy in fetch(step):
            copy.wait()
        acc = fdot(g_scr[...].reshape(rows, hidden_width), w_scr[step, 0], NT)
        acc = acc + fdot(u_scr[...].reshape(rows, hidden_width), w_scr[step, 1], NT)
        acc = (acc + fdot(q_scr[...], a_ref[:, at], NN)).astype(jnp.bfloat16)
        for r in range(n_dp):
            outs[r][:, at] = acc[r * g * rc : (r + 1) * g * rc]
        return carry

    lax.fori_loop(0, steps, body, 0)


def input_partial(meta, factors, q, sums, gate_weight, up_weight, b_gu, a_gu, n_dp, own_t):
    n_t = len(factors)
    ny, rc, _ = sums[0].shape
    g = n_t // n_dp
    width, hidden_width = gate_weight.shape
    tile = tile_of(width, 256)
    low = 2 * R * TENANTS
    rows = n_t * rc
    outs = [jax.ShapeDtypeStruct((g * rc, width + n_dp * 2 * R), jnp.bfloat16)] * n_dp
    return pl.pallas_call(
        functools.partial(input_kernel, (n_dp, n_t, g, own_t, rc, q, tile)),
        out_shape=outs,
        in_specs=[SMEM] + [VMEM] * (2 * n_t + 2) + [ANY] * 2 + [VMEM] * 2,
        out_specs=[VMEM] * n_dp,
        scratch_shapes=[
            pltpu.VMEM((n_t, rc, hidden_width), jnp.bfloat16),
            pltpu.VMEM((n_t, rc, hidden_width), jnp.bfloat16),
            pltpu.VMEM((rows, low), jnp.bfloat16),
            pltpu.VMEM((width // tile, 2, tile, hidden_width), jnp.bfloat16),
            pltpu.SemaphoreType.DMA((width // tile, 2)),
        ],
        compiler_params=pltpu.CompilerParams(vmem_limit_bytes=STREAM_LIMIT),
        cost_estimate=NO_COST,
        name="input_partial",
    )(meta, *[x for pair in factors for x in pair], *sums, gate_weight, up_weight, b_gu, a_gu)


def acts_kernel(meta, acts_ref, out_ref):
    layers, n_t, _, own_t = out_ref.shape
    for owner in range(n_t):
        tenant = tenant_of(meta, owner, own_t)
        for layer in range(layers):
            mine = acts_ref[layer * R : (layer + 1) * R, owner * own_t : (owner + 1) * own_t]
            for e in range(TENANTS):
                chosen = jnp.where(tenant == e, mine.astype(jnp.float32), 0.0)
                out_ref[layer, owner, e * R : (e + 1) * R, :] = chosen.astype(jnp.bfloat16)


def masked_acts(meta, acts, n_t):
    return pl.pallas_call(
        acts_kernel,
        out_shape=jax.ShapeDtypeStruct((3, n_t, TENANTS * R, acts.shape[1] // n_t), jnp.bfloat16),
        in_specs=[SMEM, VMEM],
        out_specs=VMEM,
        compiler_params=pltpu.CompilerParams(vmem_limit_bytes=VMEM_LIMIT),
        cost_estimate=NO_COST,
        name="masked_acts",
    )(meta, acts)


def left_of(left_ref, layer, owners):
    return jnp.concatenate([left_ref[layer, owner] for owner in owners], axis=1)


def down_outer_kernel(n_dp, g, chunks, meta, *refs):
    pieces, (left_ref, out_ref) = refs[: n_dp * chunks], refs[n_dp * chunks :]
    owners = [lax.rem(meta[0] + (n_dp - k), n_dp) * g + j for k in range(n_dp) for j in range(g)]
    right = [pieces[q * n_dp + k][j] for k in range(n_dp) for j in range(g) for q in range(chunks)]
    out = ADAPTER_SCALE * fdot(left_of(left_ref, 2, owners), jnp.concatenate(right, axis=0), NN)
    out_ref[...] = out.reshape(out_ref.shape)


def down_outer(meta, grads, left):
    n_dp, chunks = len(grads[0]), len(grads)
    pieces = [piece for pieces in grads for piece in pieces]
    g, _, width = pieces[0].shape
    tile = tile_of(width, 512)
    return pl.pallas_call(
        functools.partial(down_outer_kernel, n_dp, g, chunks),
        out_shape=jax.ShapeDtypeStruct((TENANTS, R, width), jnp.float32),
        grid_spec=pltpu.PrefetchScalarGridSpec(
            num_scalar_prefetch=1,
            grid=(width // tile,),
            in_specs=[
                pl.BlockSpec(piece.shape[:2] + (tile,), lambda f, *_: (0, 0, f)) for piece in pieces
            ]
            + [whole(left.shape)],
            out_specs=pl.BlockSpec((TENANTS, R, tile), lambda f, *_: (0, 0, f)),
        ),
        compiler_params=pltpu.CompilerParams(vmem_limit_bytes=VMEM_LIMIT),
        cost_estimate=NO_COST,
        name="down_outer",
    )(meta, *pieces, left)


def gate_up_outer_kernel(n_t, chunks, meta, *refs):
    ny = n_t // 2
    factors, refs = [refs[2 * p : 2 * p + 2] for p in range(n_t)], refs[2 * n_t :]
    sums, (left_ref, out_ref) = [refs[2 * q : 2 * q + 2] for q in range(chunks)], refs[2 * chunks :]
    y, c = meta[1] // 2, meta[1] % 2
    owners = [owner_of(p, y, c, ny) for p in range(n_t)]
    grads = []
    for p in range(n_t):
        total = jnp.concatenate([both[p % 2][owners[p] // 2] for both in sums], axis=0)
        grads.append(grads_of(total, factors[p]))
    for layer in range(2):
        right = jnp.concatenate([grad[layer] for grad in grads], axis=0)
        out = ADAPTER_SCALE * fdot(left_of(left_ref, layer, owners), right, NN)
        out_ref[:, layer * R : (layer + 1) * R, :] = out.reshape(TENANTS, R, out.shape[1])


def gate_up_outer(meta, factors, sums, left):
    n_t, chunks = len(factors), len(sums)
    rc = sums[0][0].shape[1]
    own_t, width = factors[0][0].shape
    tile = tile_of(width, 896)
    return pl.pallas_call(
        functools.partial(gate_up_outer_kernel, n_t, chunks),
        out_shape=jax.ShapeDtypeStruct((TENANTS, 2 * R, width), jnp.float32),
        grid_spec=pltpu.PrefetchScalarGridSpec(
            num_scalar_prefetch=1,
            grid=(width // tile,),
            in_specs=[pl.BlockSpec((own_t, tile), lambda f, *_: (0, f))] * (2 * n_t)
            + [pl.BlockSpec((n_t // 2, rc, tile), lambda f, *_: (0, 0, f))] * (2 * chunks)
            + [whole(left.shape)],
            out_specs=pl.BlockSpec((TENANTS, 2 * R, tile), lambda f, *_: (0, 0, f)),
        ),
        compiler_params=pltpu.CompilerParams(vmem_limit_bytes=2 * VMEM_LIMIT),
        cost_estimate=NO_COST,
        name="gate_up_outer",
    )(meta, *[x for pair in factors for x in pair], *[x for both in sums for x in both], left)


def down_part_kernel(chunks, meta, *refs):
    sums, (hidden_ref, out_ref) = refs[:chunks], refs[chunks:]
    width = hidden_ref.shape[1]
    low = jnp.concatenate([both[meta[1] // 2][:, width:] for both in sums], axis=0)
    part = fdot(low, hidden_ref[...], TN)
    out_ref[...] = sum(part[e * R : (e + 1) * R] for e in range(TENANTS)).astype(jnp.bfloat16)


def down_part(meta, sums, hidden):
    return pl.pallas_call(
        functools.partial(down_part_kernel, len(sums)),
        out_shape=jax.ShapeDtypeStruct((R, hidden.shape[1]), jnp.bfloat16),
        in_specs=[SMEM] + [VMEM] * (len(sums) + 1),
        out_specs=VMEM,
        compiler_params=pltpu.CompilerParams(vmem_limit_bytes=VMEM_LIMIT),
        cost_estimate=NO_COST,
        name="down_part",
    )(meta, *sums, hidden)


def spread_kernel(tenant_at, rows, meta, *refs):
    parts, out_ref = refs[:-1], refs[-1]
    out_ref[...] = jnp.zeros_like(out_ref)
    at = 0
    for part in parts:
        for k in range(part.shape[0] // rows):
            tenant = tenant_at(at, meta)
            term = part[k * rows : (k + 1) * rows].astype(jnp.float32)
            out_ref[tenant] = out_ref[tenant] + ADAPTER_SCALE * term
            at += 1


def spread(meta, parts, tenant_at, rows, name):
    width = parts[0].shape[1]
    out = jax.ShapeDtypeStruct((TENANTS, rows, width), jnp.float32)
    tile = tile_of(width, 1024)
    return pl.pallas_call(
        functools.partial(spread_kernel, tenant_at, rows),
        out_shape=out,
        grid_spec=pltpu.PrefetchScalarGridSpec(
            num_scalar_prefetch=1,
            grid=(width // tile,),
            in_specs=[pl.BlockSpec((part.shape[0], tile), lambda f, *_: (0, f)) for part in parts],
            out_specs=pl.BlockSpec((TENANTS, rows, tile), lambda f, *_: (0, 0, f)),
        ),
        compiler_params=pltpu.CompilerParams(vmem_limit_bytes=VMEM_LIMIT),
        cost_estimate=NO_COST,
        name=name,
    )(meta, *parts)


def in_outer_kernel(n_dp, chunks, g, meta, *refs):
    shares, inputs, out_ref = refs[: n_dp * chunks], refs[n_dp * chunks : -1], refs[-1]
    out_ref[...] = jnp.zeros_like(out_ref)
    rows, width = inputs[0].shape
    own_t = rows // g
    rc = own_t // chunks
    for k in range(n_dp):
        block = lax.rem(meta[0] + n_dp - k, n_dp)
        queries = []
        for q in range(chunks):
            query = 0.0
            for s in range(n_dp):
                at = width + (s + n_dp - k) % n_dp * 2 * R
                query = query + shares[q * n_dp + s][:, at : at + 2 * R].astype(jnp.float32)
            queries.append(query.astype(jnp.bfloat16))
        low = [queries[q][j * rc : (j + 1) * rc] for j in range(g) for q in range(chunks)]
        total = fdot(jnp.concatenate(low, axis=0), inputs[k][...], TN)
        tenant = meta[2 + block]
        out_ref[tenant] = out_ref[tenant] + ADAPTER_SCALE * total


def in_outer(meta, shares, inputs, g):
    n_dp, width = len(inputs), inputs[0].shape[1]
    chunks = len(shares)
    shares = [share for there in shares for share in there]
    return pl.pallas_call(
        functools.partial(in_outer_kernel, n_dp, chunks, g),
        out_shape=jax.ShapeDtypeStruct((TENANTS, 2 * R, width), jnp.float32),
        in_specs=[SMEM] + [VMEM] * (len(shares) + n_dp),
        out_specs=VMEM,
        compiler_params=pltpu.CompilerParams(vmem_limit_bytes=VMEM_LIMIT),
        cost_estimate=NO_COST,
        name="in_outer",
    )(meta, *shares, *inputs)


def ring(n, by):
    return [(k, (k + by) % n) for k in range(n)]


def add32(*terms):
    return sum(term.astype(jnp.float32) for term in terms)


def after(value, *done):
    return lax.optimization_barrier((value,) + done)[0]


def per_device(
    layer_input,
    out_grad,
    gate_pre,
    up_pre,
    adapter_acts,
    gate_weight,
    up_weight,
    down_weight,
    adapter_a_gu,
    adapter_b_gu,
    adapter_a_down,
    adapter_b_down,
    block_tenant,
):
    n_dp, n_t = lax.axis_size("dp"), lax.axis_size("tensor")
    ny = n_t // 2
    z, t = lax.axis_index("dp"), lax.axis_index("tensor")
    own_rows, width = out_grad.shape
    own_t, hidden_width = gate_pre.shape
    tokens = adapter_acts.shape[0]
    g = own_rows // own_t
    assert own_rows == BLOCK and g * own_t == own_rows and n_t == 2 * ny and n_t == g * n_dp
    chunks, at = [], 0
    for share in SHARES:
        chunks.append((at, own_t * share // sum(SHARES)))
        at += chunks[-1][1]

    meta = jnp.concatenate([jnp.stack([z, t]).astype(jnp.int32), block_tenant])
    b_down = adapter_b_down.reshape(TENANTS * R, width)
    a_down = jnp.transpose(adapter_a_down, (0, 2, 1)).reshape(TENANTS * R, hidden_width)
    b_gu = adapter_b_gu.reshape(TENANTS * 2 * R, hidden_width)
    a_gu = jnp.transpose(adapter_a_gu, (0, 2, 1)).reshape(TENANTS * 2 * R, width)

    pair = [(k, k ^ 1) for k in range(n_t)]
    z_next = ring(n_dp, 1)

    stored = [gate_pre, up_pre]
    far_stored = [[lax.ppermute(x, "tensor", ring(n_t, 2 * s)) for x in stored] for s in range(1, ny)]
    grads = [[out_grad.reshape(g, own_t, width)[:, at : at + rc]] for at, rc in chunks]
    for _ in range(n_dp - 1):
        grads[0].append(lax.ppermute(grads[0][-1], "dp", z_next))
    grads[1][0] = after(grads[1][0], grads[0][2])
    for _ in range(n_dp - 1):
        grads[1].append(lax.ppermute(grads[1][-1], "dp", z_next))

    def first(q, done):
        pieces = [after(grads[q][0], *done)] + grads[q][1:]
        keep, send = hidden_partial(meta, pieces, down_weight, b_down, a_down, n_t, own_t)
        return keep, send

    def factors_of(stored):
        gate_value, up_value = [x.astype(jnp.float32) for x in stored]
        sigmoid_value = jax.nn.sigmoid(gate_value)
        dgate = up_value * sigmoid_value * (1.0 + gate_value * (1.0 - sigmoid_value))
        dup = gate_value * sigmoid_value
        return [x.astype(jnp.bfloat16) for x in (dgate, dup, dup * up_value)]

    def exchange(keep, other):
        mine = add32(keep, other).astype(jnp.bfloat16)
        return mine, [lax.ppermute(mine, "tensor", ring(n_t, 2 * s)) for s in range(1, ny)]

    def total(mine, far):
        both = add32(mine, *far).astype(jnp.bfloat16)
        return [both, lax.ppermute(both, "tensor", pair)]

    def second(q, sums, done):
        sums = [after(sums[0], *done), sums[1]]
        outs = input_partial(meta, factors, q, sums, gate_weight, up_weight, b_gu, a_gu, n_dp, own_t)
        return [outs[0]] + [lax.ppermute(outs[r], "dp", ring(n_dp, r)) for r in range(1, n_dp)]

    def finish(there, rc):
        return add32(*[x[:, :width] for x in there]).astype(jnp.bfloat16).reshape(g, rc, width)

    keep_a, send_a = first(0, (grads[1][1],))
    stored[0] = after(stored[0], keep_a)
    *near, hidden = factors_of(stored)
    other_a = lax.ppermute(after(send_a, grads[1][n_dp - 2], *[x for there in far_stored for x in there]), "tensor", pair)
    mine_a, far_a = exchange(after(keep_a, near[0]), other_a)
    beside_stored = [lax.ppermute(after(x, mine_a), "tensor", pair) for x in stored]
    keep_b, send_b = first(1, (mine_a,))
    other_b = lax.ppermute(send_b, "tensor", pair)
    beside_stored[0] = after(beside_stored[0], keep_b)
    factors = [near, factors_of(beside_stored)[:2]]
    for there in far_stored:
        beside = [lax.ppermute(x, "tensor", pair) for x in [after(x, *beside_stored) for x in there]]
        for both in (there, beside):
            factors.append(factors_of([after(both[0], keep_b), both[1]])[:2])
    mine_b, far_b = exchange(after(keep_b, *far_a, *[pair[0] for pair in factors]), other_b)
    inputs = [after(layer_input, grads[1][-1], mine_a)] + [None] * (n_dp - 1)
    inputs[1] = lax.ppermute(inputs[0], "dp", z_next)
    inputs[-1] = lax.ppermute(inputs[0], "dp", ring(n_dp, -1))
    for k in range(2, n_dp // 2 + 1):
        inputs[k] = lax.ppermute(inputs[k - 1], "dp", z_next)
    for k in range(2, (n_dp + 1) // 2):
        inputs[-k] = lax.ppermute(inputs[1 - k], "dp", ring(n_dp, -1))
    sums_a = total(after(mine_a, mine_b), far_a)
    there_a = second(0, sums_a, (inputs[1],))
    sums_b = total(after(mine_b, there_a[0], inputs[n_dp // 2], inputs[-1]), far_b)
    there_b = second(1, sums_b, ())

    half_a = finish([after(x, there_b[0]) for x in there_a], chunks[0][1])
    acts = masked_acts(meta, after(adapter_acts.T, half_a), n_t)
    grad_b_down = down_outer(meta, grads, acts)
    a_part = down_part(meta, [sums_a[0], after(sums_b[0], half_a)], hidden)
    a_parts = [a_part] + [lax.ppermute(a_part, "tensor", ring(n_t, 2 * s)) for s in range(1, ny)]
    a_parts = [after(x, grad_b_down) for x in a_parts]
    a_parts += [lax.ppermute(x, "tensor", pair) for x in a_parts]
    grad_b_gu = gate_up_outer(meta, factors, [sums_a, sums_b], after(acts, grad_b_down))

    def column_tenant(p, m):
        owner = lax.rem(m[1] // 2 + ny - p % ny, ny) * 2
        return tenant_of(m, owner + (m[1] % 2 if p < ny else 1 - m[1] % 2), own_t)

    a_parts[0] = after(a_parts[0], grad_b_gu)
    grad_a_down = spread(meta, a_parts, column_tenant, R, "spread_a_down")
    there_b[0] = after(there_b[0], grad_a_down)
    grad_a_gu = in_outer(meta, [there_a, there_b], inputs, g)
    half_b = finish(there_b, chunks[1][1])
    block_input_grad = jnp.concatenate([half_a, half_b], axis=1).reshape(own_rows, width)
    return (
        block_input_grad,
        grad_a_gu.transpose(0, 2, 1),
        grad_b_gu,
        grad_a_down.transpose(0, 2, 1),
        grad_b_down,
    )


def solution(mesh):
    placed = (
        P(("groups", "dp"), "tensor"),
        P(("groups", "dp"), "tensor"),
        P(("groups", "tensor"), "dp"),
        P(("groups", "tensor"), "dp"),
        P("groups", None),
        P("tensor", "dp"),
        P("tensor", "dp"),
        P("dp", "tensor"),
        P(None, "tensor", None),
        P(None, None, "dp"),
        P(None, "dp", None),
        P(None, None, "tensor"),
        P("groups"),
    )
    return jax.shard_map(
        per_device,
        mesh=mesh,
        in_specs=placed,
        out_specs=(
            P(("groups", "dp"), "tensor"),
            P("groups", "tensor", None),
            P("groups", None, "dp"),
            P("groups", "dp", None),
            P("groups", None, "tensor"),
        ),
        check_vma=False,
    )
```

```python
import functools

import jax
import jax.numpy as jnp
from jax import lax
from jax.experimental import pallas as pl
from jax.experimental.pallas import tpu as pltpu
from jax.sharding import PartitionSpec as P

R = 16
TENANTS = 4
BLOCK = 128
SHARES = (1, 1)
LANES = 128
VMEM_LIMIT = 12 * 1024 * 1024
STREAM_LIMIT = 50 * 1024 * 1024

ADAPTER_SCALE = 2.0

NT = (((1,), (1,)), ((), ()))
NN = (((1,), (0,)), ((), ()))
TN = (((0,), (0,)), ((), ()))
ANY = pl.BlockSpec(memory_space=pl.ANY)
SMEM = pl.BlockSpec(memory_space=pltpu.SMEM)
VMEM = pl.BlockSpec(memory_space=pltpu.VMEM)
NO_COST = pl.CostEstimate(flops=1, bytes_accessed=1, transcendentals=0)


def fdot(lhs, rhs, dims):
    return lax.dot_general(lhs, rhs, dims, preferred_element_type=jnp.float32)


def tile_of(width, most):
    tile = most
    while width % tile:
        tile -= LANES
    return tile


def whole(shape):
    return pl.BlockSpec(shape, lambda *_: (0,) * len(shape))


def tenant_of(meta, owner, own_t):
    return meta[2 + (owner * own_t) // BLOCK]


def owner_of(p, y, c, ny):
    return lax.rem(y + ny - p // 2, ny) * 2 + (c if p % 2 == 0 else 1 - c)


def hidden_kernel(sizes, meta, *refs):
    n_dp, n_t, g, own_t, rc, tile = sizes
    ny = n_t // 2
    pieces, (w_ref, bd_ref, ad_ref, keep_ref, send_ref), refs = refs[:n_dp], refs[n_dp : n_dp + 5], refs[n_dp + 5 :]
    x_scr, p_scr, w_scr, w_sem = refs
    z, t = meta[0], meta[1]
    y, c = t // 2, t % 2
    hidden_width, width = w_ref.shape
    steps = hidden_width // tile

    def fetch(f):
        rows = pl.ds(pl.multiple_of(f * tile, LANES), tile)
        return pltpu.make_async_copy(w_ref.at[rows], w_scr.at[f], w_sem.at[f])

    for f in range(steps):
        fetch(f).start()

    for k in range(n_dp):
        for j in range(g):
            owner = lax.rem(z + (n_dp - k), n_dp) * g + j
            away = jnp.where(owner % 2 == c, 0, ny)
            x_scr[away + owner // 2] = pieces[k][j]
    proj = fdot(x_scr[...].reshape(n_t * rc, width), bd_ref[...], NT)
    lane = lax.broadcasted_iota(jnp.int32, (rc, TENANTS * R), 1) // R
    zeros = jnp.zeros((rc, LANES - TENANTS * R), jnp.bfloat16)
    for s in range(n_t):
        owner = (s % ny) * 2 + (c if s < ny else 1 - c)
        own = jnp.where(lane == tenant_of(meta, owner, own_t), proj[s * rc : (s + 1) * rc], 0.0)
        p_scr[s * rc : (s + 1) * rc, :] = (ADAPTER_SCALE * own).astype(jnp.bfloat16)
        out = keep_ref if s < ny else send_ref
        out[s % ny, :, hidden_width:] = jnp.concatenate([own.astype(jnp.bfloat16), zeros], axis=1)

    def body(step, carry):
        at = pl.ds(pl.multiple_of(step * tile, LANES), tile)
        fetch(step).wait()
        acc = fdot(x_scr[...].reshape(n_t * rc, width), w_scr[step], NT)
        acc = (acc + fdot(p_scr[...], ad_ref[:, at], NN)).astype(jnp.bfloat16).reshape(n_t, rc, tile)
        keep_ref[:, :, at] = acc[:ny]
        send_ref[:, :, at] = acc[ny:]
        return carry

    lax.fori_loop(0, steps, body, 0)


def hidden_partial(meta, pieces, down_weight, b_down, a_down, n_t, own_t):
    n_dp = len(pieces)
    g, rc, width = pieces[0].shape
    ny = n_t // 2
    hidden_width = down_weight.shape[0]
    tile = tile_of(hidden_width, 512)
    low = TENANTS * R
    out = jax.ShapeDtypeStruct((ny, rc, hidden_width + LANES), jnp.bfloat16)
    return pl.pallas_call(
        functools.partial(hidden_kernel, (n_dp, n_t, g, own_t, rc, tile)),
        out_shape=(out, out),
        in_specs=[SMEM] + [VMEM] * n_dp + [ANY] + [VMEM] * 2,
        out_specs=[VMEM] * 2,
        scratch_shapes=[
            pltpu.VMEM((n_t, rc, width), jnp.bfloat16),
            pltpu.VMEM((n_t * rc, low), jnp.bfloat16),
            pltpu.VMEM((hidden_width // tile, tile, width), jnp.bfloat16),
            pltpu.SemaphoreType.DMA((hidden_width // tile,)),
        ],
        compiler_params=pltpu.CompilerParams(vmem_limit_bytes=STREAM_LIMIT),
        cost_estimate=NO_COST,
        name="hidden_partial",
    )(meta, *pieces, down_weight, b_down, a_down)


def grads_of(total, factors):
    total = total.astype(jnp.float32)
    return [(total * factor[...].astype(jnp.float32)).astype(jnp.bfloat16) for factor in factors]


def input_kernel(sizes, meta, *refs):
    n_dp, n_t, g, own_t, rc, q, tile = sizes
    ny = n_t // 2
    factors, refs = [refs[2 * p : 2 * p + 2] for p in range(n_t)], refs[2 * n_t :]
    sums, (gw_ref, uw_ref, b_ref, a_ref) = refs[:2], refs[2:6]
    outs, (g_scr, u_scr, q_scr, w_scr, w_sem) = refs[6 : 6 + n_dp], refs[6 + n_dp :]
    z, t = meta[0], meta[1]
    y, c = t // 2, t % 2
    rows = n_t * rc
    width, hidden_width = gw_ref.shape
    steps = width // tile

    def fetch(f):
        at = pl.ds(pl.multiple_of(f * tile, LANES), tile)
        return [
            pltpu.make_async_copy(w.at[at], w_scr.at[f, k], w_sem.at[f, k]) for k, w in enumerate((gw_ref, uw_ref))
        ]

    for f in range(steps):
        for copy in fetch(f):
            copy.start()

    for p in range(n_t):
        owner = owner_of(p, y, c, ny)
        slot = lax.rem(owner // g + n_dp - z, n_dp) * g + owner % g
        mine = [factor[q * rc : (q + 1) * rc, :] for factor in factors[p]]
        g_scr[slot], u_scr[slot] = grads_of(sums[p % 2][owner // 2, :, :hidden_width], mine)
    q_gate = fdot(g_scr[...].reshape(rows, hidden_width), b_ref[...], NT)
    q_up = fdot(u_scr[...].reshape(rows, hidden_width), b_ref[...], NT)
    lane = lax.broadcasted_iota(jnp.int32, (rc, 2 * R * TENANTS), 1)
    shares = []
    for r in range(n_dp):
        share = []
        for j in range(g):
            at = slice((r * g + j) * rc, (r * g + j + 1) * rc)
            tenant = tenant_of(meta, lax.rem(z + r, n_dp) * g + j, own_t)
            mine = jnp.where(lane % (2 * R) < R, q_gate[at], q_up[at])
            mine = jnp.where(lane // (2 * R) == tenant, mine, 0.0)
            q_scr[at, :] = (ADAPTER_SCALE * mine).astype(jnp.bfloat16)
            share.append(sum(mine[:, e * 2 * R : (e + 1) * 2 * R] for e in range(TENANTS)))
        shares.append(jnp.concatenate(share, axis=0))
    share = jnp.concatenate(shares, axis=1).astype(jnp.bfloat16)
    for r in range(n_dp):
        outs[r][:, width:] = share

    def body(step, carry):
        at = pl.ds(pl.multiple_of(step * tile, LANES), tile)
        for copy in fetch(step):
            copy.wait()
        acc = fdot(g_scr[...].reshape(rows, hidden_width), w_scr[step, 0], NT)
        acc = acc + fdot(u_scr[...].reshape(rows, hidden_width), w_scr[step, 1], NT)
        acc = (acc + fdot(q_scr[...], a_ref[:, at], NN)).astype(jnp.bfloat16)
        for r in range(n_dp):
            outs[r][:, at] = acc[r * g * rc : (r + 1) * g * rc]
        return carry

    lax.fori_loop(0, steps, body, 0)


def input_partial(meta, factors, q, sums, gate_weight, up_weight, b_gu, a_gu, n_dp, own_t):
    n_t = len(factors)
    ny, rc, _ = sums[0].shape
    g = n_t // n_dp
    width, hidden_width = gate_weight.shape
    tile = tile_of(width, 256)
    low = 2 * R * TENANTS
    rows = n_t * rc
    outs = [jax.ShapeDtypeStruct((g * rc, width + n_dp * 2 * R), jnp.bfloat16)] * n_dp
    return pl.pallas_call(
        functools.partial(input_kernel, (n_dp, n_t, g, own_t, rc, q, tile)),
        out_shape=outs,
        in_specs=[SMEM] + [VMEM] * (2 * n_t + 2) + [ANY] * 2 + [VMEM] * 2,
        out_specs=[VMEM] * n_dp,
        scratch_shapes=[
            pltpu.VMEM((n_t, rc, hidden_width), jnp.bfloat16),
            pltpu.VMEM((n_t, rc, hidden_width), jnp.bfloat16),
            pltpu.VMEM((rows, low), jnp.bfloat16),
            pltpu.VMEM((width // tile, 2, tile, hidden_width), jnp.bfloat16),
            pltpu.SemaphoreType.DMA((width // tile, 2)),
        ],
        compiler_params=pltpu.CompilerParams(vmem_limit_bytes=STREAM_LIMIT),
        cost_estimate=NO_COST,
        name="input_partial",
    )(meta, *[x for pair in factors for x in pair], *sums, gate_weight, up_weight, b_gu, a_gu)


def acts_kernel(meta, acts_ref, out_ref):
    layers, n_t, _, own_t = out_ref.shape
    for owner in range(n_t):
        tenant = tenant_of(meta, owner, own_t)
        for layer in range(layers):
            mine = acts_ref[layer * R : (layer + 1) * R, owner * own_t : (owner + 1) * own_t]
            for e in range(TENANTS):
                chosen = jnp.where(tenant == e, mine.astype(jnp.float32), 0.0)
                out_ref[layer, owner, e * R : (e + 1) * R, :] = chosen.astype(jnp.bfloat16)


def masked_acts(meta, acts, n_t):
    return pl.pallas_call(
        acts_kernel,
        out_shape=jax.ShapeDtypeStruct((3, n_t, TENANTS * R, acts.shape[1] // n_t), jnp.bfloat16),
        in_specs=[SMEM, VMEM],
        out_specs=VMEM,
        compiler_params=pltpu.CompilerParams(vmem_limit_bytes=VMEM_LIMIT),
        cost_estimate=NO_COST,
        name="masked_acts",
    )(meta, acts)


def left_of(left_ref, layer, owners):
    return jnp.concatenate([left_ref[layer, owner] for owner in owners], axis=1)


def down_outer_kernel(n_dp, g, chunks, meta, *refs):
    pieces, (left_ref, out_ref) = refs[: n_dp * chunks], refs[n_dp * chunks :]
    owners = [lax.rem(meta[0] + (n_dp - k), n_dp) * g + j for k in range(n_dp) for j in range(g)]
    right = [pieces[q * n_dp + k][j] for k in range(n_dp) for j in range(g) for q in range(chunks)]
    out = ADAPTER_SCALE * fdot(left_of(left_ref, 2, owners), jnp.concatenate(right, axis=0), NN)
    out_ref[...] = out.reshape(out_ref.shape)


def down_outer(meta, grads, left):
    n_dp, chunks = len(grads[0]), len(grads)
    pieces = [piece for pieces in grads for piece in pieces]
    g, _, width = pieces[0].shape
    tile = tile_of(width, 512)
    return pl.pallas_call(
        functools.partial(down_outer_kernel, n_dp, g, chunks),
        out_shape=jax.ShapeDtypeStruct((TENANTS, R, width), jnp.float32),
        grid_spec=pltpu.PrefetchScalarGridSpec(
            num_scalar_prefetch=1,
            grid=(width // tile,),
            in_specs=[
                pl.BlockSpec(piece.shape[:2] + (tile,), lambda f, *_: (0, 0, f)) for piece in pieces
            ]
            + [whole(left.shape)],
            out_specs=pl.BlockSpec((TENANTS, R, tile), lambda f, *_: (0, 0, f)),
        ),
        compiler_params=pltpu.CompilerParams(vmem_limit_bytes=VMEM_LIMIT),
        cost_estimate=NO_COST,
        name="down_outer",
    )(meta, *pieces, left)


def gate_up_outer_kernel(n_t, chunks, meta, *refs):
    ny = n_t // 2
    factors, refs = [refs[2 * p : 2 * p + 2] for p in range(n_t)], refs[2 * n_t :]
    sums, (left_ref, out_ref) = [refs[2 * q : 2 * q + 2] for q in range(chunks)], refs[2 * chunks :]
    y, c = meta[1] // 2, meta[1] % 2
    owners = [owner_of(p, y, c, ny) for p in range(n_t)]
    grads = []
    for p in range(n_t):
        total = jnp.concatenate([both[p % 2][owners[p] // 2] for both in sums], axis=0)
        grads.append(grads_of(total, factors[p]))
    for layer in range(2):
        right = jnp.concatenate([grad[layer] for grad in grads], axis=0)
        out = ADAPTER_SCALE * fdot(left_of(left_ref, layer, owners), right, NN)
        out_ref[:, layer * R : (layer + 1) * R, :] = out.reshape(TENANTS, R, out.shape[1])


def gate_up_outer(meta, factors, sums, left):
    n_t, chunks = len(factors), len(sums)
    rc = sums[0][0].shape[1]
    own_t, width = factors[0][0].shape
    tile = tile_of(width, 896)
    return pl.pallas_call(
        functools.partial(gate_up_outer_kernel, n_t, chunks),
        out_shape=jax.ShapeDtypeStruct((TENANTS, 2 * R, width), jnp.float32),
        grid_spec=pltpu.PrefetchScalarGridSpec(
            num_scalar_prefetch=1,
            grid=(width // tile,),
            in_specs=[pl.BlockSpec((own_t, tile), lambda f, *_: (0, f))] * (2 * n_t)
            + [pl.BlockSpec((n_t // 2, rc, tile), lambda f, *_: (0, 0, f))] * (2 * chunks)
            + [whole(left.shape)],
            out_specs=pl.BlockSpec((TENANTS, 2 * R, tile), lambda f, *_: (0, 0, f)),
        ),
        compiler_params=pltpu.CompilerParams(vmem_limit_bytes=2 * VMEM_LIMIT),
        cost_estimate=NO_COST,
        name="gate_up_outer",
    )(meta, *[x for pair in factors for x in pair], *[x for both in sums for x in both], left)


def down_part_kernel(chunks, meta, *refs):
    sums, (hidden_ref, out_ref) = refs[:chunks], refs[chunks:]
    width = hidden_ref.shape[1]
    low = jnp.concatenate([both[meta[1] // 2][:, width:] for both in sums], axis=0)
    part = fdot(low, hidden_ref[...], TN)
    out_ref[...] = sum(part[e * R : (e + 1) * R] for e in range(TENANTS)).astype(jnp.bfloat16)


def down_part(meta, sums, hidden):
    return pl.pallas_call(
        functools.partial(down_part_kernel, len(sums)),
        out_shape=jax.ShapeDtypeStruct((R, hidden.shape[1]), jnp.bfloat16),
        in_specs=[SMEM] + [VMEM] * (len(sums) + 1),
        out_specs=VMEM,
        compiler_params=pltpu.CompilerParams(vmem_limit_bytes=VMEM_LIMIT),
        cost_estimate=NO_COST,
        name="down_part",
    )(meta, *sums, hidden)


def spread_kernel(tenant_at, rows, meta, *refs):
    parts, out_ref = refs[:-1], refs[-1]
    out_ref[...] = jnp.zeros_like(out_ref)
    at = 0
    for part in parts:
        for k in range(part.shape[0] // rows):
            tenant = tenant_at(at, meta)
            term = part[k * rows : (k + 1) * rows].astype(jnp.float32)
            out_ref[tenant] = out_ref[tenant] + ADAPTER_SCALE * term
            at += 1


def spread(meta, parts, tenant_at, rows, name):
    width = parts[0].shape[1]
    out = jax.ShapeDtypeStruct((TENANTS, rows, width), jnp.float32)
    tile = tile_of(width, 1024)
    return pl.pallas_call(
        functools.partial(spread_kernel, tenant_at, rows),
        out_shape=out,
        grid_spec=pltpu.PrefetchScalarGridSpec(
            num_scalar_prefetch=1,
            grid=(width // tile,),
            in_specs=[pl.BlockSpec((part.shape[0], tile), lambda f, *_: (0, f)) for part in parts],
            out_specs=pl.BlockSpec((TENANTS, rows, tile), lambda f, *_: (0, 0, f)),
        ),
        compiler_params=pltpu.CompilerParams(vmem_limit_bytes=VMEM_LIMIT),
        cost_estimate=NO_COST,
        name=name,
    )(meta, *parts)


def in_outer_kernel(n_dp, chunks, g, meta, *refs):
    shares, inputs, out_ref = refs[: n_dp * chunks], refs[n_dp * chunks : -1], refs[-1]
    out_ref[...] = jnp.zeros_like(out_ref)
    rows, width = inputs[0].shape
    own_t = rows // g
    rc = own_t // chunks
    for k in range(n_dp):
        block = lax.rem(meta[0] + n_dp - k, n_dp)
        queries = []
        for q in range(chunks):
            query = 0.0
            for s in range(n_dp):
                at = width + (s + n_dp - k) % n_dp * 2 * R
                query = query + shares[q * n_dp + s][:, at : at + 2 * R].astype(jnp.float32)
            queries.append(query.astype(jnp.bfloat16))
        low = [queries[q][j * rc : (j + 1) * rc] for j in range(g) for q in range(chunks)]
        total = fdot(jnp.concatenate(low, axis=0), inputs[k][...], TN)
        tenant = meta[2 + block]
        out_ref[tenant] = out_ref[tenant] + ADAPTER_SCALE * total


def in_outer(meta, shares, inputs, g):
    n_dp, width = len(inputs), inputs[0].shape[1]
    chunks = len(shares)
    shares = [share for there in shares for share in there]
    return pl.pallas_call(
        functools.partial(in_outer_kernel, n_dp, chunks, g),
        out_shape=jax.ShapeDtypeStruct((TENANTS, 2 * R, width), jnp.float32),
        in_specs=[SMEM] + [VMEM] * (len(shares) + n_dp),
        out_specs=VMEM,
        compiler_params=pltpu.CompilerParams(vmem_limit_bytes=VMEM_LIMIT),
        cost_estimate=NO_COST,
        name="in_outer",
    )(meta, *shares, *inputs)


def ring(n, by):
    return [(k, (k + by) % n) for k in range(n)]


def add32(*terms):
    return sum(term.astype(jnp.float32) for term in terms)


def after(value, *done):
    return lax.optimization_barrier((value,) + done)[0]


def per_device(
    layer_input,
    out_grad,
    gate_pre,
    up_pre,
    adapter_acts,
    gate_weight,
    up_weight,
    down_weight,
    adapter_a_gu,
    adapter_b_gu,
    adapter_a_down,
    adapter_b_down,
    block_tenant,
):
    n_dp, n_t = lax.axis_size("dp"), lax.axis_size("tensor")
    ny = n_t // 2
    z, t = lax.axis_index("dp"), lax.axis_index("tensor")
    own_rows, width = out_grad.shape
    own_t, hidden_width = gate_pre.shape
    tokens = adapter_acts.shape[0]
    g = own_rows // own_t
    assert own_rows == BLOCK and g * own_t == own_rows and n_t == 2 * ny and n_t == g * n_dp
    chunks, at = [], 0
    for share in SHARES:
        chunks.append((at, own_t * share // sum(SHARES)))
        at += chunks[-1][1]

    meta = jnp.concatenate([jnp.stack([z, t]).astype(jnp.int32), block_tenant])
    b_down = adapter_b_down.reshape(TENANTS * R, width)
    a_down = jnp.transpose(adapter_a_down, (0, 2, 1)).reshape(TENANTS * R, hidden_width)
    b_gu = adapter_b_gu.reshape(TENANTS * 2 * R, hidden_width)
    a_gu = jnp.transpose(adapter_a_gu, (0, 2, 1)).reshape(TENANTS * 2 * R, width)

    pair = [(k, k ^ 1) for k in range(n_t)]
    z_next = ring(n_dp, 1)

    stored = [gate_pre, up_pre]
    far_stored = [[lax.ppermute(x, "tensor", ring(n_t, 2 * s)) for x in stored] for s in range(1, ny)]
    grads = [[out_grad.reshape(g, own_t, width)[:, at : at + rc]] for at, rc in chunks]
    for _ in range(n_dp - 1):
        grads[0].append(lax.ppermute(grads[0][-1], "dp", z_next))
    grads[1][0] = after(grads[1][0], grads[0][2])
    for _ in range(n_dp - 1):
        grads[1].append(lax.ppermute(grads[1][-1], "dp", z_next))

    def first(q, done):
        pieces = [after(grads[q][0], *done)] + grads[q][1:]
        keep, send = hidden_partial(meta, pieces, down_weight, b_down, a_down, n_t, own_t)
        return keep, send

    def factors_of(stored):
        gate_value, up_value = [x.astype(jnp.float32) for x in stored]
        sigmoid_value = jax.nn.sigmoid(gate_value)
        dgate = up_value * sigmoid_value * (1.0 + gate_value * (1.0 - sigmoid_value))
        dup = gate_value * sigmoid_value
        return [x.astype(jnp.bfloat16) for x in (dgate, dup, dup * up_value)]

    def exchange(keep, other):
        mine = add32(keep, other).astype(jnp.bfloat16)
        return mine, [lax.ppermute(mine, "tensor", ring(n_t, 2 * s)) for s in range(1, ny)]

    def total(mine, far):
        both = add32(mine, *far).astype(jnp.bfloat16)
        return [both, lax.ppermute(both, "tensor", pair)]

    def second(q, sums, done):
        sums = [after(sums[0], *done), sums[1]]
        outs = input_partial(meta, factors, q, sums, gate_weight, up_weight, b_gu, a_gu, n_dp, own_t)
        return [outs[0]] + [lax.ppermute(outs[r], "dp", ring(n_dp, r)) for r in range(1, n_dp)]

    def finish(there, rc):
        return add32(*[x[:, :width] for x in there]).astype(jnp.bfloat16).reshape(g, rc, width)

    keep_a, send_a = first(0, (grads[1][1],))
    stored[0] = after(stored[0], keep_a)
    *near, hidden = factors_of(stored)
    other_a = lax.ppermute(after(send_a, grads[1][n_dp - 2], *[x for there in far_stored for x in there]), "tensor", pair)
    mine_a, far_a = exchange(after(keep_a, near[0]), other_a)
    beside_stored = [lax.ppermute(after(x, mine_a), "tensor", pair) for x in stored]
    keep_b, send_b = first(1, (mine_a,))
    other_b = lax.ppermute(send_b, "tensor", pair)
    beside_stored[0] = after(beside_stored[0], keep_b)
    factors = [near, factors_of(beside_stored)[:2]]
    for there in far_stored:
        beside = [lax.ppermute(x, "tensor", pair) for x in [after(x, *beside_stored) for x in there]]
        for both in (there, beside):
            factors.append(factors_of([after(both[0], keep_b), both[1]])[:2])
    mine_b, far_b = exchange(after(keep_b, *far_a, *[pair[0] for pair in factors]), other_b)
    inputs = [after(layer_input, grads[1][-1], mine_a)] + [None] * (n_dp - 1)
    inputs[1] = lax.ppermute(inputs[0], "dp", z_next)
    inputs[-1] = lax.ppermute(after(inputs[0], keep_b), "dp", ring(n_dp, -1))
    for k in range(2, n_dp // 2 + 1):
        inputs[k] = lax.ppermute(inputs[k - 1], "dp", z_next)
    for k in range(2, (n_dp + 1) // 2):
        inputs[-k] = lax.ppermute(inputs[1 - k], "dp", ring(n_dp, -1))
    sums_a = total(after(mine_a, mine_b, inputs[1], inputs[-1]), far_a)
    there_a = second(0, sums_a, ())
    sums_b = total(after(mine_b, there_a[0], inputs[n_dp // 2], inputs[-1]), far_b)
    there_b = second(1, sums_b, ())

    half_a = finish([after(x, there_b[0]) for x in there_a], chunks[0][1])
    acts = masked_acts(meta, after(adapter_acts.T, half_a), n_t)
    grad_b_down = down_outer(meta, grads, acts)
    a_part = down_part(meta, [sums_a[0], after(sums_b[0], half_a)], hidden)
    a_parts = [a_part] + [lax.ppermute(a_part, "tensor", ring(n_t, 2 * s)) for s in range(1, ny)]
    a_parts = [after(x, grad_b_down) for x in a_parts]
    a_parts += [lax.ppermute(x, "tensor", pair) for x in a_parts]
    grad_b_gu = gate_up_outer(meta, factors, [sums_a, sums_b], after(acts, grad_b_down))

    def column_tenant(p, m):
        owner = lax.rem(m[1] // 2 + ny - p % ny, ny) * 2
        return tenant_of(m, owner + (m[1] % 2 if p < ny else 1 - m[1] % 2), own_t)

    a_parts[0] = after(a_parts[0], grad_b_gu)
    grad_a_down = spread(meta, a_parts, column_tenant, R, "spread_a_down")
    there_b[0] = after(there_b[0], grad_a_down)
    grad_a_gu = in_outer(meta, [there_a, there_b], inputs, g)
    half_b = finish(there_b, chunks[1][1])
    block_input_grad = jnp.concatenate([half_a, half_b], axis=1).reshape(own_rows, width)
    return (
        block_input_grad,
        grad_a_gu.transpose(0, 2, 1),
        grad_b_gu,
        grad_a_down.transpose(0, 2, 1),
        grad_b_down,
    )


def solution(mesh):
    placed = (
        P(("groups", "dp"), "tensor"),
        P(("groups", "dp"), "tensor"),
        P(("groups", "tensor"), "dp"),
        P(("groups", "tensor"), "dp"),
        P("groups", None),
        P("tensor", "dp"),
        P("tensor", "dp"),
        P("dp", "tensor"),
        P(None, "tensor", None),
        P(None, None, "dp"),
        P(None, "dp", None),
        P(None, None, "tensor"),
        P("groups"),
    )
    return jax.shard_map(
        per_device,
        mesh=mesh,
        in_specs=placed,
        out_specs=(
            P(("groups", "dp"), "tensor"),
            P("groups", "tensor", None),
            P("groups", None, "dp"),
            P("groups", "dp", None),
            P("groups", None, "tensor"),
        ),
        check_vma=False,
    )
```
